32 devices in a mesh: ctx: 8 (over z, core), fsdp: 4 (over y, x).
Axes of the slice: x: 2, y: 2, z: 4, core: 2. Of those that a mesh axis runs over, the one named last changes fastest.
Arguments:
- layer_input: bfloat16 [4, 8192, 1024], P('fsdp', 'ctx'), may hold values from -6 to 6
- teacher_states: bfloat16 [4, 8192, 1024], P('fsdp', 'ctx'), may hold values from -6 to 6
- out_cotangent: bfloat16 [4, 8192, 1024], P('fsdp', 'ctx'), may hold values from -6 to 6
- doc_start: int32 [4, 8192], P('fsdp'), may hold values from 0 to 8191, as said below
- valid_flag: int32 [4, 8192], P('fsdp', 'ctx'), may hold values from 0 to 1
- query_weight: bfloat16 [1024, 1024], P('fsdp'), may hold values from -0.1875 to 0.1875
- query_bias: bfloat16 [1024], P('fsdp'), may hold values from -3 to 3
- key_weight: bfloat16 [1024, 1024], P('fsdp'), may hold values from -0.1875 to 0.1875
- value_weight: bfloat16 [1024, 1024], P('fsdp'), may hold values from -0.1875 to 0.1875
- value_bias: bfloat16 [1024], P('fsdp'), may hold values from -3 to 3
- proj_weight: bfloat16 [1024, 1024], P('fsdp'), may hold values from -1 to 1
- proj_bias: bfloat16 [1024], P('fsdp'), may hold values from -3 to 3
- attn_gain: bfloat16 [1024], P('fsdp'), may hold values from 0.5 to 1.5
- attn_shift: bfloat16 [1024], P('fsdp'), may hold values from -3 to 3
- inner_weight: bfloat16 [1024, 4096], P('fsdp'), may hold values from -0.1875 to 0.1875
- inner_bias: bfloat16 [4096], P('fsdp'), may hold values from -3 to 3
- outer_weight: bfloat16 [4096, 1024], P('fsdp'), may hold values from -0.09375 to 0.09375
- outer_bias: bfloat16 [1024], P('fsdp'), may hold values from -3 to 3
- final_gain: bfloat16 [1024], P('fsdp'), may hold values from 0.5 to 1.5
- final_shift: bfloat16 [1024], P('fsdp'), may hold values from -3 to 3
Outputs:
- layer_output: bfloat16 [4, 8192, 1024], P('fsdp', 'ctx')
- input_grad: float32 [4, 8192, 1024], P('fsdp', 'ctx')
- mse: float32 [], replicated
- query_weight_grad: float32 [1024, 1024], P('fsdp')
- query_bias_grad: float32 [1024], P('fsdp')
- key_weight_grad: float32 [1024, 1024], P('fsdp')
- value_weight_grad: float32 [1024, 1024], P('fsdp')
- value_bias_grad: float32 [1024], P('fsdp')
- proj_weight_grad: float32 [1024, 1024], P('fsdp')
- proj_bias_grad: float32 [1024], P('fsdp')
- attn_gain_grad: float32 [1024], P('fsdp')
- attn_shift_grad: float32 [1024], P('fsdp')
- inner_weight_grad: float32 [1024, 4096], P('fsdp')
- inner_bias_grad: float32 [4096], P('fsdp')
- outer_weight_grad: float32 [4096, 1024], P('fsdp')
- outer_bias_grad: float32 [1024], P('fsdp')
- final_gain_grad: float32 [1024], P('fsdp')
- final_shift_grad: float32 [1024], P('fsdp')
The draws below stay inside these ranges and needn't reach their ends.
Inputs may be any that keep to these rules, and one draw needn't show every extreme that they name: doc_start[p, t] is the position in pack p of the first token of the document holding token t: it never falls along t, equals t where a document begins, and t - 512 < doc_start[p, t] <= t; every pack holds a document of exactly 512 tokens.
All inputs are finite; a program needn't handle non-finite values.
Results may differ from the reference program's by a relative error of at most 0.02.
Values may be sent and summed in bfloat16 or wider, within the bound.
No kernel may reach another device: no remote copies, remote signals or barrier semaphores. Data moves between devices by JAX's collectives and lax.ppermute only.
A program may use at most 448 MiB of HBM per device.

```python
import jax
import jax.numpy as jnp
from jax import lax

D = 1024
HEADS = 16
HEAD = 64
FF = 4096
DOC_MAX = 512
QB = 512
PACKS = 4
PACK_LEN = 8192


def pack_starts(key):
    length_key, pick_key = jax.random.split(key)
    lengths = jax.random.randint(length_key, (PACK_LEN,), 1, DOC_MAX + 1)
    chosen = jax.random.randint(pick_key, (), 0, 4)
    position = jnp.arange(PACK_LEN, dtype=jnp.int32)
    lengths = jnp.where(position == chosen, DOC_MAX, lengths).astype(jnp.int32)
    begins = jnp.cumsum(lengths) - lengths
    marks = jnp.zeros((PACK_LEN,), jnp.int32).at[begins].set(1, mode='drop')
    return lax.cummax(jnp.where(marks > 0, position, 0), axis=0)


def draw_doc_start(key, part):
    key = jax.random.fold_in(key, 11)
    pack_keys = jax.random.split(key, PACKS)
    return jax.vmap(pack_starts)(pack_keys)


def draw_valid_flag(key, part):
    key = jax.random.fold_in(key, 23)
    position = jnp.arange(PACK_LEN, dtype=jnp.int32)
    ticket = jax.random.randint(key, (PACKS, PACK_LEN), 0, 4 * PACK_LEN)
    return (ticket < PACK_LEN + 2 * position[None, :]).astype(jnp.int32)


def block_scale(stream_key, shape, cuts, smallest, top_value):
    def one(axis_at, shards_of):
        heights = jax.random.uniform(jax.random.fold_in(jax.random.fold_in(stream_key, 6), axis_at), (shards_of,), jnp.float32, smallest / len(cuts), top_value / len(cuts))
        return jnp.repeat(jnp.exp(heights), shape[axis_at] // shards_of).reshape((-1,) + (1,) * (len(shape) - axis_at - 1))

    factor_of = one(*cuts[0])
    for cut in cuts[1:]:
        factor_of = factor_of * one(*cut)
    return factor_of


def scatter_about(own_key, extent, deviation, limit, cuts=(), kind=jnp.bfloat16):
    loudness = block_scale(own_key, extent, cuts, -0.22, 0.18) if cuts else 1.0
    array = jax.random.normal(own_key, extent, jnp.float32) * deviation * loudness
    return jnp.minimum(jnp.maximum(array, -limit), limit).astype(kind)


def setup_inputs(seed: int = 0) -> dict:
    splits = jax.random.split(jax.random.key(seed), 21)
    layer_input = scatter_about(splits[0], (PACKS, PACK_LEN, D), 1.0, 6.0, ((0, 4), (1, 8)))
    teacher_states = scatter_about(splits[1], (PACKS, PACK_LEN, D), 1.0, 6.0, ((0, 4), (1, 8)))
    out_cotangent = scatter_about(splits[2], (PACKS, PACK_LEN, D), 1.0, 6.0, ((0, 4), (1, 8)))
    doc_start = draw_doc_start(jax.random.fold_in(splits[20], 71), 0)
    valid_flag = draw_valid_flag(jax.random.fold_in(splits[20], 71), 0)
    query_weight = scatter_about(splits[5], (D, D), D ** -0.5, 0.1875, ((0, 4),))
    query_bias = scatter_about(splits[6], (D,), 0.5, 3.0, ((0, 4),))
    key_weight = scatter_about(splits[7], (D, D), D ** -0.5, 0.1875, ((0, 4),))
    value_weight = scatter_about(splits[8], (D, D), D ** -0.5, 0.1875, ((0, 4),))
    value_bias = scatter_about(splits[9], (D,), 0.5, 3.0, ((0, 4),))
    proj_weight = scatter_about(splits[10], (D, D), (16 * D // DOC_MAX) ** -0.5, 1.0, ((0, 4),))
    proj_bias = scatter_about(splits[11], (D,), 0.5, 3.0, ((0, 4),))
    attn_gain = jnp.clip(1.0 + 0.1 * jax.random.normal(splits[12], (D,), jnp.float32), 0.5, 1.5).astype(jnp.bfloat16)
    attn_shift = scatter_about(splits[13], (D,), 0.5, 3.0, ((0, 4),))
    inner_weight = scatter_about(splits[14], (D, FF), D ** -0.5, 0.1875, ((0, 4),))
    inner_bias = scatter_about(splits[15], (FF,), 0.5, 3.0, ((0, 4),))
    outer_weight = scatter_about(splits[16], (FF, D), FF ** -0.5, 0.09375, ((0, 4),))
    outer_bias = scatter_about(splits[17], (D,), 0.5, 3.0, ((0, 4),))
    final_gain = jnp.clip(1.0 + 0.1 * jax.random.normal(splits[18], (D,), jnp.float32), 0.5, 1.5).astype(jnp.bfloat16)
    final_shift = scatter_about(splits[19], (D,), 0.5, 3.0, ((0, 4),))
    return dict(layer_input=layer_input, teacher_states=teacher_states, out_cotangent=out_cotangent, doc_start=doc_start, valid_flag=valid_flag, query_weight=query_weight, query_bias=query_bias, key_weight=key_weight, value_weight=value_weight, value_bias=value_bias, proj_weight=proj_weight, proj_bias=proj_bias, attn_gain=attn_gain, attn_shift=attn_shift, inner_weight=inner_weight, inner_bias=inner_bias, outer_weight=outer_weight, outer_bias=outer_bias, final_gain=final_gain, final_shift=final_shift)


@jax.custom_vjp
def low(v):
    return lax.optimization_barrier(v.astype(jnp.bfloat16)).astype(jnp.float32)

@jax.custom_vjp
def low_back(v):
    return v

def low_keep(v):
    return (low(v), None)

def low_pass(kept, grad):
    return (grad,)

def back_keep(v):
    return (v, None)

def back_low(kept, grad):
    return (low(grad),)
low.defvjp(low_keep, low_pass)
low_back.defvjp(back_keep, back_low)
norm_eps = 1e-05
masked_score = -1e+30

def norm_rows(hidden, gain, shift):
    center = hidden - lax.optimization_barrier(jnp.mean(hidden, axis=-1, keepdims=True))
    spread = lax.optimization_barrier(jnp.mean(center * center, axis=-1, keepdims=True))
    return center * lax.rsqrt(spread + norm_eps) * gain + shift

def product(left, right):
    return jnp.dot(left, right, precision=lax.Precision.HIGHEST, preferred_element_type=jnp.float32)

def attention(query, keys, values, starts):
    width = query.shape[1]
    ids = (starts + 1).astype(jnp.int32)
    pad_rows = jnp.zeros((DOC_MAX, width), jnp.float32)
    pad_ids = jnp.zeros((DOC_MAX,), jnp.int32)
    keys_pad = jnp.concatenate([pad_rows, keys, pad_rows], axis=0)
    values_pad = jnp.concatenate([pad_rows, values, pad_rows], axis=0)
    ids_pad = jnp.concatenate([pad_ids, ids, pad_ids], axis=0)
    span = QB + 2 * DOC_MAX
    scale = HEAD ** (-0.5)

    def one_block(index):
        begin = (index * QB).astype(jnp.int32)
        query_block = lax.dynamic_slice_in_dim(query, begin, QB).reshape(QB, HEADS, HEAD)
        key_block = lax.dynamic_slice_in_dim(keys_pad, begin, span).reshape(span, HEADS, HEAD)
        value_block = lax.dynamic_slice_in_dim(values_pad, begin, span).reshape(span, HEADS, HEAD)
        own_ids = lax.dynamic_slice_in_dim(ids, begin, QB)
        near_ids = lax.dynamic_slice_in_dim(ids_pad, begin, span)
        seen = own_ids[:, None] == near_ids[None, :]
        scores = jnp.einsum('qhd,khd->hqk', query_block, key_block, precision=lax.Precision.HIGHEST) * scale
        scores = low_back(scores)
        scores = jnp.where(seen[None], scores, masked_score)
        probs = jax.nn.softmax(scores, axis=-1)
        mixed = jnp.einsum('hqk,khd->qhd', low(probs), value_block, precision=lax.Precision.HIGHEST)
        return mixed.reshape(QB, width)
    blocks = lax.map(jax.checkpoint(one_block), jnp.arange(PACK_LEN // QB, dtype=jnp.int32))
    return blocks.reshape(PACK_LEN, width)

def forward(params, tokens, starts):
    w_query, b_query, w_key, w_value, b_value, w_proj, b_proj, g_attn, s_attn, w_inner, b_inner, w_outer, b_outer, g_final, s_final = params
    query = low(low_back(product(tokens, w_query) + b_query))
    keys = low(low_back(product(tokens, w_key)))
    values = low(low_back(product(tokens, w_value) + b_value))
    context = low(low_back(attention(query, keys, values, starts)))
    attn_out = low_back(product(context, w_proj) + b_proj)
    normed = norm_rows(tokens + attn_out, g_attn, s_attn)
    pre_act = low_back(product(low(normed), w_inner) + b_inner)
    activated = low(jax.nn.gelu(pre_act, approximate=False))
    branch = low_back(product(activated, w_outer) + b_outer)
    return norm_rows(normed + branch, g_final, s_final)

def reference(layer_input, teacher_states, out_cotangent, doc_start, valid_flag, query_weight, query_bias, key_weight, value_weight, value_bias, proj_weight, proj_bias, attn_gain, attn_shift, inner_weight, inner_bias, outer_weight, outer_bias, final_gain, final_shift):
    params = tuple((item.astype(jnp.float32) for item in (query_weight, query_bias, key_weight, value_weight, value_bias, proj_weight, proj_bias, attn_gain, attn_shift, inner_weight, inner_bias, outer_weight, outer_bias, final_gain, final_shift)))
    count = jnp.sum(valid_flag).astype(jnp.float32)
    loss_weight = PACKS * PACK_LEN * D / 2

    def one_pack(carry, item):
        tokens, teacher, cotangent, starts, flags = item

        def objective(weights, inputs):
            output = forward(weights, inputs, starts)
            error = output - teacher
            sq_err = jnp.sum(flags[:, None] * error * error)
            total = jnp.sum(cotangent * output) + loss_weight * sq_err / (count * D)
            return (total, (output, sq_err))
        total, backward, aux = jax.vjp(objective, params, tokens, has_aux=True)
        weight_grads, token_grads = backward(jnp.ones_like(total))
        summed = tuple((old + new for old, new in zip(carry[0], weight_grads)))
        return ((summed, carry[1] + aux[1]), (aux[0].astype(jnp.bfloat16), token_grads))
    empty_grads = tuple((jnp.zeros_like(item) for item in params))
    inputs = (layer_input.astype(jnp.float32), teacher_states.astype(jnp.float32), out_cotangent.astype(jnp.float32), doc_start, valid_flag.astype(jnp.float32))
    (grads, sq_total), (outputs, input_grads) = lax.scan(one_pack, (empty_grads, jnp.zeros((), jnp.float32)), inputs)
    mse = sq_total / (count * D)
    return (outputs, input_grads, mse, grads[0], grads[1], grads[2], grads[3], grads[4], grads[5], grads[6], grads[7], grads[8], grads[9], grads[10], grads[11], grads[12], grads[13], grads[14])
```

```python
import functools

import jax
import jax.numpy as jnp
from jax import lax
from jax.experimental import pallas as pl
from jax.experimental.pallas import tpu as pltpu
from jax.sharding import PartitionSpec as P

D = 1024
FF = 4096
HEAD = 64
DOC_MAX = 512
TILE = 256
NEG = -1e30
NORM_EPS = 1e-05
VMEM_BYTES = 56 * 2**20
bf16 = jnp.bfloat16
f32 = jnp.float32


def nn(a, b):
    return jnp.dot(a, b, preferred_element_type=f32)


def nt(a, b):
    return lax.dot_general(a, b, (((1,), (1,)), ((), ())), preferred_element_type=f32)


def tn(a, b):
    return lax.dot_general(a, b, (((0,), (0,)), ((), ())), preferred_element_type=f32)


def params():
    return pltpu.CompilerParams(vmem_limit_bytes=VMEM_BYTES)


def cost(flops, bytes_accessed):
    return pl.CostEstimate(flops=int(flops), bytes_accessed=int(bytes_accessed), transcendentals=0)


def sds(shape, dtype):
    return jax.ShapeDtypeStruct(shape, dtype)


def weight_copies(where_ref, pieces, full, out, sem):
    shard, mine, other = pieces
    f, parity = where_ref[0], where_ref[1]
    rows = shard.shape[0]
    half, quarter = rows // 2, rows // 4
    copies = []

    def add(source, begin):
        begin = pl.multiple_of(begin, 16)
        copies.append(pltpu.make_async_copy(source, full.at[pl.ds(begin, source.shape[0])], sem.at[len(copies)]))

    add(shard, f * rows)
    at = 0
    for r in range(1, full.shape[0] // rows):
        base = jnp.bitwise_xor(f, r) * rows
        for offset, length in ((0, half),) if r & (r - 1) == 0 else ((0, quarter), (quarter, quarter)):
            add(mine.at[pl.ds(at, length)], base + offset + parity * half)
            add(other.at[pl.ds(at, length)], base + offset + (1 - parity) * half)
            at += length
    return copies, pltpu.make_async_copy(full, out, sem.at[len(copies)])


def join_weight(where_ref, pieces, full, out, sem):
    copies, save = weight_copies(where_ref, pieces, full, out, sem)

    @pl.when(pl.program_id(0) == 0)
    def _():
        for copy in copies:
            copy.start()
        for copy in copies:
            copy.wait()
        save.start()

    @pl.when(pl.program_id(0) == pl.num_programs(0) - 1)
    def _():
        save.wait()


WEIGHT_SPECS = [pl.BlockSpec(memory_space=pltpu.SMEM)] + [pl.BlockSpec(memory_space=pl.ANY)] * 3


def weight_scratch(rows, columns):
    return [pltpu.VMEM((rows, columns), bf16), pltpu.SemaphoreType.DMA((64,))]


def qkv_kernel(
    where_ref, shard, mine, other, x_ref, bq_ref, bv_ref, q_ref, k_ref, v_ref, kt_ref, vt_ref, full_ref, w_ref, sem
):
    join_weight(where_ref, (shard, mine, other), w_ref, full_ref, sem)
    i = pl.program_id(0)
    x = x_ref[...]

    @pl.when((i > 0) & (i < pl.num_programs(0) - 1))
    def _():
        query = (nn(x, w_ref[:, :D]) + bq_ref[...]).astype(bf16)
        q_ref[...] = query * jnp.asarray(HEAD**-0.5, bf16)

    keys = nn(x, w_ref[:, D : 2 * D]).astype(bf16)
    k_ref[...] = keys
    kt_ref[...] = jnp.transpose(keys)
    values = (nn(x, w_ref[:, 2 * D :]) + bv_ref[...]).astype(bf16)
    v_ref[...] = values
    vt_ref[...] = jnp.transpose(values)


def project_qkv(where, pieces, x_near, bq, bv):
    span = x_near.shape[0]
    rows = span - 2 * DOC_MAX
    row = pl.BlockSpec((1, D), lambda i: (0, 0))
    tall = pl.BlockSpec((512, D), lambda i: (i, 0))
    wide = pl.BlockSpec((D, 512), lambda i: (0, i))
    return pl.pallas_call(
        qkv_kernel,
        grid=(span // 512,),
        in_specs=WEIGHT_SPECS + [tall, row, row],
        out_specs=[
            pl.BlockSpec((512, D), lambda i: (jnp.clip(i - 1, 0, rows // 512 - 1), 0)),
            tall,
            tall,
            wide,
            wide,
            pl.BlockSpec(memory_space=pl.ANY),
        ],
        scratch_shapes=weight_scratch(D, 3 * D),
        out_shape=[
            sds((rows, D), bf16),
            sds((span, D), bf16),
            sds((span, D), bf16),
            sds((D, span), bf16),
            sds((D, span), bf16),
            sds((D, 3 * D), bf16),
        ],
        compiler_params=params(),
        cost_estimate=cost(2 * D * D * (rows + 2 * span), 30 * 2**20),
        name="project_qkv",
    )(where, *pieces, x_near, bq, bv)


def stack_rows(block, stack):
    lanes = lax.broadcasted_iota(jnp.int32, block.shape, 1)
    for h in range(4):
        stack[h*TILE:(h+1)*TILE, :] = jnp.where(lanes//HEAD==h, block, jnp.zeros_like(block))

def stack_columns(turned, stack):
    for h in range(4):
        hr = slice(h*HEAD,(h+1)*HEAD)
        stack[hr, h*TILE:(h+1)*TILE] = turned[hr, :]

def attn_fwd_kernel(lo_ref, hi_ref, q_ref, k_ref, vt_ref, idq_ref, idk_ref, out_ref, lse_ref, qs, acc, top, tot):
    t = pl.program_id(1)
    @pl.when((t==0)&(pl.program_id(0)==0))
    def _():
        qs[...] = jnp.zeros_like(qs)
    stack_columns(jnp.transpose(q_ref[...]), qs)
    acc[...] = jnp.zeros_like(acc)
    top[...] = jnp.full_like(top, NEG)
    tot[...] = jnp.zeros_like(tot)
    def step(kt, carry):
        rows = pl.ds(pl.multiple_of(kt*TILE, TILE), TILE)
        bias = jnp.where(idk_ref[rows,:] == idq_ref[0], 0.0, NEG)
        vt_tile = vt_ref[:, rows]
        s = nn(k_ref[rows,:], qs[...])
        for h in range(4):
            cols = slice(h*TILE,(h+1)*TILE)
            hr = slice(h*HEAD,(h+1)*HEAD)
            sh = s[:, cols] + bias
            old = top[h:h+1,:]
            new = jnp.maximum(old, jnp.max(sh, axis=0, keepdims=True))
            top[h:h+1,:] = new
            p = jnp.exp(sh - new)
            fade = jnp.exp(old-new)
            tot[h:h+1,:] = tot[h:h+1,:]*fade + jnp.sum(p, axis=0, keepdims=True)
            acc[hr,:] = acc[hr,:]*fade + nn(vt_tile[hr,:], p.astype(bf16))
        return carry
    lax.fori_loop(lo_ref[t], hi_ref[t], step, 0)
    total = tot[...]
    inv = 1.0/total
    for h in range(4):
        hr = slice(h*HEAD,(h+1)*HEAD)
        acc[hr,:] = acc[hr,:]*inv[h:h+1,:]
    out_ref[...] = jnp.transpose(acc[...]).astype(bf16)
    lse_ref[0] = top[...] + jnp.log(total)

def attn_fwd(lo, hi, q, k_near, vt_near, idq_rows, idk_col):
    rows=q.shape[0]; span=k_near.shape[0]
    return pl.pallas_call(attn_fwd_kernel,
        grid_spec=pltpu.PrefetchScalarGridSpec(num_scalar_prefetch=2, grid=(D//256, rows//TILE),
            in_specs=[pl.BlockSpec((TILE,256),lambda g,t,*_:(t,g)),
                pl.BlockSpec((span,256),lambda g,t,*_:(0,g)),
                pl.BlockSpec((256,span),lambda g,t,*_:(g,0)),
                pl.BlockSpec((1,1,TILE),lambda g,t,*_:(t,0,0)),
                pl.BlockSpec((span,1),lambda g,t,*_:(0,0))],
            out_specs=[pl.BlockSpec((TILE,256),lambda g,t,*_:(t,g)),
                pl.BlockSpec((1,8,TILE),lambda g,t,*_:(g,0,t))],
            scratch_shapes=[pltpu.VMEM((256,4*TILE),bf16),
                pltpu.VMEM((256,TILE),f32),pltpu.VMEM((8,TILE),f32),pltpu.VMEM((8,TILE),f32)]),
        out_shape=[jax.ShapeDtypeStruct((rows,D),bf16),jax.ShapeDtypeStruct((D//256,8,rows),f32)],
        compiler_params=pltpu.CompilerParams(vmem_limit_bytes=VMEM_BYTES),
        name="attn_forward",
    )(lo,hi,q,k_near,vt_near,idq_rows,idk_col)

def attn_bwd_kernel(lo_ref, hi_ref, q_ref, do_ref, ctx_ref, k_ref, kt_ref, v_ref, lse_ref, idq_ref, idk_ref,
        dq_ref, dk_ref, dv_ref, qs, dos, qst, dost, dk_acc, dv_acc, dq_acc):
    t = pl.program_id(1)
    @pl.when((t==0)&(pl.program_id(0)==0))
    def _():
        qst[...] = jnp.zeros_like(qst)
        dost[...] = jnp.zeros_like(dost)
    @pl.when(t==0)
    def _():
        dk_acc[...] = jnp.zeros_like(dk_acc)
        dv_acc[...] = jnp.zeros_like(dv_acc)
    stack_rows(q_ref[...], qs)
    stack_rows(do_ref[...], dos)
    stack_columns(jnp.transpose(q_ref[...]), qst)
    stack_columns(jnp.transpose(do_ref[...]), dost)
    prod = do_ref[...].astype(f32)*ctx_ref[...].astype(f32)
    high = prod.astype(bf16)
    low = (prod-high.astype(f32)).astype(bf16)
    sel = (lax.broadcasted_iota(jnp.int32,(8,256),1)//HEAD == lax.broadcasted_iota(jnp.int32,(8,256),0)).astype(bf16)
    delta = nt(sel, high)+nt(sel, low)
    lse = lse_ref[0]
    delta_row = jnp.concatenate([delta[h:h+1] for h in range(4)],axis=1)
    lse_row = jnp.concatenate([lse[h:h+1] for h in range(4)],axis=1)
    dq_acc[...] = jnp.zeros_like(dq_acc)
    def step(kt, carry):
        rows = pl.ds(pl.multiple_of(kt*TILE, TILE), TILE)
        seen = idk_ref[rows,:] == idq_ref[0]
        bias = jnp.where(seen, 0.0, NEG)
        s = nn(k_ref[rows,:], qst[...])
        dp = nn(v_ref[rows,:], dost[...])
        p = jnp.exp(s + jnp.concatenate([bias]*4,axis=1) - lse_row)
        ds = (p*(dp-delta_row)).astype(bf16)
        dv_acc[rows,:] += nn(p.astype(bf16), dos[...])
        dk_acc[rows,:] += nn(ds, qs[...])
        kt_tile = kt_ref[:, rows]
        for h in range(4):
            hr=slice(h*HEAD,(h+1)*HEAD)
            dq_acc[hr,:] += nn(kt_tile[hr,:], ds[:, h*TILE:(h+1)*TILE])
        return carry
    lax.fori_loop(lo_ref[t], hi_ref[t], step, 0)
    dq_ref[...] = (jnp.transpose(dq_acc[...])*(HEAD**-0.5)).astype(bf16)
    @pl.when(t==pl.num_programs(1)-1)
    def _():
        dk_ref[...] = dk_acc[...].astype(bf16)
        dv_ref[...] = dv_acc[...].astype(bf16)

def attn_bwd(lo, hi, q, do, ctx, k_near, kt_near, v_near, lse, idq_rows, idk_col, g0=0, ng=4):
    rows=q.shape[0]; span=k_near.shape[0]
    return pl.pallas_call(attn_bwd_kernel,
        grid_spec=pltpu.PrefetchScalarGridSpec(num_scalar_prefetch=2, grid=(ng, rows//TILE),
            in_specs=[pl.BlockSpec((TILE,256),lambda g,t,*_:(t,g+g0)),
                pl.BlockSpec((TILE,256),lambda g,t,*_:(t,g+g0)),
                pl.BlockSpec((TILE,256),lambda g,t,*_:(t,g+g0)),
                pl.BlockSpec((span,256),lambda g,t,*_:(0,g+g0)),
                pl.BlockSpec((256,span),lambda g,t,*_:(g+g0,0)),
                pl.BlockSpec((span,256),lambda g,t,*_:(0,g+g0)),
                pl.BlockSpec((1,8,TILE),lambda g,t,*_:(g+g0,0,t)),
                pl.BlockSpec((1,1,TILE),lambda g,t,*_:(t,0,0)),
                pl.BlockSpec((span,1),lambda g,t,*_:(0,0))],
            out_specs=[pl.BlockSpec((TILE,256),lambda g,t,*_:(t,g)),
                pl.BlockSpec((span,256),lambda g,t,*_:(0,g)),
                pl.BlockSpec((span,256),lambda g,t,*_:(0,g))],
            scratch_shapes=[pltpu.VMEM((4*TILE,256),bf16),pltpu.VMEM((4*TILE,256),bf16),
                pltpu.VMEM((256,4*TILE),bf16),pltpu.VMEM((256,4*TILE),bf16),
                pltpu.VMEM((span,256),f32),pltpu.VMEM((span,256),f32),pltpu.VMEM((256,TILE),f32)]),
        out_shape=[jax.ShapeDtypeStruct((rows,ng*256),bf16),jax.ShapeDtypeStruct((span,ng*256),bf16),jax.ShapeDtypeStruct((span,ng*256),bf16)],
        compiler_params=pltpu.CompilerParams(vmem_limit_bytes=VMEM_BYTES),
        name="attn_backward",
    )(lo,hi,q,do,ctx,k_near,kt_near,v_near,lse,idq_rows,idk_col)


def norm_stats(hidden):
    center = hidden - jnp.mean(hidden, axis=1, keepdims=True)
    rate = lax.rsqrt(jnp.mean(center * center, axis=1, keepdims=True) + NORM_EPS)
    return center * rate, rate


def norm_back(grad, unit, rate):
    return rate * (
        grad - jnp.mean(grad, axis=1, keepdims=True) - unit * jnp.mean(grad * unit, axis=1, keepdims=True)
    )


def mix_kernel(
    where_ref, shard, mine, other, c_ref, b_ref, x_ref, g_ref, s_ref, normed_ref, low_ref, rate_ref, full_ref, w_ref, sem
):
    join_weight(where_ref, (shard, mine, other), w_ref, full_ref, sem)
    hidden = x_ref[...].astype(f32) + (nn(c_ref[...], w_ref[...]) + b_ref[...])
    unit, rate = norm_stats(hidden)
    normed = unit * g_ref[...] + s_ref[...]
    normed_ref[...] = normed
    low_ref[...] = normed.astype(bf16)
    rate_ref[...] = rate


def mix_and_norm(where, pieces, context, b, tokens, gain, shift):
    rows = context.shape[0]
    tile = pl.BlockSpec((TILE, D), lambda i: (i, 0))
    row = pl.BlockSpec((1, D), lambda i: (0, 0))
    return pl.pallas_call(
        mix_kernel,
        grid=(rows // TILE,),
        in_specs=WEIGHT_SPECS + [tile, row, tile, row, row],
        out_specs=[tile, tile, pl.BlockSpec((TILE, 1), lambda i: (i, 0)), pl.BlockSpec(memory_space=pl.ANY)],
        out_shape=[sds((rows, D), f32), sds((rows, D), bf16), sds((rows, 1), f32), sds((D, D), bf16)],
        scratch_shapes=weight_scratch(D, D),
        compiler_params=params(),
        cost_estimate=cost(2 * D * D * rows, 14 * 2**20),
        name="mix_and_norm",
    )(where, *pieces, context, b, tokens, gain, shift)


def gelu_parts(u):
    t = 1.0 / (1.0 + (0.3275911 * 0.7071067811865476) * jnp.abs(u))
    poly = t * (0.254829592 + t * (-0.284496736 + t * (1.421413741 + t * (-1.453152027 + t * 1.061405429))))
    bell = jnp.exp(-0.5 * u * u)
    tail = 0.5 * poly * bell
    share = jnp.where(u >= 0, 1.0 - tail, tail)
    return u * share, share + u * bell * 0.3989422804014327


def inner_kernel(where_ref, shard, mine, other, x_ref, b_ref, act_ref, slope_ref, full_ref, w_ref, sem):
    join_weight(where_ref, (shard, mine, other), w_ref, full_ref, sem)
    wide = act_ref.shape[1]
    columns = pl.ds(pl.multiple_of(pl.program_id(0) * wide, wide), wide)
    for i in range(x_ref.shape[0] // TILE):
        rows = slice(i * TILE, (i + 1) * TILE)
        act, slope = gelu_parts(nn(x_ref[rows, :], w_ref[:, columns]) + b_ref[...])
        act_ref[rows, :] = act.astype(bf16)
        slope_ref[rows, :] = slope.astype(bf16)


def inner_forward(where, pieces, x, b):
    rows, wide = x.shape[0], 512
    block = pl.BlockSpec((rows, wide), lambda j: (0, j))
    return pl.pallas_call(
        inner_kernel,
        grid=(FF // wide,),
        in_specs=WEIGHT_SPECS
        + [pl.BlockSpec((rows, D), lambda j: (0, 0)), pl.BlockSpec((1, wide), lambda j: (0, j))],
        out_specs=[block, block, pl.BlockSpec(memory_space=pl.ANY)],
        out_shape=[sds((rows, FF), bf16), sds((rows, FF), bf16), sds((D, FF), bf16)],
        scratch_shapes=weight_scratch(D, FF),
        compiler_params=params(),
        cost_estimate=cost(2 * D * FF * rows, 26 * 2**20),
        name="inner_forward",
    )(where, *pieces, x, b)


def outer_kernel(
    where_ref, shard, mine, other, coef_ref, act_ref, b_ref, normed_ref, g_ref, s_ref, teach_ref, cot_ref, flag_ref,
    out_ref, dsum_ref, dlow_ref, sums_ref, full_ref, w_ref, sem,
):
    join_weight(where_ref, (shard, mine, other), w_ref, full_ref, sem)
    hidden = normed_ref[...] + (nn(act_ref[...], w_ref[...]) + b_ref[...])
    unit, rate = norm_stats(hidden)
    gain = g_ref[...]
    final = unit * gain + s_ref[...]
    out_ref[...] = final.astype(bf16)
    error = final - teach_ref[...].astype(f32)
    marked = flag_ref[...] * error
    grad = cot_ref[...].astype(f32) + coef_ref[0] * marked
    dsum = norm_back(grad * gain, unit, rate)
    dsum_ref[...] = dsum
    low = dsum.astype(bf16)
    dlow_ref[...] = low

    @pl.when(pl.program_id(0) == 0)
    def _():
        sums_ref[...] = jnp.zeros_like(sums_ref)

    sums_ref[0:1, :] += jnp.sum(grad * unit, axis=0, keepdims=True)
    sums_ref[1:2, :] += jnp.sum(grad, axis=0, keepdims=True)
    sums_ref[2:3, :] += jnp.sum(low.astype(f32), axis=0, keepdims=True)
    sums_ref[3:4, :] += jnp.sum(marked * error, axis=0, keepdims=True)


def outer_forward(where, pieces, coef, act, b, normed, gain, shift, teacher, cotangent, flags):
    rows = act.shape[0]
    tile = pl.BlockSpec((TILE, D), lambda i: (i, 0))
    row = pl.BlockSpec((1, D), lambda i: (0, 0))
    return pl.pallas_call(
        outer_kernel,
        grid=(rows // TILE,),
        in_specs=WEIGHT_SPECS
        + [
            pl.BlockSpec(memory_space=pltpu.SMEM),
            pl.BlockSpec((TILE, FF), lambda i: (i, 0)),
            row, tile, row, row, tile, tile,
            pl.BlockSpec((TILE, 1), lambda i: (i, 0)),
        ],
        out_specs=[
            tile, tile, tile, pl.BlockSpec((8, D), lambda i: (0, 0)), pl.BlockSpec(memory_space=pl.ANY),
        ],
        out_shape=[
            sds((rows, D), bf16), sds((rows, D), f32), sds((rows, D), bf16), sds((8, D), f32), sds((FF, D), bf16),
        ],
        scratch_shapes=weight_scratch(FF, D),
        compiler_params=params(),
        cost_estimate=cost(2 * D * FF * rows, 32 * 2**20),
        name="outer_forward",
    )(where, *pieces, coef, act, b, normed, gain, shift, teacher, cotangent, flags)


def gram_kernel(order_ref, left_ref, right_ref, keep_ref, send_ref):
    half = keep_ref.shape[1]
    grad = tn(left_ref[...], right_ref[...])
    first = order_ref[pl.num_programs(1)] == 0
    low, high = grad[:half], grad[half:]
    keep_ref[0] = jnp.where(first, low, high).astype(bf16)
    send_ref[0] = jnp.where(first, high, low).astype(bf16)


def gram(order, left, right, shards, wide):
    tokens, height = left.shape
    columns = right.shape[1]
    part = height // shards
    out = pl.BlockSpec((1, part // 2, wide), lambda j, r, order_ref: (r, 0, j))
    return pl.pallas_call(
        gram_kernel,
        grid_spec=pltpu.PrefetchScalarGridSpec(
            num_scalar_prefetch=1,
            grid=(columns // wide, shards),
            in_specs=[
                pl.BlockSpec((tokens, part), lambda j, r, order_ref: (0, order_ref[r])),
                pl.BlockSpec((tokens, wide), lambda j, r, order_ref: (0, j)),
            ],
            out_specs=[out, out],
        ),
        out_shape=[sds((shards, part // 2, columns), bf16)] * 2,
        compiler_params=params(),
        cost_estimate=cost(2 * tokens * height * columns, 2 * (tokens * (height + columns) + height * columns)),
        name="gram",
    )(order, left, right)


def feed_back_kernel(
    db_ref, wo_ref, slope_ref, wi_ref, dsum_ref, normed_ref, rate_ref, g_ref, s_ref,
    dpre_ref, bias_ref, done_ref, dattn_ref, sums_ref, total,
):
    j = pl.program_id(0)

    @pl.when(j == 0)
    def _():
        total[...] = dsum_ref[...]

    ones = jnp.ones((8, TILE), bf16)
    bias = jnp.zeros(bias_ref.shape, f32)
    for i in range(db_ref.shape[0] // TILE):
        rows = slice(i * TILE, (i + 1) * TILE)
        pre = (nt(db_ref[rows, :], wo_ref[...]) * slope_ref[rows, :].astype(f32)).astype(bf16)
        dpre_ref[rows, :] = pre
        bias += nn(ones, pre)
        total[rows, :] += nt(pre, wi_ref[...])
    bias_ref[...] = bias

    @pl.when(j == pl.num_programs(0) - 1)
    def _():
        gain = g_ref[...]
        sums_ref[...] = jnp.zeros_like(sums_ref)
        for i in range(db_ref.shape[0] // TILE):
            rows = slice(i * TILE, (i + 1) * TILE)
            grad = total[rows, :]
            unit = (normed_ref[rows, :] - s_ref[...]) / gain
            done = norm_back(grad * gain, unit, rate_ref[rows, :])
            done_ref[rows, :] = done
            low = done.astype(bf16)
            dattn_ref[rows, :] = low
            sums_ref[0:1, :] += jnp.sum(grad * unit, axis=0, keepdims=True)
            sums_ref[1:2, :] += jnp.sum(grad, axis=0, keepdims=True)
            sums_ref[2:3, :] += jnp.sum(low.astype(f32), axis=0, keepdims=True)


def feed_back(d_branch, w_outer, slope, w_inner, d_sum_two, normed, rate, gain, shift):
    rows, wide = d_branch.shape[0], 512
    whole = pl.BlockSpec((rows, D), lambda j: (0, 0))
    row = pl.BlockSpec((1, D), lambda j: (0, 0))
    tall = pl.BlockSpec((rows, wide), lambda j: (0, j))
    return pl.pallas_call(
        feed_back_kernel,
        grid=(FF // wide,),
        in_specs=[
            whole,
            pl.BlockSpec((wide, D), lambda j: (j, 0)),
            tall,
            pl.BlockSpec((D, wide), lambda j: (0, j)),
            whole, whole,
            pl.BlockSpec((rows, 1), lambda j: (0, 0)),
            row, row,
        ],
        out_specs=[tall, pl.BlockSpec((8, wide), lambda j: (0, j)), whole, whole, pl.BlockSpec((8, D), lambda j: (0, 0))],
        out_shape=[sds((rows, FF), bf16), sds((8, FF), f32), sds((rows, D), f32), sds((rows, D), bf16), sds((8, D), f32)],
        scratch_shapes=[pltpu.VMEM((rows, D), f32)],
        compiler_params=params(),
        cost_estimate=cost(4 * D * FF * rows, 50 * 2**20),
        name="feed_back",
    )(d_branch, w_outer, slope, w_inner, d_sum_two, normed, rate, gain, shift)


def turn_kernel(d_ref, w_ref, out_ref):
    out_ref[...] = nt(d_ref[...], w_ref[...]).astype(bf16)


def turned_product(d, w):
    rows = d.shape[0]
    tile = pl.BlockSpec((TILE, D), lambda i: (i, 0))
    return pl.pallas_call(
        turn_kernel,
        grid=(rows // TILE,),
        in_specs=[tile, pl.BlockSpec((D, D), lambda i: (0, 0))],
        out_specs=tile,
        out_shape=sds((rows, D), bf16),
        compiler_params=params(),
        cost_estimate=cost(2 * D * D * rows, 6 * 2**20),
        name="turned_product",
    )(d, w)


def input_kernel(base_ref, d_ref, w_ref, out_ref):
    out_ref[...] = base_ref[...] + nt(d_ref[...], w_ref[...])


def input_back(base, d, w):
    rows = base.shape[0]
    tile = pl.BlockSpec((TILE, D), lambda i: (i, 0))
    return pl.pallas_call(
        input_kernel,
        grid=(rows // TILE,),
        in_specs=[tile, pl.BlockSpec((TILE, 3 * D), lambda i: (i, 0)), pl.BlockSpec((D, 3 * D), lambda i: (0, 0))],
        out_specs=tile,
        out_shape=sds((rows, D), f32),
        compiler_params=params(),
        cost_estimate=cost(6 * D * D * rows, 20 * 2**20),
        name="input_back",
    )(base, d, w)


def swap(value, axis, bit):
    return lax.ppermute(value, axis, [(i, i ^ bit) for i in range(lax.axis_size(axis))])


def after(value, *others):
    return lax.optimization_barrier((value,) + others)[0]


def gather_weight(shard, own):
    n = lax.axis_size("fsdp")
    rows = shard.shape[0]
    half, quarter = rows // 2, rows // 4
    held, whole = {}, {}
    for r in range(1, n):
        if r & (r - 1) == 0:
            whole[r] = swap(own, "fsdp", r)
            for s in (0, 1):
                held[r, s] = whole[r][s * quarter : (s + 1) * quarter]
        else:
            for s, bit in ((0, 1 << (r.bit_length() - 1)), (1, r & -r)):
                held[r, s] = swap(held[r ^ bit, s], "fsdp", bit)
    found = []
    for r in range(1, n):
        found += [whole[r]] if r in whole else [held[r, 0], held[r, 1]]
    mine = jnp.concatenate(found, axis=0)
    other = swap(mine, "ctx", 1)
    return (shard, mine, other), [whole[r] for r in whole], mine


def half_sets(value, bit):
    shape = value.shape
    split = value.reshape((shape[0] // (2 * bit), 2, bit) + shape[1:])
    rest = (shape[0] // 2,) + shape[1:]
    return split[:, 0].reshape(rest), split[:, 1].reshape(rest)


def add_low(a, b):
    return (a.astype(f32) + b.astype(f32)).astype(bf16)


def scatter_sum(keep, send):
    n = lax.axis_size("fsdp")
    got = swap(send, "ctx", 1)
    quarter = keep.shape[1] // 2
    bits = [1 << b for b in range(n.bit_length() - 1)]
    parts = []
    for s, order in ((0, bits), (1, bits[::-1])):
        rows = slice(s * quarter, (s + 1) * quarter)
        current = add_low(keep[:, rows], got[:, rows])
        ids = list(range(n))
        for bit in order:
            where = [i for i, r in enumerate(ids) if not r & bit]
            away = [i for i, r in enumerate(ids) if r & bit]
            step = away[0] - where[0]
            mine, theirs = half_sets(current, step)
            ids = [ids[i] for i in where]
            current = add_low(mine, swap(theirs, "fsdp", bit))
        parts.append(current[0])
    return parts


def chain_sum(value):
    count = lax.axis_size("ctx") // 2
    position = lax.axis_index("ctx") // 2
    half = count // 2

    def move(value, chip_pairs):
        pairs = [(2 * a + c, 2 * b + c) for a, b in chip_pairs for c in (0, 1)]
        return lax.ppermute(value, "ctx", pairs)

    for s in range(half - 1):
        value = add_low(value, move(value, [(s, s + 1), (count - 1 - s, count - 2 - s)]))
    inner = (position == half - 1) | (position == half)
    across = move(value, [(half - 1, half), (half, half - 1)])
    value = jnp.where(inner, add_low(value, across), value)
    for s in reversed(range(half - 1)):
        back = move(value, [(s + 1, s), (count - 2 - s, count - 1 - s)])
        value = jnp.where((position == s) | (position == count - 1 - s), back, value)
    return value


def gather_small(vector, f):
    n = lax.axis_size("fsdp")
    value = vector.reshape(1, -1)
    bit = 1
    while bit < n:
        value = jnp.concatenate([value, swap(value, "fsdp", bit)], axis=0)
        bit *= 2
    bit = 1
    while bit < n:
        split = value.reshape(n // (2 * bit), 2, bit, -1)
        value = jnp.where(f & bit > 0, split[:, ::-1], split).reshape(n, -1)
        bit *= 2
    return value


def sum_everywhere(value):
    for axis in ("ctx", "fsdp"):
        bit = 1
        while bit < lax.axis_size(axis):
            value = value + swap(value, axis, bit)
            bit *= 2
    return value


def body(
    layer_input,
    teacher_states,
    out_cotangent,
    doc_start,
    valid_flag,
    query_weight,
    query_bias,
    key_weight,
    value_weight,
    value_bias,
    proj_weight,
    proj_bias,
    attn_gain,
    attn_shift,
    inner_weight,
    inner_bias,
    outer_weight,
    outer_bias,
    final_gain,
    final_shift,
):
    n_ctx, n_fsdp = lax.axis_size("ctx"), lax.axis_size("fsdp")
    c, f = lax.axis_index("ctx"), lax.axis_index("fsdp")
    parity = c % 2
    tokens = layer_input[0]
    rows = tokens.shape[0]
    part = query_weight.shape[0]
    where = jnp.stack([f, parity]).astype(jnp.int32)
    order = jnp.concatenate([f ^ jnp.arange(n_fsdp, dtype=jnp.int32), parity[None].astype(jnp.int32)])

    up = [(i, i + 1) for i in range(n_ctx - 1)]
    down = [(b, a) for a, b in up]
    before = lax.ppermute(tokens[rows - DOC_MAX :], "ctx", up)
    behind = lax.ppermute(tokens[:DOC_MAX], "ctx", down)
    x_near = jnp.concatenate([before, tokens, behind], axis=0)

    small = jnp.concatenate(
        [query_bias, value_bias, proj_bias, attn_gain, attn_shift, outer_bias, final_gain, final_shift, inner_bias]
    )
    small = gather_small(small, f).astype(f32)
    vectors = [small[:, i * part : (i + 1) * part].reshape(1, D) for i in range(8)]
    b_query, b_value, b_proj, g_attn, s_attn, b_outer, g_final, s_final = vectors
    b_inner = small[:, 8 * part :].reshape(1, FF)

    flags = valid_flag[0].astype(f32)[:, None]

    def own_half(shard):
        half = shard.shape[0] // 2
        return lax.dynamic_slice_in_dim(shard, parity * half, half)

    qkv_shard = jnp.concatenate([query_weight, key_weight, value_weight], axis=1)
    qkv_pieces, qkv_first, qkv_last = gather_weight(qkv_shard, own_half(qkv_shard))
    proj_own = after(own_half(proj_weight), *qkv_first)
    proj_pieces, proj_first, proj_last = gather_weight(proj_weight, proj_own)
    inner_own = after(own_half(inner_weight), *qkv_first)
    inner_pieces, inner_first, inner_last = gather_weight(inner_weight, inner_own)
    outer_own = after(own_half(outer_weight), *proj_first, qkv_last)
    outer_pieces, outer_first, outer_last = gather_weight(outer_weight, outer_own)

    count = sum_everywhere(after(jnp.full((8, 128), jnp.sum(flags), f32), *qkv_first))[0, 0]

    position = c * rows
    starts = doc_start[0]
    near_starts = lax.dynamic_slice_in_dim(
        jnp.concatenate(
            [jnp.full((DOC_MAX,), -1, jnp.int32), starts, jnp.full((DOC_MAX,), 2**30, jnp.int32)]
        ),
        position,
        rows + 2 * DOC_MAX,
    )
    own_starts = near_starts[DOC_MAX : DOC_MAX + rows]
    count_tiles = rows // TILE
    low_tile = (own_starts[::TILE] - position + DOC_MAX) // TILE
    last = position + TILE * (1 + jnp.arange(count_tiles, dtype=jnp.int32)) - 1
    ends = jnp.sum((near_starts[None, :] <= last[:, None]).astype(jnp.int32), axis=1)
    high_tile = (ends + TILE - 1) // TILE
    idq = own_starts.reshape(count_tiles, 1, TILE)
    idk = near_starts[:, None]

    query, keys, values, keys_t, values_t, w_qkv = project_qkv(where, qkv_pieces, x_near, b_query, b_value)
    context, log_totals = attn_fwd(low_tile, high_tile, query, keys, values_t, idq, idk)
    normed, normed_low, rate, w_proj = mix_and_norm(where, proj_pieces, context, b_proj, tokens, g_attn, s_attn)
    act, slope, w_inner = inner_forward(where, inner_pieces, normed_low, b_inner)
    coef = (n_fsdp * n_ctx * rows / count).reshape(1)
    layer_out, d_sum_two, d_branch, final_sums, w_outer = outer_forward(
        where, outer_pieces, coef, act, b_outer, normed, g_final, s_final, teacher_states[0], out_cotangent[0], flags
    )

    outer_parts = scatter_sum(*gram(order, act, d_branch, n_fsdp, 512))
    d_pre, inner_bias_sum, d_sum_one, d_attn, attn_sums = feed_back(
        d_branch, w_outer, slope, w_inner, d_sum_two, normed, rate, g_attn, s_attn
    )
    inner_parts = scatter_sum(*gram(order, normed_low, d_pre, n_fsdp, 2048))
    d_context = turned_product(d_attn, w_proj)
    proj_parts = scatter_sum(*gram(order, context, d_attn, n_fsdp, D))
    outer_total = chain_sum(jnp.concatenate(outer_parts, axis=0))
    inner_total = chain_sum(jnp.concatenate(inner_parts, axis=0))
    proj_total = chain_sum(jnp.concatenate(proj_parts, axis=0))
    d_query, near_dk, near_dv = attn_bwd(
        low_tile, high_tile, query, d_context, context, keys, keys_t, values, log_totals, idq, idk
    )
    near_d = jnp.concatenate([near_dk, near_dv], axis=1)
    from_above = lax.ppermute(near_d[:DOC_MAX], "ctx", down)
    from_below = lax.ppermute(near_d[rows + DOC_MAX :], "ctx", up)
    own = near_d[DOC_MAX : DOC_MAX + rows].astype(f32)
    rest = jnp.zeros((rows - DOC_MAX, 2 * D), f32)
    own = (
        own
        + jnp.concatenate([from_below.astype(f32), rest], axis=0)
        + jnp.concatenate([rest, from_above.astype(f32)], axis=0)
    ).astype(bf16)
    d_keys, d_values = own[:, :D], own[:, D:]
    d_joined = jnp.concatenate([d_query, own], axis=1)
    qkv_parts = scatter_sum(*gram(order, tokens, d_joined, n_fsdp, 3 * D // 2))
    input_grad = input_back(d_sum_one, d_joined, w_qkv)
    qkv_total = chain_sum(jnp.concatenate(qkv_parts, axis=0))

    def finish(mine):
        quarter = mine.shape[0] // 2
        other = swap(mine, "ctx", 1)
        first = parity == 0
        return jnp.concatenate([jnp.where(first, mine, other), jnp.where(first, other, mine)], axis=0).astype(f32)

    outer_grad, inner_grad, proj_grad, qkv_grad = (
        finish(outer_total), finish(inner_total), finish(proj_total), finish(qkv_total)
    )

    early = jnp.concatenate([final_sums[:4], attn_sums[:3], inner_bias_sum[:1].reshape(4, D)], axis=0)
    early = sum_everywhere(jnp.concatenate([early, jnp.zeros((5, D), f32)], axis=0))
    late = jnp.sum(jnp.stack([d_query, d_values]).astype(f32), axis=1)
    late = sum_everywhere(jnp.concatenate([late, jnp.zeros((6, D), f32)], axis=0))
    mse = jnp.sum(early[3]) / (count * D)

    def mine(vector):
        length = vector.shape[0] // n_fsdp
        return lax.dynamic_slice_in_dim(vector, f * length, length)

    return (
        layer_out[None],
        input_grad[None],
        mse,
        qkv_grad[:, :D],
        mine(late[0]),
        qkv_grad[:, D : 2 * D],
        qkv_grad[:, 2 * D :],
        mine(late[1]),
        proj_grad,
        mine(early[6]),
        mine(early[4]),
        mine(early[5]),
        inner_grad,
        mine(early[7:11].reshape(FF)),
        outer_grad,
        mine(early[2]),
        mine(early[0]),
        mine(early[1]),
    )


def solution(mesh):
    tokens = P("fsdp", "ctx", None)
    matrix, vector = P("fsdp", None), P("fsdp")
    weights = (
        matrix, vector, matrix, matrix, vector, matrix, vector, vector, vector, matrix, vector, matrix, vector, vector, vector,
    )
    return jax.shard_map(
        body,
        mesh=mesh,
        in_specs=(tokens, tokens, tokens, matrix, P("fsdp", "ctx")) + weights,
        out_specs=(tokens, tokens, P()) + weights,
        check_vma=False,
    )
```

```python
import functools

import jax
import jax.numpy as jnp
from jax import lax
from jax.experimental import pallas as pl
from jax.experimental.pallas import tpu as pltpu
from jax.sharding import PartitionSpec as P

D = 1024
FF = 4096
HEAD = 64
DOC_MAX = 512
TILE = 256
NEG = -1e30
NORM_EPS = 1e-05
VMEM_BYTES = 56 * 2**20
bf16 = jnp.bfloat16
f32 = jnp.float32


def nn(a, b):
    return jnp.dot(a, b, preferred_element_type=f32)


def nt(a, b):
    return lax.dot_general(a, b, (((1,), (1,)), ((), ())), preferred_element_type=f32)


def tn(a, b):
    return lax.dot_general(a, b, (((0,), (0,)), ((), ())), preferred_element_type=f32)


def params():
    return pltpu.CompilerParams(vmem_limit_bytes=VMEM_BYTES)


def cost(flops, bytes_accessed):
    return pl.CostEstimate(flops=int(flops), bytes_accessed=int(bytes_accessed), transcendentals=0)


def sds(shape, dtype):
    return jax.ShapeDtypeStruct(shape, dtype)


def weight_copies(where_ref, pieces, full, out, sem):
    shard, mine, other = pieces
    f, parity = where_ref[0], where_ref[1]
    rows = shard.shape[0]
    half, quarter = rows // 2, rows // 4
    copies = []

    def add(source, begin):
        begin = pl.multiple_of(begin, 16)
        copies.append(pltpu.make_async_copy(source, full.at[pl.ds(begin, source.shape[0])], sem.at[len(copies)]))

    add(shard, f * rows)
    at = 0
    for r in range(1, full.shape[0] // rows):
        base = jnp.bitwise_xor(f, r) * rows
        for offset, length in ((0, half),) if r & (r - 1) == 0 else ((0, quarter), (quarter, quarter)):
            add(mine.at[pl.ds(at, length)], base + offset + parity * half)
            add(other.at[pl.ds(at, length)], base + offset + (1 - parity) * half)
            at += length
    return copies, pltpu.make_async_copy(full, out, sem.at[len(copies)])


def join_weight(where_ref, pieces, full, out, sem):
    copies, save = weight_copies(where_ref, pieces, full, out, sem)

    @pl.when(pl.program_id(0) == 0)
    def _():
        for copy in copies:
            copy.start()
        for copy in copies:
            copy.wait()
        save.start()

    @pl.when(pl.program_id(0) == pl.num_programs(0) - 1)
    def _():
        save.wait()


WEIGHT_SPECS = [pl.BlockSpec(memory_space=pltpu.SMEM)] + [pl.BlockSpec(memory_space=pl.ANY)] * 3


def weight_scratch(rows, columns):
    return [pltpu.VMEM((rows, columns), bf16), pltpu.SemaphoreType.DMA((64,))]


def pack_kernel(where_ref, q_ref, k_ref, v_ref, shard_ref, own_ref):
    half = own_ref.shape[0]
    first = where_ref[1] == 0
    for side in (0, 1):
        for which, ref in enumerate((q_ref, k_ref, v_ref)):
            columns = qkv_columns(which, side)
            block = ref[:, side * D // 2 : (side + 1) * D // 2]
            shard_ref[:, columns] = block
            own_ref[:, columns] = jnp.where(first, block[:half], block[half:])


def pack_qkv(where, q, k, v):
    part = q.shape[0]
    return pl.pallas_call(
        pack_kernel,
        in_specs=[pl.BlockSpec(memory_space=pltpu.SMEM)] + [pl.BlockSpec(memory_space=pltpu.VMEM)] * 3,
        out_specs=[pl.BlockSpec(memory_space=pltpu.VMEM)] * 2,
        out_shape=[sds((part, 3 * D), bf16), sds((part // 2, 3 * D), bf16)],
        compiler_params=params(),
        cost_estimate=cost(0, 4 * 2**20),
        name="pack_qkv",
    )(where, q, k, v)


def qkv_columns(which, side):
    begin = (3 * side + which) * D // 2
    return slice(begin, begin + D // 2)


def qkv_kernel(
    where_ref, shard, mine, other, before_ref, x_ref, behind_ref, bq_ref, bv_ref, q_ref, k_ref, v_ref, kt_ref, vt_ref, full_ref, w_ref, sem
):
    join_weight(where_ref, (shard, mine, other), w_ref, full_ref, sem)
    i = pl.program_id(0)
    x = jnp.where(i == 0, before_ref[...], jnp.where(i == pl.num_programs(0) - 1, behind_ref[...], x_ref[...]))

    @pl.when((i > 0) & (i < pl.num_programs(0) - 1))
    def _():
        for s in (0, 1):
            half = slice(s * D // 2, (s + 1) * D // 2)
            query = (nn(x, w_ref[:, qkv_columns(0, s)]) + bq_ref[:, half]).astype(bf16)
            q_ref[:, half] = query * jnp.asarray(HEAD**-0.5, bf16)

    for s in (0, 1):
        half = slice(s * D // 2, (s + 1) * D // 2)
        keys = nn(x, w_ref[:, qkv_columns(1, s)]).astype(bf16)
        k_ref[:, half] = keys
        kt_ref[half, :] = jnp.transpose(keys)
        values = (nn(x, w_ref[:, qkv_columns(2, s)]) + bv_ref[:, half]).astype(bf16)
        v_ref[:, half] = values
        vt_ref[half, :] = jnp.transpose(values)


def project_qkv(where, pieces, before, tokens, behind, bq, bv):
    rows = tokens.shape[0]
    span = rows + 2 * DOC_MAX
    rim = pl.BlockSpec((512, D), lambda i: (0, 0))
    inside = pl.BlockSpec((512, D), lambda i: (jnp.clip(i - 1, 0, rows // 512 - 1), 0))
    row = pl.BlockSpec((1, D), lambda i: (0, 0))
    tall = pl.BlockSpec((512, D), lambda i: (i, 0))
    wide = pl.BlockSpec((D, 512), lambda i: (0, i))
    return pl.pallas_call(
        qkv_kernel,
        grid=(span // 512,),
        in_specs=WEIGHT_SPECS + [rim, inside, rim, row, row],
        out_specs=[
            inside,
            tall,
            tall,
            wide,
            wide,
            pl.BlockSpec(memory_space=pl.ANY),
        ],
        scratch_shapes=weight_scratch(D, 3 * D),
        out_shape=[
            sds((rows, D), bf16),
            sds((span, D), bf16),
            sds((span, D), bf16),
            sds((D, span), bf16),
            sds((D, span), bf16),
            sds((D, 3 * D), bf16),
        ],
        compiler_params=params(),
        cost_estimate=cost(2 * D * D * (rows + 2 * span), 30 * 2**20),
        name="project_qkv",
    )(where, *pieces, before, tokens, behind, bq, bv)


def stack_rows(block, stack):
    lanes = lax.broadcasted_iota(jnp.int32, block.shape, 1)
    for h in range(4):
        stack[h*TILE:(h+1)*TILE, :] = jnp.where(lanes//HEAD==h, block, jnp.zeros_like(block))

def stack_columns(turned, stack):
    for h in range(4):
        hr = slice(h*HEAD,(h+1)*HEAD)
        stack[hr, h*TILE:(h+1)*TILE] = turned[hr, :]

def attn_fwd_kernel(lo_ref, hi_ref, q_ref, k_ref, vt_ref, idq_ref, idk_ref, *refs):
    out_ref, lse_ref, qs, acc, top, tot = refs[-6:]
    t = pl.program_id(1)
    @pl.when((t==0)&(pl.program_id(0)==0))
    def _():
        qs[...] = jnp.zeros_like(qs)
    stack_columns(jnp.transpose(q_ref[...]), qs)
    acc[...] = jnp.zeros_like(acc)
    top[...] = jnp.full_like(top, NEG)
    tot[...] = jnp.zeros_like(tot)
    def step(kt, carry):
        rows = pl.ds(pl.multiple_of(kt*TILE, TILE), TILE)
        bias = jnp.where(idk_ref[rows,:] == idq_ref[0], 0.0, NEG)
        vt_tile = vt_ref[:, rows]
        s = nn(k_ref[rows,:], qs[...])
        for h in range(4):
            cols = slice(h*TILE,(h+1)*TILE)
            hr = slice(h*HEAD,(h+1)*HEAD)
            sh = s[:, cols] + bias
            old = top[h:h+1,:]
            new = jnp.maximum(old, jnp.max(sh, axis=0, keepdims=True))
            top[h:h+1,:] = new
            p = jnp.exp(sh - new)
            fade = jnp.exp(old-new)
            tot[h:h+1,:] = tot[h:h+1,:]*fade + jnp.sum(p, axis=0, keepdims=True)
            acc[hr,:] = acc[hr,:]*fade + nn(vt_tile[hr,:], p.astype(bf16))
        return carry
    lax.fori_loop(lo_ref[t], hi_ref[t], step, 0)
    total = tot[...]
    inv = 1.0/total
    for h in range(4):
        hr = slice(h*HEAD,(h+1)*HEAD)
        acc[hr,:] = acc[hr,:]*inv[h:h+1,:]
    out_ref[...] = jnp.transpose(acc[...]).astype(bf16)
    lse_ref[0] = top[...] + jnp.log(total)

def attn_fwd(lo, hi, q, k_near, vt_near, idq_rows, idk_col, g0, ng, so_far=()):
    rows=q.shape[0]; span=k_near.shape[0]
    return pl.pallas_call(attn_fwd_kernel,
        grid_spec=pltpu.PrefetchScalarGridSpec(num_scalar_prefetch=2, grid=(ng, rows//TILE),
            in_specs=[pl.BlockSpec((TILE,256),lambda g,t,*_:(t,g+g0)),
                pl.BlockSpec((span,256),lambda g,t,*_:(0,g+g0)),
                pl.BlockSpec((256,span),lambda g,t,*_:(g+g0,0)),
                pl.BlockSpec((1,1,TILE),lambda g,t,*_:(t,0,0)),
                pl.BlockSpec((span,1),lambda g,t,*_:(0,0))] + [pl.BlockSpec(memory_space=pl.ANY)] * len(so_far),
            out_specs=[pl.BlockSpec((TILE,256),lambda g,t,*_:(t,g+g0)),
                pl.BlockSpec((1,8,TILE),lambda g,t,*_:(g+g0,0,t))],
            scratch_shapes=[pltpu.VMEM((256,4*TILE),bf16),
                pltpu.VMEM((256,TILE),f32),pltpu.VMEM((8,TILE),f32),pltpu.VMEM((8,TILE),f32)]),
        out_shape=[sds((rows,D),bf16),sds((D//256,8,rows),f32)],
        input_output_aliases={7+i: i for i in range(len(so_far))},
        compiler_params=params(),
        cost_estimate=cost(ng * 10**10, 2**21),
        name="attn_forward",
    )(lo,hi,q,k_near,vt_near,idq_rows,idk_col,*so_far)

def attn_bwd_kernel(lo_ref, hi_ref, q_ref, do_ref, ctx_ref, k_ref, kt_ref, v_ref, lse_ref, idq_ref, idk_ref,
        dq_ref, own_ref, low_ref, high_ref, qs, dos, qst, dost, dk_acc, dv_acc, dq_acc):
    t = pl.program_id(1)
    @pl.when((t==0)&(pl.program_id(0)==0))
    def _():
        qst[...] = jnp.zeros_like(qst)
        dost[...] = jnp.zeros_like(dost)
    @pl.when(t==0)
    def _():
        dk_acc[...] = jnp.zeros_like(dk_acc)
        dv_acc[...] = jnp.zeros_like(dv_acc)
    stack_rows(q_ref[...], qs)
    stack_rows(do_ref[...], dos)
    stack_columns(jnp.transpose(q_ref[...]), qst)
    stack_columns(jnp.transpose(do_ref[...]), dost)
    prod = do_ref[...].astype(f32)*ctx_ref[...].astype(f32)
    high = prod.astype(bf16)
    low = (prod-high.astype(f32)).astype(bf16)
    sel = (lax.broadcasted_iota(jnp.int32,(8,256),1)//HEAD == lax.broadcasted_iota(jnp.int32,(8,256),0)).astype(bf16)
    delta = nt(sel, high)+nt(sel, low)
    lse = lse_ref[0]
    delta_row = jnp.concatenate([delta[h:h+1] for h in range(4)],axis=1)
    lse_row = jnp.concatenate([lse[h:h+1] for h in range(4)],axis=1)
    dq_acc[...] = jnp.zeros_like(dq_acc)
    def step(kt, carry):
        rows = pl.ds(pl.multiple_of(kt*TILE, TILE), TILE)
        seen = idk_ref[rows,:] == idq_ref[0]
        bias = jnp.where(seen, 0.0, NEG)
        s = nn(k_ref[rows,:], qst[...])
        dp = nn(v_ref[rows,:], dost[...])
        p = jnp.exp(s + jnp.concatenate([bias]*4,axis=1) - lse_row)
        ds = (p*(dp-delta_row)).astype(bf16)
        dv_acc[rows,:] += nn(p.astype(bf16), dos[...])
        dk_acc[rows,:] += nn(ds, qs[...])
        kt_tile = kt_ref[:, rows]
        for h in range(4):
            hr=slice(h*HEAD,(h+1)*HEAD)
            dq_acc[hr,:] += nn(kt_tile[hr,:], ds[:, h*TILE:(h+1)*TILE])
        return carry
    lax.fori_loop(lo_ref[t], hi_ref[t], step, 0)
    dq_ref[...] = (jnp.transpose(dq_acc[...])*(HEAD**-0.5)).astype(bf16)
    @pl.when(t==pl.num_programs(1)-1)
    def _():
        for s, sums in ((0, dk_acc), (1, dv_acc)):
            low_ref[s] = sums[:DOC_MAX].astype(bf16)
            own_ref[s] = sums[DOC_MAX:-DOC_MAX].astype(bf16)
            high_ref[s] = sums[-DOC_MAX:].astype(bf16)

def attn_bwd(lo, hi, q, do, ctx, k_near, kt_near, v_near, lse, idq_rows, idk_col, g0, ng):
    rows=q.shape[0]; span=k_near.shape[0]
    return pl.pallas_call(attn_bwd_kernel,
        grid_spec=pltpu.PrefetchScalarGridSpec(num_scalar_prefetch=2, grid=(ng, rows//TILE),
            in_specs=[pl.BlockSpec((TILE,256),lambda g,t,*_:(t,g+g0)),
                pl.BlockSpec((TILE,256),lambda g,t,*_:(t,g+g0)),
                pl.BlockSpec((TILE,256),lambda g,t,*_:(t,g+g0)),
                pl.BlockSpec((span,256),lambda g,t,*_:(0,g+g0)),
                pl.BlockSpec((256,span),lambda g,t,*_:(g+g0,0)),
                pl.BlockSpec((span,256),lambda g,t,*_:(0,g+g0)),
                pl.BlockSpec((1,8,TILE),lambda g,t,*_:(g+g0,0,t)),
                pl.BlockSpec((1,1,TILE),lambda g,t,*_:(t,0,0)),
                pl.BlockSpec((span,1),lambda g,t,*_:(0,0))],
            out_specs=[pl.BlockSpec((TILE,256),lambda g,t,*_:(t,g)),
                pl.BlockSpec((2,rows,256),lambda g,t,*_:(0,0,g)),
                pl.BlockSpec((2,DOC_MAX,256),lambda g,t,*_:(0,0,g)),
                pl.BlockSpec((2,DOC_MAX,256),lambda g,t,*_:(0,0,g))],
            scratch_shapes=[pltpu.VMEM((4*TILE,256),bf16),pltpu.VMEM((4*TILE,256),bf16),
                pltpu.VMEM((256,4*TILE),bf16),pltpu.VMEM((256,4*TILE),bf16),
                pltpu.VMEM((span,256),f32),pltpu.VMEM((span,256),f32),pltpu.VMEM((256,TILE),f32)]),
        out_shape=[sds((rows,ng*256),bf16),sds((2,rows,ng*256),bf16),sds((2,DOC_MAX,ng*256),bf16),sds((2,DOC_MAX,ng*256),bf16)],
        compiler_params=params(),
        cost_estimate=cost(ng * 15 * 10**9, 2**22),
        name="attn_backward",
    )(lo,hi,q,do,ctx,k_near,kt_near,v_near,lse,idq_rows,idk_col)


def norm_stats(hidden):
    center = hidden - jnp.mean(hidden, axis=1, keepdims=True)
    rate = lax.rsqrt(jnp.mean(center * center, axis=1, keepdims=True) + NORM_EPS)
    return center * rate, rate


def norm_back(grad, unit, rate):
    return rate * (
        grad - jnp.mean(grad, axis=1, keepdims=True) - unit * jnp.mean(grad * unit, axis=1, keepdims=True)
    )


def mix_kernel(
    where_ref, shard, mine, other, c_ref, b_ref, x_ref, g_ref, s_ref,
    normed_ref, low_ref, rate_ref, full_ref, w_ref, sem,
):
    join_weight(where_ref, (shard, mine, other), w_ref, full_ref, sem)
    hidden = x_ref[...].astype(f32) + (nn(c_ref[...], w_ref[...]) + b_ref[...])
    unit, rate = norm_stats(hidden)
    normed = unit * g_ref[...] + s_ref[...]
    normed_ref[...] = normed
    low_ref[...] = normed.astype(bf16)
    rate_ref[...] = rate


def mix_and_norm(where, pieces, context, b, tokens, gain, shift):
    rows = tokens.shape[0]
    tile = pl.BlockSpec((TILE, D), lambda i: (i, 0))
    row = pl.BlockSpec((1, D), lambda i: (0, 0))
    return pl.pallas_call(
        mix_kernel,
        grid=(rows // TILE,),
        in_specs=WEIGHT_SPECS + [tile, row, tile, row, row],
        out_specs=[tile, tile, pl.BlockSpec((TILE, 1), lambda i: (i, 0)), pl.BlockSpec(memory_space=pl.ANY)],
        out_shape=[sds((rows, D), f32), sds((rows, D), bf16), sds((rows, 1), f32), sds((D, D), bf16)],
        scratch_shapes=weight_scratch(D, D),
        compiler_params=params(),
        cost_estimate=cost(2 * D * D * rows, 14 * 2**20),
        name="mix_and_norm",
    )(where, *pieces, context, b, tokens, gain, shift)


def gelu_parts(u):
    t = 1.0 / (1.0 + (0.3275911 * 0.7071067811865476) * jnp.abs(u))
    poly = t * (0.254829592 + t * (-0.284496736 + t * (1.421413741 + t * (-1.453152027 + t * 1.061405429))))
    bell = jnp.exp(-0.5 * u * u)
    tail = 0.5 * poly * bell
    share = jnp.where(u >= 0, 1.0 - tail, tail)
    return u * share, share + u * bell * 0.3989422804014327


def inner_kernel(where_ref, shard, mine, other, x_ref, b_ref, act_ref, slope_ref, full_ref, w_ref, sem):
    join_weight(where_ref, (shard, mine, other), w_ref, full_ref, sem)
    wide = act_ref.shape[1]
    columns = pl.ds(pl.multiple_of(pl.program_id(0) * wide, wide), wide)
    for i in range(x_ref.shape[0] // TILE):
        rows = slice(i * TILE, (i + 1) * TILE)
        act, slope = gelu_parts(nn(x_ref[rows, :], w_ref[:, columns]) + b_ref[...])
        act_ref[rows, :] = act.astype(bf16)
        slope_ref[rows, :] = slope.astype(bf16)


def inner_forward(where, pieces, x, b):
    rows, wide = x.shape[0], 512
    block = pl.BlockSpec((rows, wide), lambda j: (0, j))
    return pl.pallas_call(
        inner_kernel,
        grid=(FF // wide,),
        in_specs=WEIGHT_SPECS
        + [pl.BlockSpec((rows, D), lambda j: (0, 0)), pl.BlockSpec((1, wide), lambda j: (0, j))],
        out_specs=[block, block, pl.BlockSpec(memory_space=pl.ANY)],
        out_shape=[sds((rows, FF), bf16), sds((rows, FF), bf16), sds((D, FF), bf16)],
        scratch_shapes=weight_scratch(D, FF),
        compiler_params=params(),
        cost_estimate=cost(2 * D * FF * rows, 26 * 2**20),
        name="inner_forward",
    )(where, *pieces, x, b)


def outer_kernel(
    where_ref, shard, mine, other, coef_ref, act_ref, b_ref, normed_ref, g_ref, s_ref, teach_ref, cot_ref, flag_ref,
    out_ref, dsum_ref, dlow_ref, sums_ref, full_ref, w_ref, sem,
):
    join_weight(where_ref, (shard, mine, other), w_ref, full_ref, sem)
    hidden = normed_ref[...] + (nn(act_ref[...], w_ref[...]) + b_ref[...])
    unit, rate = norm_stats(hidden)
    gain = g_ref[...]
    final = unit * gain + s_ref[...]
    out_ref[...] = final.astype(bf16)
    error = final - teach_ref[...].astype(f32)
    marked = flag_ref[...] * error
    grad = cot_ref[...].astype(f32) + coef_ref[0] * marked
    dsum = norm_back(grad * gain, unit, rate)
    dsum_ref[...] = dsum
    low = dsum.astype(bf16)
    dlow_ref[...] = low

    @pl.when(pl.program_id(0) == 0)
    def _():
        sums_ref[...] = jnp.zeros_like(sums_ref)

    sums_ref[0:1, :] += jnp.sum(grad * unit, axis=0, keepdims=True)
    sums_ref[1:2, :] += jnp.sum(grad, axis=0, keepdims=True)
    sums_ref[2:3, :] += jnp.sum(low.astype(f32), axis=0, keepdims=True)
    sums_ref[3:4, :] += jnp.sum(marked * error, axis=0, keepdims=True)


def outer_forward(where, pieces, coef, act, b, normed, gain, shift, teacher, cotangent, flags):
    rows = act.shape[0]
    tile = pl.BlockSpec((TILE, D), lambda i: (i, 0))
    row = pl.BlockSpec((1, D), lambda i: (0, 0))
    return pl.pallas_call(
        outer_kernel,
        grid=(rows // TILE,),
        in_specs=WEIGHT_SPECS
        + [
            pl.BlockSpec(memory_space=pltpu.SMEM),
            pl.BlockSpec((TILE, FF), lambda i: (i, 0)),
            row, tile, row, row, tile, tile,
            pl.BlockSpec((TILE, 1), lambda i: (i, 0)),
        ],
        out_specs=[
            tile, tile, tile, pl.BlockSpec((8, D), lambda i: (0, 0)), pl.BlockSpec(memory_space=pl.ANY),
        ],
        out_shape=[
            sds((rows, D), bf16), sds((rows, D), f32), sds((rows, D), bf16), sds((8, D), f32), sds((FF, D), bf16),
        ],
        scratch_shapes=weight_scratch(FF, D),
        compiler_params=params(),
        cost_estimate=cost(2 * D * FF * rows, 32 * 2**20),
        name="outer_forward",
    )(where, *pieces, coef, act, b, normed, gain, shift, teacher, cotangent, flags)


def gram_kernel(order_ref, left_ref, *refs):
    rights, keep_ref, send_ref = refs[:-2], refs[-2], refs[-1]
    half = keep_ref.shape[1]
    first = order_ref[pl.num_programs(1)] == 0
    at = 0
    for right_ref in rights:
        grad = tn(left_ref[...], right_ref[...])
        columns = slice(at, at + right_ref.shape[1])
        at += right_ref.shape[1]
        low, high = grad[:half], grad[half:]
        keep_ref[0, :, columns] = jnp.where(first, low, high).astype(bf16)
        send_ref[0, :, columns] = jnp.where(first, high, low).astype(bf16)


def gram(order, left, rights, shards, wide=D):
    tokens, height = left.shape
    columns = sum(right.shape[1] for right in rights)
    part = height // shards
    steps = columns // wide if len(rights) == 1 else 1
    out = pl.BlockSpec((1, part // 2, columns // steps), lambda j, r, order_ref: (r, 0, j))
    return pl.pallas_call(
        gram_kernel,
        grid_spec=pltpu.PrefetchScalarGridSpec(
            num_scalar_prefetch=1,
            grid=(steps, shards),
            in_specs=[pl.BlockSpec((tokens, part), lambda j, r, order_ref: (0, order_ref[r]))]
            + [pl.BlockSpec((tokens, right.shape[1] // steps), lambda j, r, order_ref: (0, j)) for right in rights],
            out_specs=[out, out],
        ),
        out_shape=[sds((shards, part // 2, columns), bf16)] * 2,
        compiler_params=params(),
        cost_estimate=cost(2 * tokens * height * columns, 2 * (tokens * (height + columns) + height * columns)),
        name="gram",
    )(order, left, *rights)


def feed_back_columns(db_ref, wo_ref, slope_ref, wi_ref, dpre_ref, bias_ref, total):
    ones = jnp.ones((8, TILE), bf16)
    bias = jnp.zeros(bias_ref.shape, f32)
    for i in range(db_ref.shape[0] // TILE):
        rows = slice(i * TILE, (i + 1) * TILE)
        pre = (nt(db_ref[rows, :], wo_ref[...]) * slope_ref[rows, :].astype(f32)).astype(bf16)
        dpre_ref[rows, :] = pre
        bias += nn(ones, pre)
        total[rows, :] += nt(pre, wi_ref[...])
    bias_ref[...] = bias


def feed_back_first_kernel(tie_ref, db_ref, wo_ref, slope_ref, wi_ref, dsum_ref, dpre_ref, bias_ref, total):
    @pl.when(pl.program_id(0) == 0)
    def _():
        total[...] = dsum_ref[...]

    feed_back_columns(db_ref, wo_ref, slope_ref, wi_ref, dpre_ref, bias_ref, total)


def feed_back_last_kernel(
    tie_ref, db_ref, wo_ref, slope_ref, wi_ref, dsum_ref, normed_ref, rate_ref, g_ref, s_ref,
    dpre_ref, bias_ref, done_ref, dattn_ref, sums_ref, total,
):
    @pl.when(pl.program_id(0) == 0)
    def _():
        total[...] = dsum_ref[...]

    feed_back_columns(db_ref, wo_ref, slope_ref, wi_ref, dpre_ref, bias_ref, total)

    @pl.when(pl.program_id(0) == pl.num_programs(0) - 1)
    def _():
        gain = g_ref[...]
        sums_ref[...] = jnp.zeros_like(sums_ref)
        for i in range(db_ref.shape[0] // TILE):
            rows = slice(i * TILE, (i + 1) * TILE)
            grad = total[rows, :]
            unit = (normed_ref[rows, :] - s_ref[...]) / gain
            done = norm_back(grad * gain, unit, rate_ref[rows, :])
            done_ref[rows, :] = done
            low = done.astype(bf16)
            dattn_ref[rows, :] = low
            sums_ref[0:1, :] += jnp.sum(grad * unit, axis=0, keepdims=True)
            sums_ref[1:2, :] += jnp.sum(grad, axis=0, keepdims=True)
            sums_ref[2:3, :] += jnp.sum(low.astype(f32), axis=0, keepdims=True)


def feed_back(tie, side, d_branch, w_outer, slope, w_inner, so_far, norm=None):
    rows, wide = d_branch.shape[0], 512
    steps = FF // wide // 2
    begin = side * steps
    whole = pl.BlockSpec((rows, D), lambda j: (0, 0))
    row = pl.BlockSpec((1, D), lambda j: (0, 0))
    in_specs = [
        pl.BlockSpec(memory_space=pltpu.SMEM),
        whole,
        pl.BlockSpec((wide, D), lambda j: (j + begin, 0)),
        pl.BlockSpec((rows, wide), lambda j: (0, j + begin)),
        pl.BlockSpec((D, wide), lambda j: (0, j + begin)),
        whole,
    ]
    out_specs = [pl.BlockSpec((rows, wide), lambda j: (0, j)), pl.BlockSpec((8, wide), lambda j: (0, j)), whole]
    out_shape = [sds((rows, FF // 2), bf16), sds((8, FF // 2), f32), sds((rows, D), f32)]
    args = (tie, d_branch, w_outer, slope, w_inner, so_far)
    common = dict(grid=(steps,), compiler_params=params(), cost_estimate=cost(2 * D * FF * rows, 30 * 2**20))
    if norm is None:
        return pl.pallas_call(
            feed_back_first_kernel,
            in_specs=in_specs,
            out_specs=out_specs,
            out_shape=out_shape,
            name="feed_back_first",
            **common,
        )(*args)
    return pl.pallas_call(
        feed_back_last_kernel,
        in_specs=in_specs + [whole, pl.BlockSpec((rows, 1), lambda j: (0, 0)), row, row],
        out_specs=out_specs + [whole, pl.BlockSpec((8, D), lambda j: (0, 0))],
        out_shape=out_shape + [sds((rows, D), bf16), sds((8, D), f32)],
        scratch_shapes=[pltpu.VMEM((rows, D), f32)],
        name="feed_back_last",
        **common,
    )(*args, *norm)


def turn_kernel(d_ref, w_ref, out_ref):
    out_ref[...] = nt(d_ref[...], w_ref[...]).astype(bf16)


def turned_product(d, w):
    rows = d.shape[0]
    tile = pl.BlockSpec((TILE, D), lambda i: (i, 0))
    return pl.pallas_call(
        turn_kernel,
        grid=(rows // TILE,),
        in_specs=[tile, pl.BlockSpec((D, D), lambda i: (0, 0))],
        out_specs=tile,
        out_shape=sds((rows, D), bf16),
        compiler_params=params(),
        cost_estimate=cost(2 * D * D * rows, 6 * 2**20),
        name="turned_product",
    )(d, w)


def qkv_gradient_kernel(order_ref, x_ref, dq_ref, own_ref, before_ref, behind_ref, *refs):
    mixing, (keep_ref, send_ref, joined_ref, sums_ref) = refs[:-4], refs[-4:]
    rows, wide = dq_ref.shape
    half = keep_ref.shape[1]
    first = order_ref[pl.num_programs(0)] == 0

    @pl.when(pl.program_id(0) == 0)
    def _():
        ones = jnp.ones((8, rows), bf16)
        if rows > 2 * DOC_MAX:
            joined_ref[:, DOC_MAX:-DOC_MAX] = own_ref[:, DOC_MAX:-DOC_MAX]
        for s in (0, 1):
            for edge, part_ref in ((slice(0, DOC_MAX), before_ref), (slice(rows - DOC_MAX, rows), behind_ref)):
                joined_ref[s, edge] = (own_ref[s, edge].astype(f32) + part_ref[s].astype(f32)).astype(bf16)
        sums_ref[:, :wide] = nn(ones, dq_ref[...])
        sums_ref[:, wide:] = nn(ones, joined_ref[1])

    def put(begin, grad):
        columns = slice(begin, begin + grad.shape[1])
        low, high = grad[:half], grad[half:]
        keep_ref[0, :, columns] = jnp.where(first, low, high).astype(bf16)
        send_ref[0, :, columns] = jnp.where(first, high, low).astype(bf16)

    x = x_ref[...]
    put(0, tn(x, dq_ref[...]))
    put(wide, tn(x, joined_ref[0]))
    put(2 * wide, tn(x, joined_ref[1]))
    if mixing:
        context_ref, d_attn_ref = mixing
        put(3 * wide, tn(context_ref[...], d_attn_ref[...]))


def qkv_gradient(order, tokens, dq, own, before, behind, shards, mixing=()):
    rows, wide = dq.shape
    part = D // shards
    columns = 3 * wide + (D if mixing else 0)
    out = pl.BlockSpec((1, part // 2, columns), lambda r, order_ref: (r, 0, 0))
    left = pl.BlockSpec((rows, part), lambda r, order_ref: (0, order_ref[r]))
    whole = pl.BlockSpec((rows, wide), lambda r, order_ref: (0, 0))
    both = pl.BlockSpec((2, rows, wide), lambda r, order_ref: (0, 0, 0))
    rim = pl.BlockSpec((2, DOC_MAX, wide), lambda r, order_ref: (0, 0, 0))
    return pl.pallas_call(
        qkv_gradient_kernel,
        grid_spec=pltpu.PrefetchScalarGridSpec(
            num_scalar_prefetch=1,
            grid=(shards,),
            in_specs=[left, whole, both, rim, rim]
            + ([left, pl.BlockSpec((rows, D), lambda r, order_ref: (0, 0))] if mixing else []),
            out_specs=[out, out, both, pl.BlockSpec((8, 2 * wide), lambda r, order_ref: (0, 0))],
        ),
        out_shape=[sds((shards, part // 2, columns), bf16)] * 2 + [sds((2, rows, wide), bf16), sds((8, 2 * wide), f32)],
        compiler_params=params(),
        cost_estimate=cost(2 * rows * D * columns, 16 * 2**20),
        name="qkv_gradient",
    )(order, tokens, dq, own, before, behind, *mixing)


def input_kernel(base_ref, dq_ref, joined_ref, w_ref, out_ref):
    wide = dq_ref.shape[1]
    total = base_ref[...] + nt(dq_ref[...], w_ref[:, :wide])
    for s in (0, 1):
        total += nt(joined_ref[s], w_ref[:, (1 + s) * wide : (2 + s) * wide])
    out_ref[...] = total


def input_back(base, dq, joined, w, side):
    rows, wide = dq.shape
    tile = pl.BlockSpec((TILE, D), lambda i: (i, 0))
    return pl.pallas_call(
        input_kernel,
        grid=(rows // TILE,),
        in_specs=[
            tile,
            pl.BlockSpec((TILE, wide), lambda i: (i, 0)),
            pl.BlockSpec((2, TILE, wide), lambda i: (0, i, 0)),
            pl.BlockSpec((D, 3 * wide), lambda i: (0, side)),
        ],
        out_specs=tile,
        out_shape=sds((rows, D), f32),
        compiler_params=params(),
        cost_estimate=cost(6 * D * wide * rows, 14 * 2**20),
        name="input_back",
    )(base, dq, joined, w)


def swap(value, axis, bit):
    return lax.ppermute(value, axis, [(i, i ^ bit) for i in range(lax.axis_size(axis))])


def after(value, *others):
    return lax.optimization_barrier((value,) + others)[0]


def arrive(gate, value):
    return value if gate[0] is None else after(value, gate[0])


def gathering(gate, shard, own):
    n = lax.axis_size("fsdp")
    quarter = shard.shape[0] // 4
    near = [1 << b for b in range(n.bit_length() - 1)]
    whole = dict(zip(near, (yield [arrive(gate, swap(own, "fsdp", r)) for r in near])))
    held = {(r, s): value[s * quarter : (s + 1) * quarter] for r, value in whole.items() for s in (0, 1)}
    found = []
    for r in range(1, n):
        if r in whole:
            found.append(whole[r])
        else:
            for s, bit in ((0, 1 << (r.bit_length() - 1)), (1, r & -r)):
                held[r, s] = arrive(gate, swap(held[r ^ bit, s], "fsdp", bit))
                found.append(held[r, s])
    (mine,) = yield [jnp.concatenate(found, axis=0)]
    yield [shard, mine, arrive(gate, swap(mine, "ctx", 1))]


def half_sets(value, bit):
    shape = value.shape
    split = value.reshape((shape[0] // (2 * bit), 2, bit) + shape[1:])
    rest = (shape[0] // 2,) + shape[1:]
    return split[:, 0].reshape(rest), split[:, 1].reshape(rest)


def add_low(a, b):
    return (a.astype(f32) + b.astype(f32)).astype(bf16)


def reduction(gate, keep, send, parity):
    got = arrive(gate, swap(send, "ctx", 1))
    n = lax.axis_size("fsdp")
    quarter = keep.shape[1] // 2
    bits = [1 << b for b in range(n.bit_length() - 1)]
    streams = [(order, list(range(n))) for order in (bits, bits[::-1])]
    parts = [add_low(keep[:, s * quarter : (s + 1) * quarter], got[:, s * quarter : (s + 1) * quarter]) for s in (0, 1)]
    parts = list((yield parts))
    for k in range(len(bits)):
        for s, (order, ids) in enumerate(streams):
            bit = order[k]
            step = [i for i, r in enumerate(ids) if r & bit][0]
            ids[:] = [r for r in ids if not r & bit]
            mine, theirs = half_sets(parts[s], step)
            parts[s] = add_low(mine, arrive(gate, swap(theirs, "fsdp", bit)))
        if k < len(bits) - 1:
            parts = list((yield parts))
    value = jnp.concatenate([part[0] for part in parts], axis=0)
    (value,) = yield [value]
    count = lax.axis_size("ctx") // 2
    position = lax.axis_index("ctx") // 2
    half = count // 2

    def move(value, chip_pairs):
        pairs = [(2 * a + c, 2 * b + c) for a, b in chip_pairs for c in (0, 1)]
        return arrive(gate, lax.ppermute(value, "ctx", pairs))

    for s in range(half - 1):
        value = add_low(value, move(value, [(s, s + 1), (count - 1 - s, count - 2 - s)]))
        (value,) = yield [value]
    inner = (position == half - 1) | (position == half)
    across = move(value, [(half - 1, half), (half, half - 1)])
    value = jnp.where(inner, add_low(value, across), value)
    (value,) = yield [value]
    for s in reversed(range(half - 1)):
        back = move(value, [(s + 1, s), (count - 2 - s, count - 1 - s)])
        value = jnp.where((position == s) | (position == count - 1 - s), back, value)
        (value,) = yield [value]
    other = arrive(gate, swap(value, "ctx", 1))
    first = parity == 0
    yield [jnp.concatenate([jnp.where(first, value, other), jnp.where(first, other, value)], axis=0).astype(f32)]


def chip_sum(gate, keep, send, pause=0):
    value = add_low(keep, arrive(gate, swap(send, "ctx", 1)))
    (value,) = yield [value]
    (value,) = yield [lax.psum_scatter(value, "fsdp", scatter_dimension=0, tiled=True)[0]]
    for _ in range(pause):
        (value,) = yield [value]
    groups = [list(range(k, lax.axis_size("ctx"), 2)) for k in (0, 1)]
    yield [lax.psum(value, "ctx", axis_index_groups=groups)]


def both_halves(value, parity):
    other = swap(value, "ctx", 1)
    first = parity == 0
    return jnp.concatenate([jnp.where(first, value, other), jnp.where(first, other, value)], axis=0).astype(f32)


def summed(gate, value):
    (value,) = yield [value]
    for axis in ("ctx", "fsdp"):
        bit = 1
        while bit < lax.axis_size(axis):
            value = value + arrive(gate, swap(value, axis, bit))
            bit *= 2
            (value,) = yield [value]


class Staged:
    def __init__(self, stages, *args):
        self.gate, self.values, self.done = [None], None, False
        self.stages = stages(self.gate, *args)

    def step(self):
        try:
            self.values = self.stages.send(self.values)
        except StopIteration:
            self.done = True
        return not self.done

    def result(self):
        while self.step():
            pass
        return self.values


def boundary(done, tie, *transfers):
    moving = []
    for transfer in transfers:
        transfer.gate[0] = done
        if transfer.step():
            moving.append(transfer)
    tie, values = lax.optimization_barrier((tie, [transfer.values for transfer in moving], done))[:2]
    for transfer, value in zip(moving, values):
        transfer.values = value
    return tie


def gather_small(vector, f):
    n = lax.axis_size("fsdp")
    value = vector.reshape(1, -1)
    bit = 1
    while bit < n:
        value = jnp.concatenate([value, swap(value, "fsdp", bit)], axis=0)
        bit *= 2
    bit = 1
    while bit < n:
        split = value.reshape(n // (2 * bit), 2, bit, -1)
        value = jnp.where(f & bit > 0, split[:, ::-1], split).reshape(n, -1)
        bit *= 2
    return value


def body(
    layer_input,
    teacher_states,
    out_cotangent,
    doc_start,
    valid_flag,
    query_weight,
    query_bias,
    key_weight,
    value_weight,
    value_bias,
    proj_weight,
    proj_bias,
    attn_gain,
    attn_shift,
    inner_weight,
    inner_bias,
    outer_weight,
    outer_bias,
    final_gain,
    final_shift,
):
    n_ctx, n_fsdp = lax.axis_size("ctx"), lax.axis_size("fsdp")
    c, f = lax.axis_index("ctx"), lax.axis_index("fsdp")
    parity = c % 2
    tokens = layer_input[0]
    rows = tokens.shape[0]
    part = query_weight.shape[0]
    where = jnp.stack([f, parity]).astype(jnp.int32)
    order = jnp.concatenate([f ^ jnp.arange(n_fsdp, dtype=jnp.int32), parity[None].astype(jnp.int32)])

    def own_half(shard):
        half = shard.shape[0] // 2
        return lax.dynamic_slice_in_dim(shard, parity * half, half)

    qkv_shard, own_qkv = pack_qkv(where, query_weight, key_weight, value_weight)
    w_qkv = Staged(gathering, qkv_shard, own_qkv)
    w_qkv.step()
    own_proj, own_inner = after((own_half(proj_weight), own_half(inner_weight)), w_qkv.values)
    w_proj = Staged(gathering, proj_weight, own_proj)
    w_inner = Staged(gathering, inner_weight, own_inner)

    up = [(i, i + 1) for i in range(n_ctx - 1)]
    down = [(b, a) for a, b in up]
    before = lax.ppermute(tokens[rows - DOC_MAX :], "ctx", up)
    behind = lax.ppermute(tokens[:DOC_MAX], "ctx", down)

    small = jnp.concatenate(
        [query_bias, value_bias, proj_bias, attn_gain, attn_shift, outer_bias, final_gain, final_shift, inner_bias]
    )
    small = gather_small(small, f).astype(f32)
    vectors = [small[:, i * part : (i + 1) * part].reshape(1, D) for i in range(8)]
    b_query, b_value, b_proj, g_attn, s_attn, b_outer, g_final, s_final = vectors
    b_inner = small[:, 8 * part :].reshape(1, FF)

    flags = valid_flag[0].astype(f32)[:, None]
    counted = Staged(summed, after(jnp.full((8, 128), jnp.sum(flags), f32), w_qkv.values))

    position = c * rows
    starts = doc_start[0]
    near_starts = lax.dynamic_slice_in_dim(
        jnp.concatenate(
            [jnp.full((DOC_MAX,), -1, jnp.int32), starts, jnp.full((DOC_MAX,), 2**30, jnp.int32)]
        ),
        position,
        rows + 2 * DOC_MAX,
    )
    own_starts = near_starts[DOC_MAX : DOC_MAX + rows]
    count_tiles = rows // TILE
    low_tile = (own_starts[::TILE] - position + DOC_MAX) // TILE
    last = position + TILE * (1 + jnp.arange(count_tiles, dtype=jnp.int32)) - 1
    ends = jnp.sum((near_starts[None, :] <= last[:, None]).astype(jnp.int32), axis=1)
    high_tile = (ends + TILE - 1) // TILE
    idq = own_starts.reshape(count_tiles, 1, TILE)
    idk = near_starts[:, None]

    w_qkv.step()
    w_qkv.values, b_query, b_value, b_proj, g_attn, s_attn, b_inner, idq, idk, low_tile, high_tile = lax.optimization_barrier(
        (w_qkv.values, b_query, b_value, b_proj, g_attn, s_attn, b_inner, idq, idk, low_tile, high_tile)
    )

    def attend(side, tie, *so_far):
        return attn_fwd(tie, high_tile, query, keys, values_t, idq, idk, 2 * side, 2, so_far)

    query, keys, values, keys_t, values_t, w_qkv = project_qkv(where, w_qkv.result(), before, tokens, behind, b_query, b_value)
    context_a, log_a = attend(0, boundary(query, low_tile, w_proj, counted))
    tie, own_outer = boundary(context_a, (low_tile, own_half(outer_weight)), w_proj, w_inner, counted)
    w_outer = Staged(gathering, outer_weight, own_outer)
    context, log_totals = attend(1, tie, context_a, log_a)
    normed, normed_low, rate, w_proj = mix_and_norm(
        boundary(context, where, w_proj, w_inner, counted), w_proj.values, context, b_proj, tokens, g_attn, s_attn
    )
    act, slope, w_inner = inner_forward(boundary(normed, where, w_inner, w_outer, counted), w_inner.values, normed_low, b_inner)
    count = counted.result()[0][0, 0]
    coef = (n_fsdp * n_ctx * rows / count).reshape(1)
    tie = boundary(act, where, w_outer)
    layer_out, d_sum_two, d_branch, final_sums, w_outer = outer_forward(
        tie, w_outer.result(), coef, act, b_outer, normed, g_final, s_final, teacher_states[0], out_cotangent[0], flags
    )

    plain = jnp.concatenate([jnp.arange(n_fsdp, dtype=jnp.int32), order[n_fsdp:]])
    outer = Staged(chip_sum, *gram(plain, act, [d_branch], n_fsdp))
    d_pre_a, bias_a, so_far = feed_back(where, 0, d_branch, w_outer, slope, w_inner, d_sum_two)
    d_pre_b, bias_b, d_sum_one, d_attn, attn_sums = feed_back(
        boundary(d_pre_a, where, outer), 1, d_branch, w_outer, slope, w_inner, so_far, (normed, rate, g_attn, s_attn)
    )
    early = Staged(
        summed,
        jnp.concatenate(
            [final_sums[:4], attn_sums[:3], bias_a[:1].reshape(2, D), bias_b[:1].reshape(2, D), jnp.zeros((5, D), f32)]
        ),
    )
    inner_pair = gram(boundary(d_attn, plain), normed_low, [d_pre_a, d_pre_b], n_fsdp)
    inner = Staged(chip_sum, *inner_pair, 1)
    d_context = turned_product(d_attn, boundary(inner_pair[0], w_proj, early))

    def attend_back(side, tie):
        dq, own, low, high = attn_bwd(
            tie, high_tile, query, d_context, context, keys, keys_t, values, log_totals, idq, idk, 2 * side, 2
        )
        return dq, own, lax.ppermute(high, "ctx", up), lax.ppermute(low, "ctx", down)

    parts_a = attend_back(0, boundary(d_context, low_tile, outer, inner, early))
    *first_pair, joined_a, sums_a = qkv_gradient(
        boundary(parts_a[0], order, early), tokens, *parts_a, n_fsdp, (context, d_attn)
    )
    first = Staged(reduction, *first_pair, parity)
    parts_b = attend_back(1, boundary(first_pair[0], low_tile, inner, early))
    *last_pair, joined_b, sums_b = qkv_gradient(
        boundary(parts_b[0], order, first, outer, inner, early), tokens, *parts_b, n_fsdp
    )
    last = Staged(reduction, *last_pair, parity)
    late = jnp.stack([sums_a[0], sums_b[0]]).reshape(2, 2, D // 2).transpose(1, 0, 2).reshape(2, D)
    late = Staged(summed, jnp.concatenate([late, jnp.zeros((6, D), f32)]))
    input_a = input_back(
        d_sum_one, parts_a[0], joined_a, boundary(last_pair[0], w_qkv, first, early, late), 0
    )
    input_grad = input_back(
        input_a, parts_b[0], joined_b, boundary(input_a, w_qkv, last, first, early, late), 1
    )
    boundary(input_grad, where, last, first, late)
    first, last, early, late = (transfer.result()[0] for transfer in (first, last, early, late))
    outer_grad, inner_grad = both_halves(outer.result()[0], parity), both_halves(inner.result()[0], parity)
    proj_grad = first[:, 3 * D // 2 :]
    sixth = D // 2
    query_grad, key_grad, value_grad = (
        jnp.concatenate([grad[:, i * sixth : (i + 1) * sixth] for grad in (first, last)], axis=1)
        for i in range(3)
    )
    mse = jnp.sum(early[3]) / (count * D)

    def mine(vector):
        length = vector.shape[0] // n_fsdp
        return lax.dynamic_slice_in_dim(vector, f * length, length)

    return (
        layer_out[None],
        input_grad[None],
        mse,
        query_grad,
        mine(late[0]),
        key_grad,
        value_grad,
        mine(late[1]),
        proj_grad,
        mine(early[6]),
        mine(early[4]),
        mine(early[5]),
        inner_grad,
        mine(early[7:11].reshape(FF)),
        outer_grad,
        mine(early[2]),
        mine(early[0]),
        mine(early[1]),
    )


def solution(mesh):
    tokens = P("fsdp", "ctx", None)
    matrix, vector = P("fsdp", None), P("fsdp")
    weights = (
        matrix, vector, matrix, matrix, vector, matrix, vector, vector, vector, matrix, vector, matrix, vector, vector, vector,
    )
    return jax.shard_map(
        body,
        mesh=mesh,
        in_specs=(tokens, tokens, tokens, matrix, P("fsdp", "ctx")) + weights,
        out_specs=(tokens, tokens, P()) + weights,
        check_vma=False,
    )
```

```python
import functools

import jax
import jax.numpy as jnp
from jax import lax
from jax.experimental import pallas as pl
from jax.experimental.pallas import tpu as pltpu
from jax.sharding import PartitionSpec as P

D = 1024
FF = 4096
HEAD = 64
DOC_MAX = 512
TILE = 256
RIM = DOC_MAX // TILE
NEG = -1e30
NORM_EPS = 1e-05
VMEM_BYTES = 56 * 2**20
bf16 = jnp.bfloat16
f32 = jnp.float32


def nn(a, b):
    return jnp.dot(a, b, preferred_element_type=f32)


def nt(a, b):
    return lax.dot_general(a, b, (((1,), (1,)), ((), ())), preferred_element_type=f32)


def tn(a, b):
    return lax.dot_general(a, b, (((0,), (0,)), ((), ())), preferred_element_type=f32)


def params():
    return pltpu.CompilerParams(vmem_limit_bytes=VMEM_BYTES)


def cost(flops, bytes_accessed):
    return pl.CostEstimate(flops=int(flops), bytes_accessed=int(bytes_accessed), transcendentals=0)


def sds(shape, dtype):
    return jax.ShapeDtypeStruct(shape, dtype)


def weight_copies(where_ref, pieces, full, out, sem):
    shard, mine, other = pieces[0], pieces[1 : len(pieces) // 2 + 1], pieces[len(pieces) // 2 + 1 :]
    f, parity = where_ref[0], where_ref[1]
    rows = shard.shape[0]
    half, quarter = rows // 2, rows // 4
    copies = []

    def add(source, begin):
        begin = pl.multiple_of(begin, 16)
        copies.append(pltpu.make_async_copy(source, full.at[pl.ds(begin, source.shape[0])], sem.at[len(copies)]))

    add(shard, f * rows)
    at = 0
    for r in range(1, full.shape[0] // rows):
        base = jnp.bitwise_xor(f, r) * rows
        for offset in (0,) if r & (r - 1) == 0 else (0, quarter):
            add(mine[at], base + offset + parity * half)
            add(other[at], base + offset + (1 - parity) * half)
            at += 1
    return copies, pltpu.make_async_copy(full, out, sem.at[len(copies)])


def join_weight(where_ref, pieces, full, out, sem):
    copies, save = weight_copies(where_ref, pieces, full, out, sem)

    @pl.when(pl.program_id(0) == 0)
    def _():
        for copy in copies:
            copy.start()
        for copy in copies:
            copy.wait()
        save.start()

    @pl.when(pl.program_id(0) == pl.num_programs(0) - 1)
    def _():
        save.wait()


def weight_specs(pieces):
    return [pl.BlockSpec(memory_space=pltpu.SMEM)] + [pl.BlockSpec(memory_space=pl.ANY)] * len(pieces)


def weight_scratch(rows, columns):
    return [pltpu.VMEM((rows, columns), bf16), pltpu.SemaphoreType.DMA((64,))]


def pack_kernel(where_ref, q_ref, k_ref, v_ref, shard_ref, own_ref):
    half = own_ref.shape[0]
    first = where_ref[1] == 0
    for side in (0, 1):
        for which, ref in enumerate((q_ref, k_ref, v_ref)):
            columns = qkv_columns(which, side)
            block = ref[:, side * D // 2 : (side + 1) * D // 2]
            shard_ref[:, columns] = block
            own_ref[:, columns] = jnp.where(first, block[:half], block[half:])


def pack_shards(where, q, k, v):
    part = q.shape[0]
    return pl.pallas_call(
        pack_kernel,
        in_specs=[pl.BlockSpec(memory_space=pltpu.SMEM)] + [pl.BlockSpec(memory_space=pltpu.VMEM)] * 3,
        out_specs=[pl.BlockSpec(memory_space=pltpu.VMEM)] * 2,
        out_shape=[sds((part, 3 * D), bf16), sds((part // 2, 3 * D), bf16)],
        compiler_params=params(),
        cost_estimate=cost(0, 4 * 2**20),
        name="pack_shards",
    )(where, q, k, v)


def unpack_kernel(where_ref, packed_ref, *outs):
    packed = packed_ref[...].astype(f32)
    shards = packed.shape[0]
    at = 0
    for out in outs:
        part = out.shape[1] // shards
        for r in range(shards):
            begin = pl.multiple_of(jnp.bitwise_xor(where_ref[0], r) * part, part)
            out[:, pl.ds(begin, part)] = packed[r : r + 1, at : at + part]
        at += part


def unpack_vectors(where, packed):
    return pl.pallas_call(
        unpack_kernel,
        in_specs=[pl.BlockSpec(memory_space=pltpu.SMEM), pl.BlockSpec(memory_space=pltpu.VMEM)],
        out_specs=[pl.BlockSpec(memory_space=pltpu.VMEM)] * 9,
        out_shape=[sds((1, D), f32)] * 8 + [sds((1, FF), f32)],
        compiler_params=params(),
        cost_estimate=cost(0, 2**17),
        name="unpack_vectors",
    )(where, packed)


def qkv_columns(which, side):
    begin = (3 * side + which) * D // 2
    return slice(begin, begin + D // 2)


def qkv_kernel(count, where_ref, *refs):
    pieces, refs = refs[:count], refs[count:]
    before_ref, x_ref, behind_ref, bq_ref, bv_ref, q_ref, k_ref, v_ref, kt_ref, vt_ref, full_ref, w_ref, sem = refs
    join_weight(where_ref, pieces, w_ref, full_ref, sem)
    i = pl.program_id(0)
    x = jnp.where(i == 0, before_ref[...], jnp.where(i == pl.num_programs(0) - 1, behind_ref[...], x_ref[...]))

    for s in (0, 1):
        half = slice(s * D // 2, (s + 1) * D // 2)
        query = (nn(x, w_ref[:, qkv_columns(0, s)]) + bq_ref[:, half]).astype(bf16)
        q_ref[:, half] = query * jnp.asarray(HEAD**-0.5, bf16)
        keys = nn(x, w_ref[:, qkv_columns(1, s)]).astype(bf16)
        k_ref[:, half] = keys
        kt_ref[half, :] = jnp.transpose(keys)
        values = (nn(x, w_ref[:, qkv_columns(2, s)]) + bv_ref[:, half]).astype(bf16)
        v_ref[:, half] = values
        vt_ref[half, :] = jnp.transpose(values)


def project_qkv(where, pieces, before, tokens, behind, bq, bv):
    rows = tokens.shape[0]
    span = rows + 2 * DOC_MAX
    rim = pl.BlockSpec((512, D), lambda i: (0, 0))
    inside = pl.BlockSpec((512, D), lambda i: (jnp.clip(i - 1, 0, rows // 512 - 1), 0))
    row = pl.BlockSpec((1, D), lambda i: (0, 0))
    tall = pl.BlockSpec((512, D), lambda i: (i, 0))
    wide = pl.BlockSpec((D, 512), lambda i: (0, i))
    return pl.pallas_call(
        functools.partial(qkv_kernel, len(pieces)),
        grid=(span // 512,),
        in_specs=weight_specs(pieces) + [rim, inside, rim, row, row],
        out_specs=[
            tall,
            tall,
            tall,
            wide,
            wide,
            pl.BlockSpec(memory_space=pl.ANY),
        ],
        scratch_shapes=weight_scratch(D, 3 * D),
        out_shape=[
            sds((span, D), bf16),
            sds((span, D), bf16),
            sds((span, D), bf16),
            sds((D, span), bf16),
            sds((D, span), bf16),
            sds((D, 3 * D), bf16),
        ],
        compiler_params=params(),
        cost_estimate=cost(2 * D * D * (rows + 2 * span), 30 * 2**20),
        name="project_qkv",
    )(where, *pieces, before, tokens, behind, bq, bv)


def stack_rows(block, stack):
    lanes = lax.broadcasted_iota(jnp.int32, block.shape, 1)
    for h in range(4):
        stack[h * TILE : (h + 1) * TILE, :] = jnp.where(lanes // HEAD == h, block, jnp.zeros_like(block))


def stack_columns(turned, stack):
    for h in range(4):
        heads = slice(h * HEAD, (h + 1) * HEAD)
        stack[heads, h * TILE : (h + 1) * TILE] = turned[heads, :]


def attn_fwd_kernel(lo_ref, hi_ref, q_ref, k_ref, vt_ref, idq_ref, idk_ref, *refs):
    out_ref, lse_ref, qs, acc, top, tot = refs[-6:]
    quads = qs.shape[0]
    t = pl.program_id(0)

    @pl.when(t == 0)
    def _():
        qs[...] = jnp.zeros_like(qs)

    turned = jnp.transpose(q_ref[...])
    for g in range(quads):
        stack_columns(turned[g * 256 : (g + 1) * 256], qs.at[g])
    acc[...] = jnp.zeros_like(acc)
    top[...] = jnp.full_like(top, NEG)
    tot[...] = jnp.zeros_like(tot)

    def step(kt, carry):
        rows = pl.ds(pl.multiple_of(kt * TILE, TILE), TILE)
        bias = jnp.where(idk_ref[rows, :] == idq_ref[0], 0.0, NEG)
        scores = [nn(k_ref[rows, g * 256 : (g + 1) * 256], qs[g]) for g in range(quads)]
        for g in range(quads):
            vt_tile = vt_ref[g * 256 : (g + 1) * 256, rows]
            for h in range(4):
                heads = slice(h * HEAD, (h + 1) * HEAD)
                own = scores[g][:, h * TILE : (h + 1) * TILE] + bias
                old = top[g, h : h + 1, :]
                new = jnp.maximum(old, jnp.max(own, axis=0, keepdims=True))
                top[g, h : h + 1, :] = new
                p = jnp.exp(own - new)
                fade = jnp.exp(old - new)
                tot[g, h : h + 1, :] = tot[g, h : h + 1, :] * fade + jnp.sum(p, axis=0, keepdims=True)
                acc[g, heads, :] = acc[g, heads, :] * fade + nn(vt_tile[heads, :], p.astype(bf16))
        return carry

    lax.fori_loop(lo_ref[t + RIM], hi_ref[t + RIM], step, 0)
    for g in range(quads):
        total = tot[g]
        inverse = 1.0 / total
        for h in range(4):
            heads = slice(h * HEAD, (h + 1) * HEAD)
            acc[g, heads, :] = acc[g, heads, :] * inverse[h : h + 1, :]
        out_ref[:, g * 256 : (g + 1) * 256] = jnp.transpose(acc[g]).astype(bf16)
        lse_ref[g] = top[g] + jnp.log(total)


def attn_fwd(lo, hi, q, k_near, vt_near, idq_rows, idk_col, side, quads, so_far=()):
    span, wide = k_near.shape[0], quads * 256
    rows = span - 2 * DOC_MAX
    return pl.pallas_call(
        attn_fwd_kernel,
        grid_spec=pltpu.PrefetchScalarGridSpec(
            num_scalar_prefetch=2,
            grid=(rows // TILE,),
            in_specs=[
                pl.BlockSpec((TILE, wide), lambda t, *_: (t + RIM, side)),
                pl.BlockSpec((span, wide), lambda t, *_: (0, side)),
                pl.BlockSpec((wide, span), lambda t, *_: (side, 0)),
                pl.BlockSpec((1, 1, TILE), lambda t, *_: (t + RIM, 0, 0)),
                pl.BlockSpec((span, 1), lambda t, *_: (0, 0)),
            ]
            + [pl.BlockSpec(memory_space=pl.ANY)] * len(so_far),
            out_specs=[
                pl.BlockSpec((TILE, wide), lambda t, *_: (t, side)),
                pl.BlockSpec((quads, 8, TILE), lambda t, *_: (side, 0, t)),
            ],
            scratch_shapes=[
                pltpu.VMEM((quads, 256, 4 * TILE), bf16),
                pltpu.VMEM((quads, 256, TILE), f32),
                pltpu.VMEM((quads, 8, TILE), f32),
                pltpu.VMEM((quads, 8, TILE), f32),
            ],
        ),
        out_shape=[sds((rows, D), bf16), sds((D // 256, 8, rows), f32)],
        input_output_aliases={7 + i: i for i in range(len(so_far))},
        compiler_params=params(),
        cost_estimate=cost(quads * 10**10, 2**21),
        name="attn_forward",
    )(lo, hi, q, k_near, vt_near, idq_rows, idk_col, *so_far)


def attn_bwd_kernel(
    lo_ref, hi_ref, q_ref, before_ref, do_ref, behind_ref, k_ref, kt_ref, v_ref, stats_ref, idq_ref, idk_ref,
    dq_ref, joined_ref, qs, dos, qst, dost, dk_acc, dv_acc, dq_acc,
):
    t = pl.program_id(1)
    low, high = lo_ref[t], hi_ref[t]
    end = pl.num_programs(1) - RIM
    own_low, own_high = jnp.maximum(low, RIM), jnp.minimum(high, end)

    @pl.when((t == 0) & (pl.program_id(0) == 0))
    def _():
        qst[...] = jnp.zeros_like(qst)
        dost[...] = jnp.zeros_like(dost)

    @pl.when(t == 0)
    def _():
        dk_acc[...] = jnp.zeros_like(dk_acc)
        dv_acc[...] = jnp.zeros_like(dv_acc)

    @pl.when(low < high)
    def _():
        q = q_ref[...]
        do = jnp.where(t < RIM, before_ref[...], jnp.where(t >= end, behind_ref[...], do_ref[...]))
        stack_rows(q, qs)
        stack_rows(do, dos)
        stack_columns(jnp.transpose(q), qst)
        stack_columns(jnp.transpose(do), dost)
        lse_row, delta_row = (
            jnp.concatenate([stats_ref[s, 0, h : h + 1] for h in range(4)], axis=1) for s in (0, 1)
        )
        dq_acc[...] = jnp.zeros_like(dq_acc)

        def step(own, kt, carry):
            rows = pl.ds(pl.multiple_of(kt * TILE, TILE), TILE)
            bias = jnp.where(idk_ref[rows, :] == idq_ref[0], 0.0, NEG)
            s = nn(k_ref[rows, :], qst[...])
            dp = nn(v_ref[rows, :], dost[...])
            p = jnp.exp(s + jnp.concatenate([bias] * 4, axis=1) - lse_row)
            ds = (p * (dp - delta_row)).astype(bf16)
            if own:
                inside = pl.ds(pl.multiple_of((kt - RIM) * TILE, TILE), TILE)
                dv_acc[inside, :] += nn(p.astype(bf16), dos[...])
                dk_acc[inside, :] += nn(ds, qs[...])
            kt_tile = kt_ref[:, rows]
            for h in range(4):
                heads = slice(h * HEAD, (h + 1) * HEAD)
                dq_acc[heads, :] += nn(kt_tile[heads, :], ds[:, h * TILE : (h + 1) * TILE])
            return carry

        lax.fori_loop(low, jnp.minimum(high, RIM), functools.partial(step, False), 0)
        lax.fori_loop(own_low, own_high, functools.partial(step, True), 0)
        lax.fori_loop(jnp.maximum(low, end), high, functools.partial(step, False), 0)

        @pl.when((t >= RIM) & (t < end))
        def _():
            dq_ref[...] = (jnp.transpose(dq_acc[...]) * (HEAD**-0.5)).astype(bf16)

    @pl.when(t == pl.num_programs(1) - 1)
    def _():
        joined_ref[0] = dk_acc[...].astype(bf16)
        joined_ref[1] = dv_acc[...].astype(bf16)


def attn_bwd(lo, hi, q_near, before, do, behind, k_near, kt_near, v_near, stats, idq_rows, idk_col, side, quads):
    rows, span = do.shape[0], k_near.shape[0]
    tiles, first = rows // TILE, side * quads
    near = pl.BlockSpec((span, 256), lambda g, t, *_: (0, g + first))
    return pl.pallas_call(
        attn_bwd_kernel,
        grid_spec=pltpu.PrefetchScalarGridSpec(
            num_scalar_prefetch=2,
            grid=(quads, span // TILE),
            in_specs=[
                pl.BlockSpec((TILE, 256), lambda g, t, *_: (t, g + first)),
                pl.BlockSpec((TILE, 256), lambda g, t, *_: (jnp.clip(t, 0, RIM - 1), g + first)),
                pl.BlockSpec((TILE, 256), lambda g, t, *_: (jnp.clip(t - RIM, 0, tiles - 1), g + first)),
                pl.BlockSpec((TILE, 256), lambda g, t, *_: (jnp.clip(t - RIM - tiles, 0, RIM - 1), g + first)),
                near,
                pl.BlockSpec((256, span), lambda g, t, *_: (g + first, 0)),
                near,
                pl.BlockSpec((2, 1, 8, TILE), lambda g, t, *_: (0, g + first, 0, t)),
                pl.BlockSpec((1, 1, TILE), lambda g, t, *_: (t, 0, 0)),
                pl.BlockSpec((span, 1), lambda g, t, *_: (0, 0)),
            ],
            out_specs=[
                pl.BlockSpec((TILE, 256), lambda g, t, *_: (jnp.clip(t - RIM, 0, tiles - 1), g)),
                pl.BlockSpec((2, rows, 256), lambda g, t, *_: (0, 0, g)),
            ],
            scratch_shapes=[
                pltpu.VMEM((4 * TILE, 256), bf16),
                pltpu.VMEM((4 * TILE, 256), bf16),
                pltpu.VMEM((256, 4 * TILE), bf16),
                pltpu.VMEM((256, 4 * TILE), bf16),
                pltpu.VMEM((rows, 256), f32),
                pltpu.VMEM((rows, 256), f32),
                pltpu.VMEM((256, TILE), f32),
            ],
        ),
        out_shape=[sds((rows, quads * 256), bf16), sds((2, rows, quads * 256), bf16)],
        compiler_params=params(),
        cost_estimate=cost(quads * 15 * 10**9, 2**22),
        name="attn_backward",
    )(lo, hi, q_near, before, do, behind, k_near, kt_near, v_near, stats, idq_rows, idk_col)


def norm_stats(hidden):
    center = hidden - jnp.mean(hidden, axis=1, keepdims=True)
    rate = lax.rsqrt(jnp.mean(center * center, axis=1, keepdims=True) + NORM_EPS)
    return center * rate, rate


def norm_back(grad, unit, rate):
    return rate * (
        grad - jnp.mean(grad, axis=1, keepdims=True) - unit * jnp.mean(grad * unit, axis=1, keepdims=True)
    )


def mix_kernel(count, where_ref, *refs):
    pieces, refs = refs[:count], refs[count:]
    c_ref, b_ref, x_ref, g_ref, s_ref, normed_ref, low_ref, rate_ref, full_ref, w_ref, sem = refs
    join_weight(where_ref, pieces, w_ref, full_ref, sem)
    hidden = x_ref[...].astype(f32) + (nn(c_ref[...], w_ref[...]) + b_ref[...])
    unit, rate = norm_stats(hidden)
    normed = unit * g_ref[...] + s_ref[...]
    normed_ref[...] = normed
    low_ref[...] = normed.astype(bf16)
    rate_ref[...] = rate


def mix_and_norm(where, pieces, context, b, tokens, gain, shift):
    rows = tokens.shape[0]
    tile = pl.BlockSpec((TILE, D), lambda i: (i, 0))
    row = pl.BlockSpec((1, D), lambda i: (0, 0))
    return pl.pallas_call(
        functools.partial(mix_kernel, len(pieces)),
        grid=(rows // TILE,),
        in_specs=weight_specs(pieces) + [tile, row, tile, row, row],
        out_specs=[tile, tile, pl.BlockSpec((TILE, 1), lambda i: (i, 0)), pl.BlockSpec(memory_space=pl.ANY)],
        out_shape=[sds((rows, D), f32), sds((rows, D), bf16), sds((rows, 1), f32), sds((D, D), bf16)],
        scratch_shapes=weight_scratch(D, D),
        compiler_params=params(),
        cost_estimate=cost(2 * D * D * rows, 14 * 2**20),
        name="mix_and_norm",
    )(where, *pieces, context, b, tokens, gain, shift)


def gelu_parts(u):
    t = 1.0 / (1.0 + (0.3275911 * 0.7071067811865476) * jnp.abs(u))
    poly = t * (0.254829592 + t * (-0.284496736 + t * (1.421413741 + t * (-1.453152027 + t * 1.061405429))))
    bell = jnp.exp(-0.5 * u * u)
    tail = 0.5 * poly * bell
    share = jnp.where(u >= 0, 1.0 - tail, tail)
    return u * share, share + u * bell * 0.3989422804014327


def inner_kernel(count, where_ref, *refs):
    pieces, (x_ref, b_ref, act_ref, slope_ref, full_ref, w_ref, sem) = refs[:count], refs[count:]
    join_weight(where_ref, pieces, w_ref, full_ref, sem)
    wide = act_ref.shape[1]
    columns = pl.ds(pl.multiple_of(pl.program_id(0) * wide, wide), wide)
    weight = w_ref[:, columns]
    parts = [slice(i, i + 128) for i in range(0, x_ref.shape[0], 128)]
    ahead = nn(x_ref[parts[0], :], weight)
    for i, rows in enumerate(parts):
        pre = ahead
        if i + 1 < len(parts):
            ahead = nn(x_ref[parts[i + 1], :], weight)
        act, slope = gelu_parts(pre + b_ref[...])
        act_ref[rows, :] = act.astype(bf16)
        slope_ref[rows, :] = slope.astype(bf16)


def inner_forward(where, pieces, x, b):
    rows, wide = x.shape[0], 512
    block = pl.BlockSpec((rows, wide), lambda j: (0, j))
    return pl.pallas_call(
        functools.partial(inner_kernel, len(pieces)),
        grid=(FF // wide,),
        in_specs=weight_specs(pieces)
        + [pl.BlockSpec((rows, D), lambda j: (0, 0)), pl.BlockSpec((1, wide), lambda j: (0, j))],
        out_specs=[block, block, pl.BlockSpec(memory_space=pl.ANY)],
        out_shape=[sds((rows, FF), bf16), sds((rows, FF), bf16), sds((D, FF), bf16)],
        scratch_shapes=weight_scratch(D, FF),
        compiler_params=params(),
        cost_estimate=cost(2 * D * FF * rows, 26 * 2**20),
        name="inner_forward",
    )(where, *pieces, x, b)


def outer_kernel(count, where_ref, *refs):
    pieces, refs = refs[:count], refs[count:]
    coef_ref, act_ref, b_ref, normed_ref, g_ref, s_ref, teach_ref, cot_ref, flag_ref = refs[:9]
    out_ref, dsum_ref, dlow_ref, sums_ref, full_ref, w_ref, sem = refs[9:]
    join_weight(where_ref, pieces, w_ref, full_ref, sem)
    hidden = normed_ref[...] + (nn(act_ref[...], w_ref[...]) + b_ref[...])
    unit, rate = norm_stats(hidden)
    gain = g_ref[...]
    final = unit * gain + s_ref[...]
    out_ref[...] = final.astype(bf16)
    error = final - teach_ref[...].astype(f32)
    marked = flag_ref[...] * error
    grad = cot_ref[...].astype(f32) + coef_ref[0] * marked
    dsum = norm_back(grad * gain, unit, rate)
    dsum_ref[...] = dsum
    low = dsum.astype(bf16)
    dlow_ref[...] = low

    @pl.when(pl.program_id(0) == 0)
    def _():
        sums_ref[...] = jnp.zeros_like(sums_ref)

    sums_ref[0:1, :] += jnp.sum(grad * unit, axis=0, keepdims=True)
    sums_ref[1:2, :] += jnp.sum(grad, axis=0, keepdims=True)
    sums_ref[2:3, :] += jnp.sum(low.astype(f32), axis=0, keepdims=True)
    sums_ref[3:4, :] += jnp.sum(marked * error, axis=0, keepdims=True)


def outer_forward(where, pieces, coef, act, b, normed, gain, shift, teacher, cotangent, flags):
    rows = act.shape[0]
    tile = pl.BlockSpec((TILE, D), lambda i: (i, 0))
    row = pl.BlockSpec((1, D), lambda i: (0, 0))
    return pl.pallas_call(
        functools.partial(outer_kernel, len(pieces)),
        grid=(rows // TILE,),
        in_specs=weight_specs(pieces)
        + [
            pl.BlockSpec(memory_space=pltpu.SMEM),
            pl.BlockSpec((TILE, FF), lambda i: (i, 0)),
            row, tile, row, row, tile, tile,
            pl.BlockSpec((TILE, 1), lambda i: (i, 0)),
        ],
        out_specs=[
            tile, tile, tile, pl.BlockSpec((8, D), lambda i: (0, 0)), pl.BlockSpec(memory_space=pl.ANY),
        ],
        out_shape=[
            sds((rows, D), bf16), sds((rows, D), f32), sds((rows, D), bf16), sds((8, D), f32), sds((FF, D), bf16),
        ],
        scratch_shapes=weight_scratch(FF, D),
        compiler_params=params(),
        cost_estimate=cost(2 * D * FF * rows, 32 * 2**20),
        name="outer_forward",
    )(where, *pieces, coef, act, b, normed, gain, shift, teacher, cotangent, flags)


def put_halves(keep_ref, send_ref, first, begin, grad):
    half = keep_ref.shape[1]
    columns = slice(begin, begin + grad.shape[1])
    low, high = grad[:half], grad[half:]
    keep_ref[0, :, columns] = jnp.where(first, low, high).astype(bf16)
    send_ref[0, :, columns] = jnp.where(first, high, low).astype(bf16)


def gram_kernel(counts, order_ref, *refs):
    operands, keep_ref, send_ref = list(refs[:-2]), refs[-2], refs[-1]
    first = order_ref[pl.num_programs(0)] == 0
    at = 0
    for count in counts:
        left = operands.pop(0)[...]
        for _ in range(count):
            right_ref = operands.pop(0)
            put_halves(keep_ref, send_ref, first, at, tn(left, right_ref[...]))
            at += right_ref.shape[1]


def gram(order, shards, *groups):
    tokens, height = groups[0][0].shape
    part = height // shards
    columns = sum(right.shape[1] for group in groups for right in group[1:])
    out = pl.BlockSpec((1, part // 2, columns), lambda r, order_ref: (r, 0, 0))
    in_specs = []
    for group in groups:
        in_specs.append(pl.BlockSpec((tokens, part), lambda r, order_ref: (0, order_ref[r])))
        in_specs += [pl.BlockSpec((tokens, right.shape[1]), lambda r, order_ref: (0, 0)) for right in group[1:]]
    return pl.pallas_call(
        functools.partial(gram_kernel, [len(group) - 1 for group in groups]),
        grid_spec=pltpu.PrefetchScalarGridSpec(
            num_scalar_prefetch=1, grid=(shards,), in_specs=in_specs, out_specs=[out, out]
        ),
        out_shape=[sds((shards, part // 2, columns), bf16)] * 2,
        compiler_params=params(),
        cost_estimate=cost(2 * tokens * height * columns, 2 * (tokens * (height + columns) + height * columns)),
        name="gram",
    )(order, *[operand for group in groups for operand in group])


def feed_back_columns(db_ref, wo_ref, slope_ref, wi_ref, dpre_ref, bias_ref, total):
    ones = jnp.ones((8, TILE), bf16)
    bias = jnp.zeros(bias_ref.shape, f32)
    for i in range(db_ref.shape[0] // TILE):
        rows = slice(i * TILE, (i + 1) * TILE)
        pre = (nt(db_ref[rows, :], wo_ref[...]) * slope_ref[rows, :].astype(f32)).astype(bf16)
        dpre_ref[rows, :] = pre
        bias += nn(ones, pre)
        total[rows, :] += nt(pre, wi_ref[...])
    bias_ref[...] = bias


def feed_back_first_kernel(tie_ref, db_ref, wo_ref, slope_ref, wi_ref, dsum_ref, dpre_ref, bias_ref, total):
    @pl.when(pl.program_id(0) == 0)
    def _():
        total[...] = dsum_ref[...]

    feed_back_columns(db_ref, wo_ref, slope_ref, wi_ref, dpre_ref, bias_ref, total)


def feed_back_last_kernel(
    tie_ref, db_ref, wo_ref, slope_ref, wi_ref, dsum_ref, normed_ref, rate_ref, g_ref, s_ref,
    dpre_ref, bias_ref, done_ref, dattn_ref, sums_ref, total,
):
    @pl.when(pl.program_id(0) == 0)
    def _():
        total[...] = dsum_ref[...]

    feed_back_columns(db_ref, wo_ref, slope_ref, wi_ref, dpre_ref, bias_ref, total)

    @pl.when(pl.program_id(0) == pl.num_programs(0) - 1)
    def _():
        gain = g_ref[...]
        sums_ref[...] = jnp.zeros_like(sums_ref)
        for i in range(db_ref.shape[0] // TILE):
            rows = slice(i * TILE, (i + 1) * TILE)
            grad = total[rows, :]
            unit = (normed_ref[rows, :] - s_ref[...]) / gain
            done = norm_back(grad * gain, unit, rate_ref[rows, :])
            done_ref[rows, :] = done
            low = done.astype(bf16)
            dattn_ref[rows, :] = low
            sums_ref[0:1, :] += jnp.sum(grad * unit, axis=0, keepdims=True)
            sums_ref[1:2, :] += jnp.sum(grad, axis=0, keepdims=True)
            sums_ref[2:3, :] += jnp.sum(low.astype(f32), axis=0, keepdims=True)


def feed_back(tie, side, d_branch, w_outer, slope, w_inner, so_far, norm=None):
    rows, wide = d_branch.shape[0], 512
    steps = FF // wide // 2
    begin = side * steps
    whole = pl.BlockSpec((rows, D), lambda j: (0, 0))
    row = pl.BlockSpec((1, D), lambda j: (0, 0))
    in_specs = [
        pl.BlockSpec(memory_space=pltpu.SMEM),
        whole,
        pl.BlockSpec((wide, D), lambda j: (j + begin, 0)),
        pl.BlockSpec((rows, wide), lambda j: (0, j + begin)),
        pl.BlockSpec((D, wide), lambda j: (0, j + begin)),
        whole,
    ]
    out_specs = [pl.BlockSpec((rows, wide), lambda j: (0, j)), pl.BlockSpec((8, wide), lambda j: (0, j)), whole]
    out_shape = [sds((rows, FF // 2), bf16), sds((8, FF // 2), f32), sds((rows, D), f32)]
    args = (tie, d_branch, w_outer, slope, w_inner, so_far)
    common = dict(grid=(steps,), compiler_params=params(), cost_estimate=cost(2 * D * FF * rows, 30 * 2**20))
    if norm is None:
        return pl.pallas_call(
            feed_back_first_kernel,
            in_specs=in_specs,
            out_specs=out_specs,
            out_shape=out_shape,
            name="feed_back_first",
            **common,
        )(*args)
    return pl.pallas_call(
        feed_back_last_kernel,
        in_specs=in_specs + [whole, pl.BlockSpec((rows, 1), lambda j: (0, 0)), row, row],
        out_specs=out_specs + [whole, pl.BlockSpec((8, D), lambda j: (0, 0))],
        out_shape=out_shape + [sds((rows, D), bf16), sds((8, D), f32)],
        scratch_shapes=[pltpu.VMEM((rows, D), f32)],
        name="feed_back_last",
        **common,
    )(*args, *norm)


def turn_kernel(d_ref, w_ref, context_ref, out_ref, delta_ref):
    out = nt(d_ref[...], w_ref[...]).astype(bf16)
    out_ref[...] = out
    select = (
        lax.broadcasted_iota(jnp.int32, (8, 256), 1) // HEAD == lax.broadcasted_iota(jnp.int32, (8, 256), 0)
    ).astype(bf16)
    for g in range(D // 256):
        lanes = slice(g * 256, (g + 1) * 256)
        product = out[:, lanes].astype(f32) * context_ref[:, lanes].astype(f32)
        high = product.astype(bf16)
        low = (product - high.astype(f32)).astype(bf16)
        delta_ref[g] = nt(select, high) + nt(select, low)


def context_back(d, w, context):
    rows = d.shape[0]
    tile = pl.BlockSpec((TILE, D), lambda i: (i, 0))
    return pl.pallas_call(
        turn_kernel,
        grid=(rows // TILE,),
        in_specs=[tile, pl.BlockSpec((D, D), lambda i: (0, 0)), tile],
        out_specs=[tile, pl.BlockSpec((D // 256, 8, TILE), lambda i: (0, 0, i))],
        out_shape=[sds((rows, D), bf16), sds((D // 256, 8, rows), f32)],
        compiler_params=params(),
        cost_estimate=cost(2 * D * D * rows, 8 * 2**20),
        name="context_back",
    )(d, w, context)


def qkv_gradient_kernel(used, order_ref, x_ref, dq_ref, joined_ref, *refs):
    riders, (keep_ref, send_ref, sums_ref, rider) = refs[:-4], refs[-4:]
    rows, wide = dq_ref.shape
    first = order_ref[pl.num_programs(0)] == 0

    @pl.when(pl.program_id(0) == 0)
    def _():
        ones = jnp.ones((8, rows), bf16)
        sums_ref[:, :wide] = nn(ones, dq_ref[...])
        sums_ref[:, wide:] = nn(ones, joined_ref[1])

    x = x_ref[...]
    for i, grad in enumerate((dq_ref[...], joined_ref[0], joined_ref[1])):
        put_halves(keep_ref, send_ref, first, i * wide, tn(x, grad))
    if keep_ref.shape[2] > 3 * wide:
        lanes = rider.shape[1]

        @pl.when(pl.program_id(0) == 0)
        def _():
            rider[...] = jnp.zeros_like(rider)
            at = 0
            for ref, height in zip((*riders, sums_ref), (*used, 1)):
                for i in range(height):
                    for begin in range(0, ref.shape[1], lanes):
                        rider[at : at + 1, :] = ref[i : i + 1, begin : begin + lanes]
                        at += 1

        low = rider[...].astype(bf16)
        keep_ref[0, :, 3 * wide :] = low
        send_ref[0, :, 3 * wide :] = low


def qkv_gradient(order, tokens, dq, joined, shards, riders=()):
    rows, wide = dq.shape
    part = D // shards
    lanes = 16 * D // (part // 2)
    columns = 3 * wide + (lanes if riders else 0)
    sums = [array for array, _ in riders]
    out = pl.BlockSpec((1, part // 2, columns), lambda r, order_ref: (r, 0, 0))
    left = pl.BlockSpec((rows, part), lambda r, order_ref: (0, order_ref[r]))
    whole = pl.BlockSpec((rows, wide), lambda r, order_ref: (0, 0))
    both = pl.BlockSpec((2, rows, wide), lambda r, order_ref: (0, 0, 0))
    return pl.pallas_call(
        functools.partial(qkv_gradient_kernel, [height for _, height in riders]),
        grid_spec=pltpu.PrefetchScalarGridSpec(
            num_scalar_prefetch=1,
            grid=(shards,),
            in_specs=[left, whole, both]
            + [pl.BlockSpec(array.shape, lambda r, order_ref: (0, 0)) for array in sums],
            out_specs=[out, out, pl.BlockSpec((8, 2 * wide), lambda r, order_ref: (0, 0))],
            scratch_shapes=[pltpu.VMEM((part // 2, lanes), f32)],
        ),
        out_shape=[sds((shards, part // 2, columns), bf16)] * 2 + [sds((8, 2 * wide), f32)],
        compiler_params=params(),
        cost_estimate=cost(2 * rows * D * columns, 16 * 2**20),
        name="qkv_gradient",
    )(order, tokens, dq, joined, *sums)


def input_kernel(base_ref, *refs):
    grads, w_ref, out_ref = refs[:-2], refs[-2], refs[-1]
    total = base_ref[...]
    for side in (0, 1):
        dq_ref, joined_ref = grads[2 * side : 2 * side + 2]
        for which, grad in enumerate((dq_ref[...], joined_ref[0], joined_ref[1])):
            total += nt(grad, w_ref[:, qkv_columns(which, side)])
    out_ref[...] = total


def input_back(base, grads, w):
    rows = base.shape[0]
    tile = pl.BlockSpec((TILE, D), lambda i: (i, 0))
    side = [pl.BlockSpec((TILE, D // 2), lambda i: (i, 0)), pl.BlockSpec((2, TILE, D // 2), lambda i: (0, i, 0))]
    return pl.pallas_call(
        input_kernel,
        grid=(rows // TILE,),
        in_specs=[tile, *side, *side, pl.BlockSpec((D, 3 * D), lambda i: (0, 0))],
        out_specs=tile,
        out_shape=sds((rows, D), f32),
        compiler_params=params(),
        cost_estimate=cost(6 * D * D * rows, 20 * 2**20),
        name="input_back",
    )(base, *grads, w)


def swap(value, axis, bit):
    return lax.ppermute(value, axis, [(i, i ^ bit) for i in range(lax.axis_size(axis))])


def after(value, *others):
    return lax.optimization_barrier((value,) + others)[0]


def arrive(gate, value):
    return value if gate[0] is None else after(value, gate[0])


def gathering(gate, shard, own):
    n = lax.axis_size("fsdp")
    quarter = shard.shape[0] // 4
    near = [1 << b for b in range(n.bit_length() - 1)]
    whole = dict(zip(near, (yield [arrive(gate, swap(own, "fsdp", r)) for r in near])))
    held = {(r, s): value[s * quarter : (s + 1) * quarter] for r, value in whole.items() for s in (0, 1)}
    found = []
    for r in range(1, n):
        if r in whole:
            found.append(whole[r])
        else:
            for s, bit in ((0, 1 << (r.bit_length() - 1)), (1, r & -r)):
                held[r, s] = arrive(gate, swap(held[r ^ bit, s], "fsdp", bit))
                found.append(held[r, s])
    found = yield found
    yield [shard, *found, *[arrive(gate, swap(value, "ctx", 1)) for value in found]]


def half_sets(value, bit):
    shape = value.shape
    split = value.reshape((shape[0] // (2 * bit), 2, bit) + shape[1:])
    rest = (shape[0] // 2,) + shape[1:]
    return split[:, 0].reshape(rest), split[:, 1].reshape(rest)


def add_low(a, b):
    return (a.astype(f32) + b.astype(f32)).astype(bf16)


def reduction(gate, keep, send, parity, short=False):
    got = arrive(gate, swap(send, "ctx", 1))
    n = lax.axis_size("fsdp")
    quarter = keep.shape[1] // 2
    bits = [1 << b for b in range(n.bit_length() - 1)]
    streams = [(order, list(range(n))) for order in (bits, bits[::-1])]
    parts = [add_low(keep[:, s * quarter : (s + 1) * quarter], got[:, s * quarter : (s + 1) * quarter]) for s in (0, 1)]
    parts = list((yield parts))
    for k in range(len(bits)):
        for s, (order, ids) in enumerate(streams):
            bit = order[k]
            step = [i for i, r in enumerate(ids) if r & bit][0]
            ids[:] = [r for r in ids if not r & bit]
            mine, theirs = half_sets(parts[s], step)
            parts[s] = add_low(mine, arrive(gate, swap(theirs, "fsdp", bit)))
        if k < len(bits) - 1:
            parts = list((yield parts))
    value = jnp.concatenate([part[0] for part in parts], axis=0)
    (value,) = yield [value]
    if short:
        bit = 2
        while bit < lax.axis_size("ctx"):
            value = add_low(value, arrive(gate, swap(value, "ctx", bit)))
            (value,) = yield [value]
            bit *= 2
        yield from both_halves(gate, value, parity)
    else:
        yield from chain(gate, value, parity)


def chain(gate, value, parity):
    count = lax.axis_size("ctx") // 2
    position = lax.axis_index("ctx") // 2
    half = count // 2

    def move(value, chip_pairs):
        pairs = [(2 * a + c, 2 * b + c) for a, b in chip_pairs for c in (0, 1)]
        return arrive(gate, lax.ppermute(value, "ctx", pairs))

    for s in range(half - 1):
        value = add_low(value, move(value, [(s, s + 1), (count - 1 - s, count - 2 - s)]))
        (value,) = yield [value]
    inner = (position == half - 1) | (position == half)
    across = move(value, [(half - 1, half), (half, half - 1)])
    value = jnp.where(inner, add_low(value, across), value)
    (value,) = yield [value]
    for s in reversed(range(half - 1)):
        back = move(value, [(s + 1, s), (count - 2 - s, count - 1 - s)])
        value = jnp.where((position == s) | (position == count - 1 - s), back, value)
        (value,) = yield [value]
    yield from both_halves(gate, value, parity)


def wide_reduction(gate, keep, send, parity):
    value = add_low(keep, arrive(gate, swap(send, "ctx", 1)))
    (value,) = yield [value]
    (value,) = yield [lax.psum_scatter(value, "fsdp", scatter_dimension=0, tiled=True)[0]]
    yield from chain(gate, value, parity)


def both_halves(gate, value, parity):
    other = arrive(gate, swap(value, "ctx", 1))
    first = parity == 0
    yield [jnp.concatenate([jnp.where(first, value, other), jnp.where(first, other, value)], axis=0).astype(f32)]


def whole_reduction(gate, keep, send, parity):
    value = add_low(keep, arrive(gate, swap(send, "ctx", 1)))
    (value,) = yield [value]
    (value,) = yield [lax.psum_scatter(value, "fsdp", scatter_dimension=0, tiled=True)[0]]
    groups = [list(range(k, lax.axis_size("ctx"), 2)) for k in (0, 1)]
    (value,) = yield [lax.psum(value, "ctx", axis_index_groups=groups)]
    yield from both_halves(gate, value, parity)


class Staged:
    def __init__(self, stages, *args):
        self.gate, self.values, self.done = [None], None, False
        self.stages = stages(self.gate, *args)

    def step(self):
        try:
            self.values = self.stages.send(self.values)
        except StopIteration:
            self.done = True
        return not self.done

    def result(self):
        while self.step():
            pass
        return self.values


def boundary(done, tie, *transfers, hold=()):
    moving = list(hold)
    for transfer in transfers:
        transfer.gate[0] = done
        if transfer.step():
            moving.append(transfer)
    gates = () if done is None else (done,)
    tie, values = lax.optimization_barrier((tie, [transfer.values for transfer in moving], gates))[:2]
    for transfer, value in zip(moving, values):
        transfer.values = value
    return tie


def gathering_rows(gate, row):
    (value,) = yield [row]
    bit = 1
    while bit < lax.axis_size("fsdp"):
        value = jnp.concatenate([value, swap(value, "fsdp", bit)], axis=0)
        bit *= 2
        (value,) = yield [value]


def body(
    layer_input,
    teacher_states,
    out_cotangent,
    doc_start,
    valid_flag,
    query_weight,
    query_bias,
    key_weight,
    value_weight,
    value_bias,
    proj_weight,
    proj_bias,
    attn_gain,
    attn_shift,
    inner_weight,
    inner_bias,
    outer_weight,
    outer_bias,
    final_gain,
    final_shift,
):
    n_ctx, n_fsdp = lax.axis_size("ctx"), lax.axis_size("fsdp")
    c, f = lax.axis_index("ctx"), lax.axis_index("fsdp")
    parity = c % 2
    tokens = layer_input[0]
    rows = tokens.shape[0]
    part = query_weight.shape[0]
    where = jnp.stack([f, parity]).astype(jnp.int32)
    order = jnp.concatenate([f ^ jnp.arange(n_fsdp, dtype=jnp.int32), parity[None].astype(jnp.int32)])

    def own_half(shard):
        half = shard.shape[0] // 2
        return lax.dynamic_slice_in_dim(shard, parity * half, half)

    qkv_shard, own_qkv = pack_shards(where, query_weight, key_weight, value_weight)
    w_qkv = Staged(gathering, qkv_shard, own_qkv)

    up = [(i, i + 1) for i in range(n_ctx - 1)]
    down = [(b, a) for a, b in up]
    before = lax.ppermute(tokens[rows - DOC_MAX :], "ctx", up)
    behind = lax.ppermute(tokens[:DOC_MAX], "ctx", down)
    flags = valid_flag[0]
    valid = jnp.sum(flags)
    valid = jnp.pad(jnp.stack([valid // 64, valid % 64]).astype(bf16), (0, 126))
    flags = flags.astype(f32)[:, None]
    small = jnp.concatenate(
        [query_bias, value_bias, proj_bias, attn_gain, attn_shift, outer_bias, final_gain, final_shift, inner_bias, valid]
    )
    small = Staged(gathering_rows, small.reshape(1, -1))
    small.step()
    small.step()
    position = c * rows
    starts = doc_start[0]
    near_starts = lax.dynamic_slice_in_dim(
        jnp.concatenate(
            [jnp.full((DOC_MAX,), -1, jnp.int32), starts, jnp.full((DOC_MAX,), 2**30, jnp.int32)]
        ),
        position,
        rows + 2 * DOC_MAX,
    )
    tiles = near_starts.shape[0] // TILE
    low_tile = (near_starts[::TILE] - position + DOC_MAX) // TILE
    last = position - DOC_MAX + TILE * (1 + jnp.arange(tiles, dtype=jnp.int32)) - 1
    ends = jnp.sum((near_starts[None, :] <= last[:, None]).astype(jnp.int32), axis=1)
    high_tile = (ends + TILE - 1) // TILE
    inside = (jnp.arange(tiles) >= RIM) & (jnp.arange(tiles) < tiles - RIM)
    low_tile = jnp.where(inside, low_tile, jnp.maximum(low_tile, RIM))
    high_tile = jnp.where(inside, high_tile, jnp.minimum(high_tile, tiles - RIM))
    idq = near_starts.reshape(tiles, 1, TILE)
    idk = near_starts[:, None]

    before, behind, idq, idk, low_tile, high_tile, flags, own_proj, own_inner = boundary(
        None, (before, behind, idq, idk, low_tile, high_tile, flags, own_half(proj_weight), own_half(inner_weight)),
        w_qkv, small,
    )
    w_proj = Staged(gathering, proj_weight, own_proj)
    w_inner = Staged(gathering, inner_weight, own_inner)
    boundary(None, where, w_qkv)
    small = small.result()[0]
    valid = jnp.sum(small[:, -128:].astype(f32), axis=0)
    counted = valid[0] * 64 + valid[1]
    bit = 1
    while bit < n_ctx:
        counted = jnp.full((8, 128), counted, f32) if counted.ndim == 0 else counted
        counted = counted + swap(counted, "ctx", bit)
        bit *= 2
    count = counted[0, 0]
    b_query, b_value, b_proj, g_attn, s_attn, b_outer, g_final, s_final, b_inner = unpack_vectors(where, small)
    w_qkv.values, b_query, b_value, count = lax.optimization_barrier((w_qkv.values, b_query, b_value, count))

    def attend(side, tie, *so_far):
        return attn_fwd(tie, high_tile, query, keys, values_t, idq, idk, side, 2, so_far)

    query, keys, values, keys_t, values_t, w_qkv = project_qkv(where, w_qkv.result(), before, tokens, behind, b_query, b_value)
    tie, own_outer = boundary(query, (low_tile, own_half(outer_weight)), w_proj)
    w_outer = Staged(gathering, outer_weight, own_outer)
    context_a, log_a = attend(0, tie)
    context, log_totals = attend(1, boundary(context_a, low_tile, w_proj, w_inner, w_outer), context_a, log_a)
    normed, normed_low, rate, w_proj = mix_and_norm(
        boundary(context, where, w_proj, w_inner, w_outer), w_proj.values, context, b_proj, tokens, g_attn, s_attn
    )
    tie = boundary(normed, where, w_inner, w_outer)
    act, slope, w_inner = inner_forward(tie, w_inner.values, normed_low, b_inner)
    coef = (n_fsdp * n_ctx * rows / count).reshape(1)
    layer_out, d_sum_two, d_branch, final_sums, w_outer = outer_forward(
        where, w_outer.result(), coef, act, b_outer, normed, g_final, s_final, teacher_states[0], out_cotangent[0], flags
    )

    plain = jnp.concatenate([jnp.arange(n_fsdp, dtype=jnp.int32), order[n_fsdp:]])
    outer = Staged(wide_reduction, *gram(plain, n_fsdp, (act, d_branch)), parity)
    d_pre_a, bias_a, so_far = feed_back(where, 0, d_branch, w_outer, slope, w_inner, d_sum_two)
    d_pre_b, bias_b, d_sum_one, d_attn, attn_sums = feed_back(
        boundary(d_pre_a, where, outer), 1, d_branch, w_outer, slope, w_inner, so_far, (normed, rate, g_attn, s_attn)
    )
    inner_pair = gram(
        after(plain, d_attn), n_fsdp, (normed_low, d_pre_a, d_pre_b), (context, d_attn)
    )
    inner = Staged(whole_reduction, *inner_pair, parity)

    d_context, delta = context_back(after(d_attn, inner_pair[0]), w_proj, context)
    stats = jnp.stack([log_totals, delta])

    def rims(value, axis):
        size = value.shape[axis]
        before = lax.ppermute(lax.slice_in_dim(value, size - DOC_MAX, size, axis=axis), "ctx", up)
        behind = lax.ppermute(lax.slice_in_dim(value, 0, DOC_MAX, axis=axis), "ctx", down)
        return before, behind

    do_before, do_behind = rims(d_context, 0)
    stats_before, stats_behind = rims(stats, 3)
    stats = jnp.concatenate([stats_before, stats, stats_behind], axis=3)
    def attend_back(side, tie):
        return attn_bwd(
            tie, high_tile, query, do_before, d_context, do_behind, keys, keys_t, values, stats, idq, idk, side, 2
        )

    parts_a = attend_back(0, boundary(d_context, low_tile, outer, inner))
    *first_pair, sums_a = qkv_gradient(boundary(parts_a[0], order, outer), tokens, *parts_a, n_fsdp)
    first = Staged(reduction, *first_pair, parity)
    parts_b = attend_back(1, boundary(first_pair[0], low_tile, outer, inner))
    riders = [(final_sums, 4), (attn_sums, 3), (bias_a, 1), (bias_b, 1), (sums_a, 1)]
    *last_pair, sums_b = qkv_gradient(
        boundary(parts_b[0], order, first, hold=[outer]), tokens, *parts_b, n_fsdp, riders
    )
    last = Staged(reduction, *last_pair, parity, True)
    input_grad = input_back(d_sum_one, (*parts_a, *parts_b), boundary(last_pair[0], w_qkv, first))
    boundary(input_grad, where, last, first)
    boundary(last.values[0], where, last, first)
    boundary(last.values[0], where, last, first, outer, inner)
    outer_grad, inner_grad, first, last = (transfer.result()[0] for transfer in (outer, inner, first, last))
    vectors = last[: part // 2, 3 * D // 2 :].reshape(16, D)
    query_sum, value_sum = vectors[11:13].reshape(2, 2, D // 2).transpose(1, 0, 2).reshape(2, D)
    inner_grad, proj_grad = inner_grad[:, :FF], inner_grad[:, FF:]
    sixth = D // 2
    query_grad, key_grad, value_grad = (
        jnp.concatenate([grad[:, i * sixth : (i + 1) * sixth] for grad in (first, last)], axis=1)
        for i in range(3)
    )
    mse = jnp.sum(vectors[3]) / (count * D)

    def mine(vector):
        length = vector.shape[0] // n_fsdp
        return lax.dynamic_slice_in_dim(vector, f * length, length)

    return (
        layer_out[None],
        input_grad[None],
        mse,
        query_grad,
        mine(query_sum),
        key_grad,
        value_grad,
        mine(value_sum),
        proj_grad,
        mine(vectors[6]),
        mine(vectors[4]),
        mine(vectors[5]),
        inner_grad,
        mine(vectors[7:11].reshape(FF)),
        outer_grad,
        mine(vectors[2]),
        mine(vectors[0]),
        mine(vectors[1]),
    )


def solution(mesh):
    tokens = P("fsdp", "ctx", None)
    matrix, vector = P("fsdp", None), P("fsdp")
    weights = (
        matrix, vector, matrix, matrix, vector, matrix, vector, vector, vector, matrix, vector, matrix, vector, vector, vector,
    )
    return jax.shard_map(
        body,
        mesh=mesh,
        in_specs=(tokens, tokens, tokens, matrix, P("fsdp", "ctx")) + weights,
        out_specs=(tokens, tokens, P()) + weights,
        check_vma=False,
    )
```

```python
import functools

import jax
import jax.numpy as jnp
from jax import lax
from jax.experimental import pallas as pl
from jax.experimental.pallas import tpu as pltpu
from jax.sharding import PartitionSpec as P

D = 1024
FF = 4096
HEAD = 64
DOC_MAX = 512
TILE = 256
RIM = DOC_MAX // TILE
NEG = -1e30
NORM_EPS = 1e-05
VMEM_BYTES = 56 * 2**20
bf16 = jnp.bfloat16
f32 = jnp.float32


def nn(a, b):
    return jnp.dot(a, b, preferred_element_type=f32)


def nt(a, b):
    return lax.dot_general(a, b, (((1,), (1,)), ((), ())), preferred_element_type=f32)


def tn(a, b):
    return lax.dot_general(a, b, (((0,), (0,)), ((), ())), preferred_element_type=f32)


def params():
    return pltpu.CompilerParams(vmem_limit_bytes=VMEM_BYTES)


def cost(flops, bytes_accessed):
    return pl.CostEstimate(flops=int(flops), bytes_accessed=int(bytes_accessed), transcendentals=0)


def sds(shape, dtype):
    return jax.ShapeDtypeStruct(shape, dtype)


def weight_copies(where_ref, pieces, full, out, sem):
    shard, mine, other = pieces[0], pieces[1 : len(pieces) // 2 + 1], pieces[len(pieces) // 2 + 1 :]
    f, parity = where_ref[0], where_ref[1]
    rows = shard.shape[0]
    half, quarter = rows // 2, rows // 4
    copies = []

    def add(source, begin):
        begin = pl.multiple_of(begin, 16)
        copies.append(pltpu.make_async_copy(source, full.at[pl.ds(begin, source.shape[0])], sem.at[len(copies)]))

    add(shard, f * rows)
    at = 0
    for r in range(1, full.shape[0] // rows):
        base = jnp.bitwise_xor(f, r) * rows
        for offset in (0,) if r & (r - 1) == 0 else (0, quarter):
            add(mine[at], base + offset + parity * half)
            add(other[at], base + offset + (1 - parity) * half)
            at += 1
    return copies, pltpu.make_async_copy(full, out, sem.at[len(copies)])


def join_weight(where_ref, pieces, full, out, sem):
    copies, save = weight_copies(where_ref, pieces, full, out, sem)

    @pl.when(pl.program_id(0) == 0)
    def _():
        for copy in copies:
            copy.start()
        for copy in copies:
            copy.wait()
        save.start()

    @pl.when(pl.program_id(0) == pl.num_programs(0) - 1)
    def _():
        save.wait()


def weight_specs(pieces):
    return [pl.BlockSpec(memory_space=pltpu.SMEM)] + [pl.BlockSpec(memory_space=pl.ANY)] * len(pieces)


def weight_scratch(rows, columns):
    return [pltpu.VMEM((rows, columns), bf16), pltpu.SemaphoreType.DMA((64,))]


def pack_kernel(where_ref, q_ref, k_ref, v_ref, shard_ref, own_ref):
    half = own_ref.shape[0]
    first = where_ref[1] == 0
    for side in (0, 1):
        for which, ref in enumerate((q_ref, k_ref, v_ref)):
            columns = qkv_columns(which, side)
            block = ref[:, side * D // 2 : (side + 1) * D // 2]
            shard_ref[:, columns] = block
            own_ref[:, columns] = jnp.where(first, block[:half], block[half:])


def pack_shards(where, q, k, v):
    part = q.shape[0]
    return pl.pallas_call(
        pack_kernel,
        in_specs=[pl.BlockSpec(memory_space=pltpu.SMEM)] + [pl.BlockSpec(memory_space=pltpu.VMEM)] * 3,
        out_specs=[pl.BlockSpec(memory_space=pltpu.VMEM)] * 2,
        out_shape=[sds((part, 3 * D), bf16), sds((part // 2, 3 * D), bf16)],
        compiler_params=params(),
        cost_estimate=cost(0, 4 * 2**20),
        name="pack_shards",
    )(where, q, k, v)


def unpack_kernel(where_ref, packed_ref, *outs):
    packed = packed_ref[...].astype(f32)
    shards = packed.shape[0]
    at = 0
    for out in outs:
        part = out.shape[1] // shards
        for r in range(shards):
            begin = pl.multiple_of(jnp.bitwise_xor(where_ref[0], r) * part, part)
            out[:, pl.ds(begin, part)] = packed[r : r + 1, at : at + part]
        at += part


def unpack_vectors(where, packed):
    return pl.pallas_call(
        unpack_kernel,
        in_specs=[pl.BlockSpec(memory_space=pltpu.SMEM), pl.BlockSpec(memory_space=pltpu.VMEM)],
        out_specs=[pl.BlockSpec(memory_space=pltpu.VMEM)] * 9,
        out_shape=[sds((1, D), f32)] * 8 + [sds((1, FF), f32)],
        compiler_params=params(),
        cost_estimate=cost(0, 2**17),
        name="unpack_vectors",
    )(where, packed)


def qkv_columns(which, side):
    begin = (3 * side + which) * D // 2
    return slice(begin, begin + D // 2)


def qkv_kernel(count, where_ref, *refs):
    pieces, refs = refs[:count], refs[count:]
    before_ref, x_ref, behind_ref, bq_ref, bv_ref, q_ref, k_ref, v_ref, kt_ref, vt_ref, full_ref, w_ref, sem = refs
    join_weight(where_ref, pieces, w_ref, full_ref, sem)
    i = pl.program_id(0)
    x = jnp.where(i == 0, before_ref[...], jnp.where(i == pl.num_programs(0) - 1, behind_ref[...], x_ref[...]))

    for s in (0, 1):
        half = slice(s * D // 2, (s + 1) * D // 2)
        query = (nn(x, w_ref[:, qkv_columns(0, s)]) + bq_ref[:, half]).astype(bf16)
        q_ref[:, half] = query * jnp.asarray(HEAD**-0.5, bf16)
        keys = nn(x, w_ref[:, qkv_columns(1, s)]).astype(bf16)
        k_ref[:, half] = keys
        kt_ref[half, :] = jnp.transpose(keys)
        values = (nn(x, w_ref[:, qkv_columns(2, s)]) + bv_ref[:, half]).astype(bf16)
        v_ref[:, half] = values
        vt_ref[half, :] = jnp.transpose(values)


def project_qkv(where, pieces, before, tokens, behind, bq, bv):
    rows = tokens.shape[0]
    span = rows + 2 * DOC_MAX
    rim = pl.BlockSpec((512, D), lambda i: (0, 0))
    inside = pl.BlockSpec((512, D), lambda i: (jnp.clip(i - 1, 0, rows // 512 - 1), 0))
    row = pl.BlockSpec((1, D), lambda i: (0, 0))
    tall = pl.BlockSpec((512, D), lambda i: (i, 0))
    wide = pl.BlockSpec((D, 512), lambda i: (0, i))
    return pl.pallas_call(
        functools.partial(qkv_kernel, len(pieces)),
        grid=(span // 512,),
        in_specs=weight_specs(pieces) + [rim, inside, rim, row, row],
        out_specs=[
            tall,
            tall,
            tall,
            wide,
            wide,
            pl.BlockSpec(memory_space=pl.ANY),
        ],
        scratch_shapes=weight_scratch(D, 3 * D),
        out_shape=[
            sds((span, D), bf16),
            sds((span, D), bf16),
            sds((span, D), bf16),
            sds((D, span), bf16),
            sds((D, span), bf16),
            sds((D, 3 * D), bf16),
        ],
        compiler_params=params(),
        cost_estimate=cost(2 * D * D * (rows + 2 * span), 30 * 2**20),
        name="project_qkv",
    )(where, *pieces, before, tokens, behind, bq, bv)


def stack_rows(block, stack):
    lanes = lax.broadcasted_iota(jnp.int32, block.shape, 1)
    for h in range(4):
        stack[h * TILE : (h + 1) * TILE, :] = jnp.where(lanes // HEAD == h, block, jnp.zeros_like(block))


def stack_columns(turned, stack):
    for h in range(4):
        heads = slice(h * HEAD, (h + 1) * HEAD)
        stack[heads, h * TILE : (h + 1) * TILE] = turned[heads, :]


def attn_fwd_kernel(lo_ref, hi_ref, q_ref, k_ref, vt_ref, idq_ref, idk_ref, *refs):
    out_ref, lse_ref, qs, acc, top, tot = refs[-6:]
    quads = qs.shape[0]
    t = pl.program_id(0)

    @pl.when(t == 0)
    def _():
        qs[...] = jnp.zeros_like(qs)

    turned = jnp.transpose(q_ref[...])
    for g in range(quads):
        stack_columns(turned[g * 256 : (g + 1) * 256], qs.at[g])
    acc[...] = jnp.zeros_like(acc)
    top[...] = jnp.full_like(top, NEG)
    tot[...] = jnp.zeros_like(tot)

    def step(kt, carry):
        rows = pl.ds(pl.multiple_of(kt * TILE, TILE), TILE)
        bias = jnp.where(idk_ref[rows, :] == idq_ref[0], 0.0, NEG)
        scores = [nn(k_ref[rows, g * 256 : (g + 1) * 256], qs[g]) for g in range(quads)]
        for g in range(quads):
            vt_tile = vt_ref[g * 256 : (g + 1) * 256, rows]
            for h in range(4):
                heads = slice(h * HEAD, (h + 1) * HEAD)
                own = scores[g][:, h * TILE : (h + 1) * TILE] + bias
                old = top[g, h : h + 1, :]
                new = jnp.maximum(old, jnp.max(own, axis=0, keepdims=True))
                top[g, h : h + 1, :] = new
                p = jnp.exp(own - new)
                fade = jnp.exp(old - new)
                tot[g, h : h + 1, :] = tot[g, h : h + 1, :] * fade + jnp.sum(p, axis=0, keepdims=True)
                acc[g, heads, :] = acc[g, heads, :] * fade + nn(vt_tile[heads, :], p.astype(bf16))
        return carry

    lax.fori_loop(lo_ref[t + RIM], hi_ref[t + RIM], step, 0)
    for g in range(quads):
        total = tot[g]
        inverse = 1.0 / total
        for h in range(4):
            heads = slice(h * HEAD, (h + 1) * HEAD)
            acc[g, heads, :] = acc[g, heads, :] * inverse[h : h + 1, :]
        out_ref[:, g * 256 : (g + 1) * 256] = jnp.transpose(acc[g]).astype(bf16)
        lse_ref[g] = top[g] + jnp.log(total)


def attn_fwd(lo, hi, q, k_near, vt_near, idq_rows, idk_col, side, quads, so_far=()):
    span, wide = k_near.shape[0], quads * 256
    rows = span - 2 * DOC_MAX
    return pl.pallas_call(
        attn_fwd_kernel,
        grid_spec=pltpu.PrefetchScalarGridSpec(
            num_scalar_prefetch=2,
            grid=(rows // TILE,),
            in_specs=[
                pl.BlockSpec((TILE, wide), lambda t, *_: (t + RIM, side)),
                pl.BlockSpec((span, wide), lambda t, *_: (0, side)),
                pl.BlockSpec((wide, span), lambda t, *_: (side, 0)),
                pl.BlockSpec((1, 1, TILE), lambda t, *_: (t + RIM, 0, 0)),
                pl.BlockSpec((span, 1), lambda t, *_: (0, 0)),
            ]
            + [pl.BlockSpec(memory_space=pl.ANY)] * len(so_far),
            out_specs=[
                pl.BlockSpec((TILE, wide), lambda t, *_: (t, side)),
                pl.BlockSpec((quads, 8, TILE), lambda t, *_: (side, 0, t)),
            ],
            scratch_shapes=[
                pltpu.VMEM((quads, 256, 4 * TILE), bf16),
                pltpu.VMEM((quads, 256, TILE), f32),
                pltpu.VMEM((quads, 8, TILE), f32),
                pltpu.VMEM((quads, 8, TILE), f32),
            ],
        ),
        out_shape=[sds((rows, D), bf16), sds((D // 256, 8, rows), f32)],
        input_output_aliases={7 + i: i for i in range(len(so_far))},
        compiler_params=params(),
        cost_estimate=cost(quads * 10**10, 2**21),
        name="attn_forward",
    )(lo, hi, q, k_near, vt_near, idq_rows, idk_col, *so_far)


def attn_bwd_kernel(
    lo_ref, hi_ref, q_ref, before_ref, do_ref, behind_ref, k_ref, kt_ref, v_ref, stats_ref, idq_ref, idk_ref, *refs
):
    dq_ref, joined_ref, qs, dos, qst, dost, dk_acc, dv_acc, dq_acc = refs[-9:]
    t = pl.program_id(1)
    low, high = lo_ref[t], hi_ref[t]
    end = pl.num_programs(1) - RIM
    own_low, own_high = jnp.maximum(low, RIM), jnp.minimum(high, end)

    @pl.when((t == 0) & (pl.program_id(0) == 0))
    def _():
        qst[...] = jnp.zeros_like(qst)
        dost[...] = jnp.zeros_like(dost)

    @pl.when(t == 0)
    def _():
        dk_acc[...] = jnp.zeros_like(dk_acc)
        dv_acc[...] = jnp.zeros_like(dv_acc)

    @pl.when(low < high)
    def _():
        q = q_ref[...]
        do = jnp.where(t < RIM, before_ref[...], jnp.where(t >= end, behind_ref[...], do_ref[...]))
        stack_rows(q, qs)
        stack_rows(do, dos)
        stack_columns(jnp.transpose(q), qst)
        stack_columns(jnp.transpose(do), dost)
        lse_row, delta_row = (
            jnp.concatenate([stats_ref[s, 0, h : h + 1] for h in range(4)], axis=1) for s in (0, 1)
        )
        dq_acc[...] = jnp.zeros_like(dq_acc)

        def step(own, kt, carry):
            rows = pl.ds(pl.multiple_of(kt * TILE, TILE), TILE)
            bias = jnp.where(idk_ref[rows, :] == idq_ref[0], 0.0, NEG)
            s = nn(k_ref[rows, :], qst[...])
            dp = nn(v_ref[rows, :], dost[...])
            p = jnp.exp(s + jnp.concatenate([bias] * 4, axis=1) - lse_row)
            ds = (p * (dp - delta_row)).astype(bf16)
            if own:
                inside = pl.ds(pl.multiple_of((kt - RIM) * TILE, TILE), TILE)
                dv_acc[inside, :] += nn(p.astype(bf16), dos[...])
                dk_acc[inside, :] += nn(ds, qs[...])
            kt_tile = kt_ref[:, rows]
            for h in range(4):
                heads = slice(h * HEAD, (h + 1) * HEAD)
                dq_acc[heads, :] += nn(kt_tile[heads, :], ds[:, h * TILE : (h + 1) * TILE])
            return carry

        lax.fori_loop(low, jnp.minimum(high, RIM), functools.partial(step, False), 0)
        lax.fori_loop(own_low, own_high, functools.partial(step, True), 0)
        lax.fori_loop(jnp.maximum(low, end), high, functools.partial(step, False), 0)

        @pl.when((t >= RIM) & (t < end))
        def _():
            dq_ref[...] = (jnp.transpose(dq_acc[...]) * (HEAD**-0.5)).astype(bf16)

    @pl.when(t == pl.num_programs(1) - 1)
    def _():
        joined_ref[0] = dk_acc[...].astype(bf16)
        joined_ref[1] = dv_acc[...].astype(bf16)


def attn_bwd(lo, hi, q_near, before, do, behind, k_near, kt_near, v_near, stats, idq_rows, idk_col, side, begin=0, quads=2, so_far=()):
    rows, span = do.shape[0], k_near.shape[0]
    tiles, first = rows // TILE, 2 * side + begin
    near = pl.BlockSpec((span, 256), lambda g, t, *_: (0, g + first))
    return pl.pallas_call(
        attn_bwd_kernel,
        grid_spec=pltpu.PrefetchScalarGridSpec(
            num_scalar_prefetch=2,
            grid=(quads, span // TILE),
            in_specs=[
                pl.BlockSpec((TILE, 256), lambda g, t, *_: (t, g + first)),
                pl.BlockSpec((TILE, 256), lambda g, t, *_: (jnp.clip(t, 0, RIM - 1), g + first)),
                pl.BlockSpec((TILE, 256), lambda g, t, *_: (jnp.clip(t - RIM, 0, tiles - 1), g + first)),
                pl.BlockSpec((TILE, 256), lambda g, t, *_: (jnp.clip(t - RIM - tiles, 0, RIM - 1), g + first)),
                near,
                pl.BlockSpec((256, span), lambda g, t, *_: (g + first, 0)),
                near,
                pl.BlockSpec((2, 1, 8, TILE), lambda g, t, *_: (0, g + first, 0, t)),
                pl.BlockSpec((1, 1, TILE), lambda g, t, *_: (t, 0, 0)),
                pl.BlockSpec((span, 1), lambda g, t, *_: (0, 0)),
            ]
            + [pl.BlockSpec(memory_space=pl.ANY)] * len(so_far),
            out_specs=[
                pl.BlockSpec((TILE, 256), lambda g, t, *_: (jnp.clip(t - RIM, 0, tiles - 1), g + begin)),
                pl.BlockSpec((2, rows, 256), lambda g, t, *_: (0, 0, g + begin)),
            ],
            scratch_shapes=[
                pltpu.VMEM((4 * TILE, 256), bf16),
                pltpu.VMEM((4 * TILE, 256), bf16),
                pltpu.VMEM((256, 4 * TILE), bf16),
                pltpu.VMEM((256, 4 * TILE), bf16),
                pltpu.VMEM((rows, 256), f32),
                pltpu.VMEM((rows, 256), f32),
                pltpu.VMEM((256, TILE), f32),
            ],
        ),
        out_shape=[sds((rows, 512), bf16), sds((2, rows, 512), bf16)],
        input_output_aliases={12 + i: i for i in range(len(so_far))},
        compiler_params=params(),
        cost_estimate=cost(quads * 15 * 10**9, 2**22),
        name="attn_backward",
    )(lo, hi, q_near, before, do, behind, k_near, kt_near, v_near, stats, idq_rows, idk_col, *so_far)


def norm_stats(hidden):
    center = hidden - jnp.mean(hidden, axis=1, keepdims=True)
    rate = lax.rsqrt(jnp.mean(center * center, axis=1, keepdims=True) + NORM_EPS)
    return center * rate, rate


def norm_back(grad, unit, rate):
    return rate * (
        grad - jnp.mean(grad, axis=1, keepdims=True) - unit * jnp.mean(grad * unit, axis=1, keepdims=True)
    )


def mix_kernel(count, where_ref, *refs):
    pieces, refs = refs[:count], refs[count:]
    c_ref, b_ref, x_ref, g_ref, s_ref, normed_ref, low_ref, rate_ref, full_ref, w_ref, sem = refs
    join_weight(where_ref, pieces, w_ref, full_ref, sem)
    hidden = x_ref[...].astype(f32) + (nn(c_ref[...], w_ref[...]) + b_ref[...])
    unit, rate = norm_stats(hidden)
    normed = unit * g_ref[...] + s_ref[...]
    normed_ref[...] = normed
    low_ref[...] = normed.astype(bf16)
    rate_ref[...] = rate


def mix_and_norm(where, pieces, context, b, tokens, gain, shift):
    rows = tokens.shape[0]
    tile = pl.BlockSpec((TILE, D), lambda i: (i, 0))
    row = pl.BlockSpec((1, D), lambda i: (0, 0))
    return pl.pallas_call(
        functools.partial(mix_kernel, len(pieces)),
        grid=(rows // TILE,),
        in_specs=weight_specs(pieces) + [tile, row, tile, row, row],
        out_specs=[tile, tile, pl.BlockSpec((TILE, 1), lambda i: (i, 0)), pl.BlockSpec(memory_space=pl.ANY)],
        out_shape=[sds((rows, D), f32), sds((rows, D), bf16), sds((rows, 1), f32), sds((D, D), bf16)],
        scratch_shapes=weight_scratch(D, D),
        compiler_params=params(),
        cost_estimate=cost(2 * D * D * rows, 14 * 2**20),
        name="mix_and_norm",
    )(where, *pieces, context, b, tokens, gain, shift)


def gelu_parts(u):
    t = 1.0 / (1.0 + (0.3275911 * 0.7071067811865476) * jnp.abs(u))
    poly = t * (0.254829592 + t * (-0.284496736 + t * (1.421413741 + t * (-1.453152027 + t * 1.061405429))))
    bell = jnp.exp(-0.5 * u * u)
    tail = 0.5 * poly * bell
    share = jnp.where(u >= 0, 1.0 - tail, tail)
    return u * share, share + u * bell * 0.3989422804014327


def inner_kernel(count, where_ref, *refs):
    pieces, (x_ref, b_ref, act_ref, slope_ref, full_ref, w_ref, sem) = refs[:count], refs[count:]
    join_weight(where_ref, pieces, w_ref, full_ref, sem)
    wide = act_ref.shape[1]
    columns = pl.ds(pl.multiple_of(pl.program_id(0) * wide, wide), wide)
    weight = w_ref[:, columns]
    parts = [slice(i, i + 128) for i in range(0, x_ref.shape[0], 128)]
    ahead = nn(x_ref[parts[0], :], weight)
    for i, rows in enumerate(parts):
        pre = ahead
        if i + 1 < len(parts):
            ahead = nn(x_ref[parts[i + 1], :], weight)
        act, slope = gelu_parts(pre + b_ref[...])
        act_ref[rows, :] = act.astype(bf16)
        slope_ref[rows, :] = slope.astype(bf16)


def inner_forward(where, pieces, x, b):
    rows, wide = x.shape[0], 512
    block = pl.BlockSpec((rows, wide), lambda j: (0, j))
    return pl.pallas_call(
        functools.partial(inner_kernel, len(pieces)),
        grid=(FF // wide,),
        in_specs=weight_specs(pieces)
        + [pl.BlockSpec((rows, D), lambda j: (0, 0)), pl.BlockSpec((1, wide), lambda j: (0, j))],
        out_specs=[block, block, pl.BlockSpec(memory_space=pl.ANY)],
        out_shape=[sds((rows, FF), bf16), sds((rows, FF), bf16), sds((D, FF), bf16)],
        scratch_shapes=weight_scratch(D, FF),
        compiler_params=params(),
        cost_estimate=cost(2 * D * FF * rows, 26 * 2**20),
        name="inner_forward",
    )(where, *pieces, x, b)


def outer_kernel(count, where_ref, *refs):
    pieces, refs = refs[:count], refs[count:]
    coef_ref, act_ref, b_ref, normed_ref, g_ref, s_ref, teach_ref, cot_ref, flag_ref = refs[:9]
    out_ref, dsum_ref, dlow_ref, sums_ref, full_ref, w_ref, sem = refs[9:]
    join_weight(where_ref, pieces, w_ref, full_ref, sem)
    hidden = normed_ref[...] + (nn(act_ref[...], w_ref[...]) + b_ref[...])
    unit, rate = norm_stats(hidden)
    gain = g_ref[...]
    final = unit * gain + s_ref[...]
    out_ref[...] = final.astype(bf16)
    error = final - teach_ref[...].astype(f32)
    marked = flag_ref[...] * error
    grad = cot_ref[...].astype(f32) + coef_ref[0] * marked
    dsum = norm_back(grad * gain, unit, rate)
    dsum_ref[...] = dsum
    low = dsum.astype(bf16)
    dlow_ref[...] = low

    @pl.when(pl.program_id(0) == 0)
    def _():
        sums_ref[...] = jnp.zeros_like(sums_ref)

    sums_ref[0:1, :] += jnp.sum(grad * unit, axis=0, keepdims=True)
    sums_ref[1:2, :] += jnp.sum(grad, axis=0, keepdims=True)
    sums_ref[2:3, :] += jnp.sum(low.astype(f32), axis=0, keepdims=True)
    sums_ref[3:4, :] += jnp.sum(marked * error, axis=0, keepdims=True)


def outer_forward(where, pieces, coef, act, b, normed, gain, shift, teacher, cotangent, flags):
    rows = act.shape[0]
    tile = pl.BlockSpec((TILE, D), lambda i: (i, 0))
    row = pl.BlockSpec((1, D), lambda i: (0, 0))
    return pl.pallas_call(
        functools.partial(outer_kernel, len(pieces)),
        grid=(rows // TILE,),
        in_specs=weight_specs(pieces)
        + [
            pl.BlockSpec(memory_space=pltpu.SMEM),
            pl.BlockSpec((TILE, FF), lambda i: (i, 0)),
            row, tile, row, row, tile, tile,
            pl.BlockSpec((TILE, 1), lambda i: (i, 0)),
        ],
        out_specs=[
            tile, tile, tile, pl.BlockSpec((8, D), lambda i: (0, 0)), pl.BlockSpec(memory_space=pl.ANY),
        ],
        out_shape=[
            sds((rows, D), bf16), sds((rows, D), f32), sds((rows, D), bf16), sds((8, D), f32), sds((FF, D), bf16),
        ],
        scratch_shapes=weight_scratch(FF, D),
        compiler_params=params(),
        cost_estimate=cost(2 * D * FF * rows, 32 * 2**20),
        name="outer_forward",
    )(where, *pieces, coef, act, b, normed, gain, shift, teacher, cotangent, flags)


def put_halves(keep_ref, send_ref, first, begin, grad):
    half = keep_ref.shape[1]
    columns = slice(begin, begin + grad.shape[1])
    low, high = grad[:half], grad[half:]
    keep_ref[0, :, columns] = jnp.where(first, low, high).astype(bf16)
    send_ref[0, :, columns] = jnp.where(first, high, low).astype(bf16)


def gram_kernel(counts, order_ref, *refs):
    operands, keep_ref, send_ref = list(refs[:-2]), refs[-2], refs[-1]
    first = order_ref[pl.num_programs(0)] == 0
    at = 0
    for count in counts:
        left = operands.pop(0)[...]
        for _ in range(count):
            right_ref = operands.pop(0)
            put_halves(keep_ref, send_ref, first, at, tn(left, right_ref[...]))
            at += right_ref.shape[1]


def gram(order, shards, *groups):
    tokens, height = groups[0][0].shape
    part = height // shards
    columns = sum(right.shape[1] for group in groups for right in group[1:])
    out = pl.BlockSpec((1, part // 2, columns), lambda r, order_ref: (r, 0, 0))
    in_specs = []
    for group in groups:
        in_specs.append(pl.BlockSpec((tokens, part), lambda r, order_ref: (0, order_ref[r])))
        in_specs += [pl.BlockSpec((tokens, right.shape[1]), lambda r, order_ref: (0, 0)) for right in group[1:]]
    return pl.pallas_call(
        functools.partial(gram_kernel, [len(group) - 1 for group in groups]),
        grid_spec=pltpu.PrefetchScalarGridSpec(
            num_scalar_prefetch=1, grid=(shards,), in_specs=in_specs, out_specs=[out, out]
        ),
        out_shape=[sds((shards, part // 2, columns), bf16)] * 2,
        compiler_params=params(),
        cost_estimate=cost(2 * tokens * height * columns, 2 * (tokens * (height + columns) + height * columns)),
        name="gram",
    )(order, *[operand for group in groups for operand in group])


def feed_back_columns(db_ref, wo_ref, slope_ref, wi_ref, dpre_ref, bias_ref, total):
    ones = jnp.ones((8, TILE), bf16)
    bias = jnp.zeros(bias_ref.shape, f32)
    for i in range(db_ref.shape[0] // TILE):
        rows = slice(i * TILE, (i + 1) * TILE)
        pre = (nt(db_ref[rows, :], wo_ref[...]) * slope_ref[rows, :].astype(f32)).astype(bf16)
        dpre_ref[rows, :] = pre
        bias += nn(ones, pre)
        total[rows, :] += nt(pre, wi_ref[...])
    bias_ref[...] = bias


def feed_back_first_kernel(tie_ref, db_ref, wo_ref, slope_ref, wi_ref, dsum_ref, dpre_ref, bias_ref, total):
    @pl.when(pl.program_id(0) == 0)
    def _():
        total[...] = dsum_ref[...]

    feed_back_columns(db_ref, wo_ref, slope_ref, wi_ref, dpre_ref, bias_ref, total)


def feed_back_last_kernel(
    tie_ref, db_ref, wo_ref, slope_ref, wi_ref, dsum_ref, normed_ref, rate_ref, g_ref, s_ref,
    dpre_ref, bias_ref, done_ref, dattn_ref, sums_ref, total,
):
    @pl.when(pl.program_id(0) == 0)
    def _():
        total[...] = dsum_ref[...]

    feed_back_columns(db_ref, wo_ref, slope_ref, wi_ref, dpre_ref, bias_ref, total)

    @pl.when(pl.program_id(0) == pl.num_programs(0) - 1)
    def _():
        gain = g_ref[...]
        sums_ref[...] = jnp.zeros_like(sums_ref)
        for i in range(db_ref.shape[0] // TILE):
            rows = slice(i * TILE, (i + 1) * TILE)
            grad = total[rows, :]
            unit = (normed_ref[rows, :] - s_ref[...]) / gain
            done = norm_back(grad * gain, unit, rate_ref[rows, :])
            done_ref[rows, :] = done
            low = done.astype(bf16)
            dattn_ref[rows, :] = low
            sums_ref[0:1, :] += jnp.sum(grad * unit, axis=0, keepdims=True)
            sums_ref[1:2, :] += jnp.sum(grad, axis=0, keepdims=True)
            sums_ref[2:3, :] += jnp.sum(low.astype(f32), axis=0, keepdims=True)


def feed_back(tie, side, d_branch, w_outer, slope, w_inner, so_far, norm=None):
    rows, wide = d_branch.shape[0], 512
    steps = FF // wide // 2
    begin = side * steps
    whole = pl.BlockSpec((rows, D), lambda j: (0, 0))
    row = pl.BlockSpec((1, D), lambda j: (0, 0))
    in_specs = [
        pl.BlockSpec(memory_space=pltpu.SMEM),
        whole,
        pl.BlockSpec((wide, D), lambda j: (j + begin, 0)),
        pl.BlockSpec((rows, wide), lambda j: (0, j + begin)),
        pl.BlockSpec((D, wide), lambda j: (0, j + begin)),
        whole,
    ]
    out_specs = [pl.BlockSpec((rows, wide), lambda j: (0, j)), pl.BlockSpec((8, wide), lambda j: (0, j)), whole]
    out_shape = [sds((rows, FF // 2), bf16), sds((8, FF // 2), f32), sds((rows, D), f32)]
    args = (tie, d_branch, w_outer, slope, w_inner, so_far)
    common = dict(grid=(steps,), compiler_params=params(), cost_estimate=cost(2 * D * FF * rows, 30 * 2**20))
    if norm is None:
        return pl.pallas_call(
            feed_back_first_kernel,
            in_specs=in_specs,
            out_specs=out_specs,
            out_shape=out_shape,
            name="feed_back_first",
            **common,
        )(*args)
    return pl.pallas_call(
        feed_back_last_kernel,
        in_specs=in_specs + [whole, pl.BlockSpec((rows, 1), lambda j: (0, 0)), row, row],
        out_specs=out_specs + [whole, pl.BlockSpec((8, D), lambda j: (0, 0))],
        out_shape=out_shape + [sds((rows, D), bf16), sds((8, D), f32)],
        scratch_shapes=[pltpu.VMEM((rows, D), f32)],
        name="feed_back_last",
        **common,
    )(*args, *norm)


def turn_kernel(d_ref, w_ref, context_ref, out_ref, delta_ref):
    out = nt(d_ref[...], w_ref[...]).astype(bf16)
    out_ref[...] = out
    select = (
        lax.broadcasted_iota(jnp.int32, (8, 256), 1) // HEAD == lax.broadcasted_iota(jnp.int32, (8, 256), 0)
    ).astype(bf16)
    for g in range(D // 256):
        lanes = slice(g * 256, (g + 1) * 256)
        product = out[:, lanes].astype(f32) * context_ref[:, lanes].astype(f32)
        high = product.astype(bf16)
        low = (product - high.astype(f32)).astype(bf16)
        delta_ref[g] = nt(select, high) + nt(select, low)


def context_back(d, w, context):
    rows = d.shape[0]
    tile = pl.BlockSpec((TILE, D), lambda i: (i, 0))
    return pl.pallas_call(
        turn_kernel,
        grid=(rows // TILE,),
        in_specs=[tile, pl.BlockSpec((D, D), lambda i: (0, 0)), tile],
        out_specs=[tile, pl.BlockSpec((D // 256, 8, TILE), lambda i: (0, 0, i))],
        out_shape=[sds((rows, D), bf16), sds((D // 256, 8, rows), f32)],
        compiler_params=params(),
        cost_estimate=cost(2 * D * D * rows, 8 * 2**20),
        name="context_back",
    )(d, w, context)


def qkv_gradient_kernel(used, order_ref, x_ref, dq_ref, joined_ref, *refs):
    riders, (keep_ref, send_ref, sums_ref, rider) = refs[:-4], refs[-4:]
    rows, wide = dq_ref.shape
    first = order_ref[pl.num_programs(0)] == 0

    @pl.when(pl.program_id(0) == 0)
    def _():
        ones = jnp.ones((8, rows), bf16)
        sums_ref[:, :wide] = nn(ones, dq_ref[...])
        sums_ref[:, wide:] = nn(ones, joined_ref[1])

    x = x_ref[...]
    for i, grad in enumerate((dq_ref[...], joined_ref[0], joined_ref[1])):
        put_halves(keep_ref, send_ref, first, i * wide, tn(x, grad))
    if keep_ref.shape[2] > 3 * wide:
        lanes = rider.shape[1]

        @pl.when(pl.program_id(0) == 0)
        def _():
            rider[...] = jnp.zeros_like(rider)
            at = 0
            for ref, height in zip((*riders, sums_ref), (*used, 1)):
                for i in range(height):
                    for begin in range(0, ref.shape[1], lanes):
                        rider[at : at + 1, :] = ref[i : i + 1, begin : begin + lanes]
                        at += 1

        low = rider[...].astype(bf16)
        keep_ref[0, :, 3 * wide :] = low
        send_ref[0, :, 3 * wide :] = low


def qkv_gradient(order, tokens, dq, joined, shards, riders=()):
    rows, wide = dq.shape
    part = D // shards
    lanes = 16 * D // (part // 2)
    columns = 3 * wide + (lanes if riders else 0)
    sums = [array for array, _ in riders]
    out = pl.BlockSpec((1, part // 2, columns), lambda r, order_ref: (r, 0, 0))
    left = pl.BlockSpec((rows, part), lambda r, order_ref: (0, order_ref[r]))
    whole = pl.BlockSpec((rows, wide), lambda r, order_ref: (0, 0))
    both = pl.BlockSpec((2, rows, wide), lambda r, order_ref: (0, 0, 0))
    return pl.pallas_call(
        functools.partial(qkv_gradient_kernel, [height for _, height in riders]),
        grid_spec=pltpu.PrefetchScalarGridSpec(
            num_scalar_prefetch=1,
            grid=(shards,),
            in_specs=[left, whole, both]
            + [pl.BlockSpec(array.shape, lambda r, order_ref: (0, 0)) for array in sums],
            out_specs=[out, out, pl.BlockSpec((8, 2 * wide), lambda r, order_ref: (0, 0))],
            scratch_shapes=[pltpu.VMEM((part // 2, lanes), f32)],
        ),
        out_shape=[sds((shards, part // 2, columns), bf16)] * 2 + [sds((8, 2 * wide), f32)],
        compiler_params=params(),
        cost_estimate=cost(2 * rows * D * columns, 16 * 2**20),
        name="qkv_gradient",
    )(order, tokens, dq, joined, *sums)


def input_kernel(base_ref, *refs):
    grads, w_ref, out_ref = refs[:-2], refs[-2], refs[-1]
    total = base_ref[...]
    for side in (0, 1):
        dq_ref, joined_ref = grads[2 * side : 2 * side + 2]
        for which, grad in enumerate((dq_ref[...], joined_ref[0], joined_ref[1])):
            total += nt(grad, w_ref[:, qkv_columns(which, side)])
    out_ref[...] = total


def input_back(base, grads, w):
    rows = base.shape[0]
    tile = pl.BlockSpec((TILE, D), lambda i: (i, 0))
    side = [pl.BlockSpec((TILE, D // 2), lambda i: (i, 0)), pl.BlockSpec((2, TILE, D // 2), lambda i: (0, i, 0))]
    return pl.pallas_call(
        input_kernel,
        grid=(rows // TILE,),
        in_specs=[tile, *side, *side, pl.BlockSpec((D, 3 * D), lambda i: (0, 0))],
        out_specs=tile,
        out_shape=sds((rows, D), f32),
        compiler_params=params(),
        cost_estimate=cost(6 * D * D * rows, 20 * 2**20),
        name="input_back",
    )(base, *grads, w)


def swap(value, axis, bit):
    return lax.ppermute(value, axis, [(i, i ^ bit) for i in range(lax.axis_size(axis))])


def after(value, *others):
    return lax.optimization_barrier((value,) + others)[0]


def arrive(gate, value):
    return value if gate[0] is None else after(value, gate[0])


def gathering(gate, shard, own):
    n = lax.axis_size("fsdp")
    quarter = shard.shape[0] // 4
    near = [1 << b for b in range(n.bit_length() - 1)]
    whole = dict(zip(near, (yield [arrive(gate, swap(own, "fsdp", r)) for r in near])))
    held = {(r, s): value[s * quarter : (s + 1) * quarter] for r, value in whole.items() for s in (0, 1)}
    found = []
    for r in range(1, n):
        if r in whole:
            found.append(whole[r])
        else:
            for s, bit in ((0, 1 << (r.bit_length() - 1)), (1, r & -r)):
                held[r, s] = arrive(gate, swap(held[r ^ bit, s], "fsdp", bit))
                found.append(held[r, s])
    found = yield found
    yield [shard, *found, *[arrive(gate, swap(value, "ctx", 1)) for value in found]]


def half_sets(value, bit):
    shape = value.shape
    split = value.reshape((shape[0] // (2 * bit), 2, bit) + shape[1:])
    rest = (shape[0] // 2,) + shape[1:]
    return split[:, 0].reshape(rest), split[:, 1].reshape(rest)


def add_low(a, b):
    return (a.astype(f32) + b.astype(f32)).astype(bf16)


def reduction(gate, keep, send, parity, short=False):
    got = arrive(gate, swap(send, "ctx", 1))
    n = lax.axis_size("fsdp")
    quarter = keep.shape[1] // 2
    bits = [1 << b for b in range(n.bit_length() - 1)]
    streams = [(order, list(range(n))) for order in (bits, bits[::-1])]
    parts = [add_low(keep[:, s * quarter : (s + 1) * quarter], got[:, s * quarter : (s + 1) * quarter]) for s in (0, 1)]
    parts = list((yield parts))
    for k in range(len(bits)):
        for s, (order, ids) in enumerate(streams):
            bit = order[k]
            step = [i for i, r in enumerate(ids) if r & bit][0]
            ids[:] = [r for r in ids if not r & bit]
            mine, theirs = half_sets(parts[s], step)
            parts[s] = add_low(mine, arrive(gate, swap(theirs, "fsdp", bit)))
        if k < len(bits) - 1:
            parts = list((yield parts))
    value = jnp.concatenate([part[0] for part in parts], axis=0)
    (value,) = yield [value]
    if short:
        bit = 2
        while bit < lax.axis_size("ctx"):
            value = add_low(value, arrive(gate, swap(value, "ctx", bit)))
            (value,) = yield [value]
            bit *= 2
        yield from both_halves(gate, value, parity)
    else:
        yield from chain(gate, value, parity)


def chain(gate, value, parity):
    count = lax.axis_size("ctx") // 2
    position = lax.axis_index("ctx") // 2
    half = count // 2

    def move(value, chip_pairs):
        pairs = [(2 * a + c, 2 * b + c) for a, b in chip_pairs for c in (0, 1)]
        return arrive(gate, lax.ppermute(value, "ctx", pairs))

    for s in range(half - 1):
        value = add_low(value, move(value, [(s, s + 1), (count - 1 - s, count - 2 - s)]))
        (value,) = yield [value]
    inner = (position == half - 1) | (position == half)
    across = move(value, [(half - 1, half), (half, half - 1)])
    value = jnp.where(inner, add_low(value, across), value)
    (value,) = yield [value]
    for s in reversed(range(half - 1)):
        back = move(value, [(s + 1, s), (count - 2 - s, count - 1 - s)])
        value = jnp.where((position == s) | (position == count - 1 - s), back, value)
        (value,) = yield [value]
    yield from both_halves(gate, value, parity)


def wide_reduction(gate, keep, send, parity):
    value = add_low(keep, arrive(gate, swap(send, "ctx", 1)))
    (value,) = yield [value]
    (value,) = yield [lax.psum_scatter(value, "fsdp", scatter_dimension=0, tiled=True)[0]]
    yield from chain(gate, value, parity)


def both_halves(gate, value, parity):
    other = arrive(gate, swap(value, "ctx", 1))
    first = parity == 0
    yield [jnp.concatenate([jnp.where(first, value, other), jnp.where(first, other, value)], axis=0).astype(f32)]


def whole_reduction(gate, keep, send, parity):
    value = add_low(keep, arrive(gate, swap(send, "ctx", 1)))
    (value,) = yield [value]
    (value,) = yield [lax.psum_scatter(value, "fsdp", scatter_dimension=0, tiled=True)[0]]
    groups = [list(range(k, lax.axis_size("ctx"), 2)) for k in (0, 1)]
    (value,) = yield [lax.psum(value, "ctx", axis_index_groups=groups)]
    yield from both_halves(gate, value, parity)


class Staged:
    def __init__(self, stages, *args):
        self.gate, self.values, self.done = [None], None, False
        self.stages = stages(self.gate, *args)

    def step(self):
        try:
            self.values = self.stages.send(self.values)
        except StopIteration:
            self.done = True
        return not self.done

    def result(self):
        while self.step():
            pass
        return self.values


def boundary(done, tie, *transfers, hold=()):
    moving = list(hold)
    for transfer in transfers:
        transfer.gate[0] = done
        if transfer.step():
            moving.append(transfer)
    gates = () if done is None else (done,)
    tie, values = lax.optimization_barrier((tie, [transfer.values for transfer in moving], gates))[:2]
    for transfer, value in zip(moving, values):
        transfer.values = value
    return tie


def gathering_rows(gate, row):
    (value,) = yield [row]
    bit = 1
    while bit < lax.axis_size("fsdp"):
        value = jnp.concatenate([value, swap(value, "fsdp", bit)], axis=0)
        bit *= 2
        (value,) = yield [value]


def body(
    layer_input,
    teacher_states,
    out_cotangent,
    doc_start,
    valid_flag,
    query_weight,
    query_bias,
    key_weight,
    value_weight,
    value_bias,
    proj_weight,
    proj_bias,
    attn_gain,
    attn_shift,
    inner_weight,
    inner_bias,
    outer_weight,
    outer_bias,
    final_gain,
    final_shift,
):
    n_ctx, n_fsdp = lax.axis_size("ctx"), lax.axis_size("fsdp")
    c, f = lax.axis_index("ctx"), lax.axis_index("fsdp")
    parity = c % 2
    tokens = layer_input[0]
    rows = tokens.shape[0]
    part = query_weight.shape[0]
    where = jnp.stack([f, parity]).astype(jnp.int32)
    order = jnp.concatenate([f ^ jnp.arange(n_fsdp, dtype=jnp.int32), parity[None].astype(jnp.int32)])

    def own_half(shard):
        half = shard.shape[0] // 2
        return lax.dynamic_slice_in_dim(shard, parity * half, half)

    qkv_shard, own_qkv = pack_shards(where, query_weight, key_weight, value_weight)
    w_qkv = Staged(gathering, qkv_shard, own_qkv)

    up = [(i, i + 1) for i in range(n_ctx - 1)]
    down = [(b, a) for a, b in up]
    before = lax.ppermute(tokens[rows - DOC_MAX :], "ctx", up)
    behind = lax.ppermute(tokens[:DOC_MAX], "ctx", down)
    flags = valid_flag[0]
    valid = jnp.sum(flags)
    valid = jnp.pad(jnp.stack([valid // 64, valid % 64]).astype(bf16), (0, 126))
    flags = flags.astype(f32)[:, None]
    small = jnp.concatenate(
        [query_bias, value_bias, proj_bias, attn_gain, attn_shift, outer_bias, final_gain, final_shift, inner_bias, valid]
    )
    small = Staged(gathering_rows, small.reshape(1, -1))
    small.step()
    small.step()
    position = c * rows
    starts = doc_start[0]
    near_starts = lax.dynamic_slice_in_dim(
        jnp.concatenate(
            [jnp.full((DOC_MAX,), -1, jnp.int32), starts, jnp.full((DOC_MAX,), 2**30, jnp.int32)]
        ),
        position,
        rows + 2 * DOC_MAX,
    )
    tiles = near_starts.shape[0] // TILE
    low_tile = (near_starts[::TILE] - position + DOC_MAX) // TILE
    last = position - DOC_MAX + TILE * (1 + jnp.arange(tiles, dtype=jnp.int32)) - 1
    ends = jnp.sum((near_starts[None, :] <= last[:, None]).astype(jnp.int32), axis=1)
    high_tile = (ends + TILE - 1) // TILE
    inside = (jnp.arange(tiles) >= RIM) & (jnp.arange(tiles) < tiles - RIM)
    low_tile = jnp.where(inside, low_tile, jnp.maximum(low_tile, RIM))
    high_tile = jnp.where(inside, high_tile, jnp.minimum(high_tile, tiles - RIM))
    idq = near_starts.reshape(tiles, 1, TILE)
    idk = near_starts[:, None]

    before, behind, idq, idk, low_tile, high_tile, flags, own_proj, own_inner = boundary(
        None, (before, behind, idq, idk, low_tile, high_tile, flags, own_half(proj_weight), own_half(inner_weight)),
        w_qkv, small,
    )
    w_proj = Staged(gathering, proj_weight, own_proj)
    w_inner = Staged(gathering, inner_weight, own_inner)
    boundary(None, where, w_qkv)
    small = small.result()[0]
    valid = jnp.sum(small[:, -128:].astype(f32), axis=0)
    counted = valid[0] * 64 + valid[1]
    bit = 1
    while bit < n_ctx:
        counted = jnp.full((8, 128), counted, f32) if counted.ndim == 0 else counted
        counted = counted + swap(counted, "ctx", bit)
        bit *= 2
    count = counted[0, 0]
    b_query, b_value, b_proj, g_attn, s_attn, b_outer, g_final, s_final, b_inner = unpack_vectors(where, small)
    w_qkv.values, b_query, b_value, count = lax.optimization_barrier((w_qkv.values, b_query, b_value, count))

    def attend(side, tie, *so_far):
        return attn_fwd(tie, high_tile, query, keys, values_t, idq, idk, side, 2, so_far)

    query, keys, values, keys_t, values_t, w_qkv = project_qkv(where, w_qkv.result(), before, tokens, behind, b_query, b_value)
    tie, own_outer = boundary(query, (low_tile, own_half(outer_weight)), w_proj)
    w_outer = Staged(gathering, outer_weight, own_outer)
    context_a, log_a = attend(0, tie)
    context, log_totals = attend(1, boundary(context_a, low_tile, w_proj, w_inner, w_outer), context_a, log_a)
    normed, normed_low, rate, w_proj = mix_and_norm(
        boundary(context, where, w_proj, w_inner, w_outer), w_proj.values, context, b_proj, tokens, g_attn, s_attn
    )
    tie = boundary(normed, where, w_inner, w_outer)
    act, slope, w_inner = inner_forward(tie, w_inner.values, normed_low, b_inner)
    coef = (n_fsdp * n_ctx * rows / count).reshape(1)
    layer_out, d_sum_two, d_branch, final_sums, w_outer = outer_forward(
        where, w_outer.result(), coef, act, b_outer, normed, g_final, s_final, teacher_states[0], out_cotangent[0], flags
    )

    plain = jnp.concatenate([jnp.arange(n_fsdp, dtype=jnp.int32), order[n_fsdp:]])
    outer = Staged(wide_reduction, *gram(plain, n_fsdp, (act, d_branch)), parity)
    d_pre_a, bias_a, so_far = feed_back(where, 0, d_branch, w_outer, slope, w_inner, d_sum_two)
    d_pre_b, bias_b, d_sum_one, d_attn, attn_sums = feed_back(
        boundary(d_pre_a, where, outer), 1, d_branch, w_outer, slope, w_inner, so_far, (normed, rate, g_attn, s_attn)
    )
    inner_pair = gram(
        after(plain, d_attn), n_fsdp, (normed_low, d_pre_a, d_pre_b), (context, d_attn)
    )
    inner = Staged(whole_reduction, *inner_pair, parity)

    d_context, delta = context_back(after(d_attn, inner_pair[0]), w_proj, context)
    stats = jnp.stack([log_totals, delta])

    def rims(value, axis):
        size = value.shape[axis]
        before = lax.ppermute(lax.slice_in_dim(value, size - DOC_MAX, size, axis=axis), "ctx", up)
        behind = lax.ppermute(lax.slice_in_dim(value, 0, DOC_MAX, axis=axis), "ctx", down)
        return before, behind

    do_before, do_behind = rims(d_context, 0)
    stats_before, stats_behind = rims(stats, 3)
    stats = jnp.concatenate([stats_before, stats, stats_behind], axis=3)
    def attend_back(tie, *part):
        return attn_bwd(
            tie, high_tile, query, do_before, d_context, do_behind, keys, keys_t, values, stats, idq, idk, *part
        )

    parts_a = attend_back(boundary(d_context, low_tile, outer, inner), 0, 0, 1)
    parts_a = attend_back(boundary(parts_a[0], low_tile, outer), 0, 1, 1, parts_a)
    *first_pair, sums_a = qkv_gradient(boundary(parts_a[0], order, outer), tokens, *parts_a, n_fsdp)
    first = Staged(reduction, *first_pair, parity)
    parts_b = attend_back(boundary(first_pair[0], low_tile, inner, hold=[outer]), 1)
    riders = [(final_sums, 4), (attn_sums, 3), (bias_a, 1), (bias_b, 1), (sums_a, 1)]
    *last_pair, sums_b = qkv_gradient(
        boundary(parts_b[0], order, first, outer), tokens, *parts_b, n_fsdp, riders
    )
    last = Staged(reduction, *last_pair, parity, True)
    input_grad = input_back(d_sum_one, (*parts_a, *parts_b), boundary(last_pair[0], w_qkv, first))
    boundary(input_grad, where, last, first, inner)
    boundary(last.values[0], where, last, first)
    boundary(last.values[0], where, last, first)
    outer_grad, inner_grad, first, last = (transfer.result()[0] for transfer in (outer, inner, first, last))
    vectors = last[: part // 2, 3 * D // 2 :].reshape(16, D)
    query_sum, value_sum = vectors[11:13].reshape(2, 2, D // 2).transpose(1, 0, 2).reshape(2, D)
    inner_grad, proj_grad = inner_grad[:, :FF], inner_grad[:, FF:]
    sixth = D // 2
    query_grad, key_grad, value_grad = (
        jnp.concatenate([grad[:, i * sixth : (i + 1) * sixth] for grad in (first, last)], axis=1)
        for i in range(3)
    )
    mse = jnp.sum(vectors[3]) / (count * D)

    def mine(vector):
        length = vector.shape[0] // n_fsdp
        return lax.dynamic_slice_in_dim(vector, f * length, length)

    return (
        layer_out[None],
        input_grad[None],
        mse,
        query_grad,
        mine(query_sum),
        key_grad,
        value_grad,
        mine(value_sum),
        proj_grad,
        mine(vectors[6]),
        mine(vectors[4]),
        mine(vectors[5]),
        inner_grad,
        mine(vectors[7:11].reshape(FF)),
        outer_grad,
        mine(vectors[2]),
        mine(vectors[0]),
        mine(vectors[1]),
    )


def solution(mesh):
    tokens = P("fsdp", "ctx", None)
    matrix, vector = P("fsdp", None), P("fsdp")
    weights = (
        matrix, vector, matrix, matrix, vector, matrix, vector, vector, vector, matrix, vector, matrix, vector, vector, vector,
    )
    return jax.shard_map(
        body,
        mesh=mesh,
        in_specs=(tokens, tokens, tokens, matrix, P("fsdp", "ctx")) + weights,
        out_specs=(tokens, tokens, P()) + weights,
        check_vma=False,
    )
```

```python
import functools

import jax
import jax.numpy as jnp
from jax import lax
from jax.experimental import pallas as pl
from jax.experimental.pallas import tpu as pltpu
from jax.sharding import PartitionSpec as P

D = 1024
FF = 4096
HEAD = 64
DOC_MAX = 512
TILE = 256
RIM = DOC_MAX // TILE
NEG = -1e30
NORM_EPS = 1e-05
VMEM_BYTES = 56 * 2**20
bf16 = jnp.bfloat16
f32 = jnp.float32


def nn(a, b):
    return jnp.dot(a, b, preferred_element_type=f32)


def nt(a, b):
    return lax.dot_general(a, b, (((1,), (1,)), ((), ())), preferred_element_type=f32)


def tn(a, b):
    return lax.dot_general(a, b, (((0,), (0,)), ((), ())), preferred_element_type=f32)


def params():
    return pltpu.CompilerParams(vmem_limit_bytes=VMEM_BYTES)


def cost(flops, bytes_accessed):
    return pl.CostEstimate(flops=int(flops), bytes_accessed=int(bytes_accessed), transcendentals=0)


def sds(shape, dtype):
    return jax.ShapeDtypeStruct(shape, dtype)


def weight_copies(where_ref, pieces, full, out, sem):
    shard, mine, other = pieces[0], pieces[1 : len(pieces) // 2 + 1], pieces[len(pieces) // 2 + 1 :]
    f, parity = where_ref[0], where_ref[1]
    rows = shard.shape[0]
    half, quarter = rows // 2, rows // 4
    copies = []

    def add(source, begin):
        begin = pl.multiple_of(begin, 16)
        copies.append(pltpu.make_async_copy(source, full.at[pl.ds(begin, source.shape[0])], sem.at[len(copies)]))

    add(shard, f * rows)
    at = 0
    for r in range(1, full.shape[0] // rows):
        base = jnp.bitwise_xor(f, r) * rows
        for offset in (0,) if r & (r - 1) == 0 else (0, quarter):
            add(mine[at], base + offset + parity * half)
            add(other[at], base + offset + (1 - parity) * half)
            at += 1
    return copies, pltpu.make_async_copy(full, out, sem.at[len(copies)])


def join_weight(where_ref, pieces, full, out, sem):
    copies, save = weight_copies(where_ref, pieces, full, out, sem)

    @pl.when(pl.program_id(0) == 0)
    def _():
        for copy in copies:
            copy.start()
        for copy in copies:
            copy.wait()
        save.start()

    @pl.when(pl.program_id(0) == pl.num_programs(0) - 1)
    def _():
        save.wait()


def weight_specs(pieces):
    return [pl.BlockSpec(memory_space=pltpu.SMEM)] + [pl.BlockSpec(memory_space=pl.ANY)] * len(pieces)


def weight_scratch(rows, columns):
    return [pltpu.VMEM((rows, columns), bf16), pltpu.SemaphoreType.DMA((64,))]


def pack_kernel(where_ref, q_ref, k_ref, v_ref, shard_ref, own_ref):
    half = own_ref.shape[0]
    first = where_ref[1] == 0
    for side in (0, 1):
        for which, ref in enumerate((q_ref, k_ref, v_ref)):
            columns = qkv_columns(which, side)
            block = ref[:, side * D // 2 : (side + 1) * D // 2]
            shard_ref[:, columns] = block
            own_ref[:, columns] = jnp.where(first, block[:half], block[half:])


def pack_shards(where, q, k, v):
    part = q.shape[0]
    return pl.pallas_call(
        pack_kernel,
        in_specs=[pl.BlockSpec(memory_space=pltpu.SMEM)] + [pl.BlockSpec(memory_space=pltpu.VMEM)] * 3,
        out_specs=[pl.BlockSpec(memory_space=pltpu.VMEM)] * 2,
        out_shape=[sds((part, 3 * D), bf16), sds((part // 2, 3 * D), bf16)],
        compiler_params=params(),
        cost_estimate=cost(0, 4 * 2**20),
        name="pack_shards",
    )(where, q, k, v)


def unpack_kernel(where_ref, packed_ref, *outs):
    packed = packed_ref[...].astype(f32)
    shards = packed.shape[0]
    at = 0
    for out in outs:
        part = out.shape[1] // shards
        for r in range(shards):
            begin = pl.multiple_of(jnp.bitwise_xor(where_ref[0], r) * part, part)
            out[:, pl.ds(begin, part)] = packed[r : r + 1, at : at + part]
        at += part


def unpack_vectors(where, packed):
    return pl.pallas_call(
        unpack_kernel,
        in_specs=[pl.BlockSpec(memory_space=pltpu.SMEM), pl.BlockSpec(memory_space=pltpu.VMEM)],
        out_specs=[pl.BlockSpec(memory_space=pltpu.VMEM)] * 9,
        out_shape=[sds((1, D), f32)] * 8 + [sds((1, FF), f32)],
        compiler_params=params(),
        cost_estimate=cost(0, 2**17),
        name="unpack_vectors",
    )(where, packed)


def qkv_columns(which, side):
    begin = (3 * side + which) * D // 2
    return slice(begin, begin + D // 2)


def qkv_kernel(count, where_ref, *refs):
    pieces, refs = refs[:count], refs[count:]
    before_ref, x_ref, behind_ref, bq_ref, bv_ref, q_ref, k_ref, v_ref, kt_ref, vt_ref, full_ref, w_ref, sem = refs
    join_weight(where_ref, pieces, w_ref, full_ref, sem)
    i = pl.program_id(0)
    x = jnp.where(i == 0, before_ref[...], jnp.where(i == pl.num_programs(0) - 1, behind_ref[...], x_ref[...]))

    for s in (0, 1):
        half = slice(s * D // 2, (s + 1) * D // 2)
        query = (nn(x, w_ref[:, qkv_columns(0, s)]) + bq_ref[:, half]).astype(bf16)
        q_ref[:, half] = query * jnp.asarray(HEAD**-0.5, bf16)
        keys = nn(x, w_ref[:, qkv_columns(1, s)]).astype(bf16)
        k_ref[:, half] = keys
        kt_ref[half, :] = jnp.transpose(keys)
        values = (nn(x, w_ref[:, qkv_columns(2, s)]) + bv_ref[:, half]).astype(bf16)
        v_ref[:, half] = values
        vt_ref[half, :] = jnp.transpose(values)


def project_qkv(where, pieces, before, tokens, behind, bq, bv):
    rows = tokens.shape[0]
    span = rows + 2 * DOC_MAX
    rim = pl.BlockSpec((512, D), lambda i: (0, 0))
    inside = pl.BlockSpec((512, D), lambda i: (jnp.clip(i - 1, 0, rows // 512 - 1), 0))
    row = pl.BlockSpec((1, D), lambda i: (0, 0))
    tall = pl.BlockSpec((512, D), lambda i: (i, 0))
    wide = pl.BlockSpec((D, 512), lambda i: (0, i))
    return pl.pallas_call(
        functools.partial(qkv_kernel, len(pieces)),
        grid=(span // 512,),
        in_specs=weight_specs(pieces) + [rim, inside, rim, row, row],
        out_specs=[
            tall,
            tall,
            tall,
            wide,
            wide,
            pl.BlockSpec(memory_space=pl.ANY),
        ],
        scratch_shapes=weight_scratch(D, 3 * D),
        out_shape=[
            sds((span, D), bf16),
            sds((span, D), bf16),
            sds((span, D), bf16),
            sds((D, span), bf16),
            sds((D, span), bf16),
            sds((D, 3 * D), bf16),
        ],
        compiler_params=params(),
        cost_estimate=cost(2 * D * D * (rows + 2 * span), 30 * 2**20),
        name="project_qkv",
    )(where, *pieces, before, tokens, behind, bq, bv)


def stack_rows(block, stack):
    lanes = lax.broadcasted_iota(jnp.int32, block.shape, 1)
    for h in range(4):
        stack[h * TILE : (h + 1) * TILE, :] = jnp.where(lanes // HEAD == h, block, jnp.zeros_like(block))


def stack_columns(turned, stack):
    for h in range(4):
        heads = slice(h * HEAD, (h + 1) * HEAD)
        stack[heads, h * TILE : (h + 1) * TILE] = turned[heads, :]


def attn_fwd_kernel(lo_ref, hi_ref, q_ref, k_ref, vt_ref, idq_ref, idk_ref, *refs):
    out_ref, lse_ref, qs, acc, top, tot = refs[-6:]
    quads = qs.shape[0]
    t = pl.program_id(0)

    @pl.when(t == 0)
    def _():
        qs[...] = jnp.zeros_like(qs)

    turned = jnp.transpose(q_ref[...])
    for g in range(quads):
        stack_columns(turned[g * 256 : (g + 1) * 256], qs.at[g])
    acc[...] = jnp.zeros_like(acc)
    top[...] = jnp.full_like(top, NEG)
    tot[...] = jnp.zeros_like(tot)

    def step(kt, carry):
        rows = pl.ds(pl.multiple_of(kt * TILE, TILE), TILE)
        bias = jnp.where(idk_ref[rows, :] == idq_ref[0], 0.0, NEG)
        scores = [nn(k_ref[rows, g * 256 : (g + 1) * 256], qs[g]) for g in range(quads)]
        for g in range(quads):
            vt_tile = vt_ref[g * 256 : (g + 1) * 256, rows]
            for h in range(4):
                heads = slice(h * HEAD, (h + 1) * HEAD)
                own = scores[g][:, h * TILE : (h + 1) * TILE] + bias
                old = top[g, h : h + 1, :]
                new = jnp.maximum(old, jnp.max(own, axis=0, keepdims=True))
                top[g, h : h + 1, :] = new
                p = jnp.exp(own - new)
                fade = jnp.exp(old - new)
                tot[g, h : h + 1, :] = tot[g, h : h + 1, :] * fade + jnp.sum(p, axis=0, keepdims=True)
                acc[g, heads, :] = acc[g, heads, :] * fade + nn(vt_tile[heads, :], p.astype(bf16))
        return carry

    lax.fori_loop(lo_ref[t + RIM], hi_ref[t + RIM], step, 0)
    for g in range(quads):
        total = tot[g]
        inverse = 1.0 / total
        for h in range(4):
            heads = slice(h * HEAD, (h + 1) * HEAD)
            acc[g, heads, :] = acc[g, heads, :] * inverse[h : h + 1, :]
        out_ref[:, g * 256 : (g + 1) * 256] = jnp.transpose(acc[g]).astype(bf16)
        lse_ref[g] = top[g] + jnp.log(total)


def attn_fwd(lo, hi, q, k_near, vt_near, idq_rows, idk_col, side, quads, so_far=()):
    span, wide = k_near.shape[0], quads * 256
    rows = span - 2 * DOC_MAX
    return pl.pallas_call(
        attn_fwd_kernel,
        grid_spec=pltpu.PrefetchScalarGridSpec(
            num_scalar_prefetch=2,
            grid=(rows // TILE,),
            in_specs=[
                pl.BlockSpec((TILE, wide), lambda t, *_: (t + RIM, side)),
                pl.BlockSpec((span, wide), lambda t, *_: (0, side)),
                pl.BlockSpec((wide, span), lambda t, *_: (side, 0)),
                pl.BlockSpec((1, 1, TILE), lambda t, *_: (t + RIM, 0, 0)),
                pl.BlockSpec((span, 1), lambda t, *_: (0, 0)),
            ]
            + [pl.BlockSpec(memory_space=pl.ANY)] * len(so_far),
            out_specs=[
                pl.BlockSpec((TILE, wide), lambda t, *_: (t, side)),
                pl.BlockSpec((quads, 8, TILE), lambda t, *_: (side, 0, t)),
            ],
            scratch_shapes=[
                pltpu.VMEM((quads, 256, 4 * TILE), bf16),
                pltpu.VMEM((quads, 256, TILE), f32),
                pltpu.VMEM((quads, 8, TILE), f32),
                pltpu.VMEM((quads, 8, TILE), f32),
            ],
        ),
        out_shape=[sds((rows, D), bf16), sds((D // 256, 8, rows), f32)],
        input_output_aliases={7 + i: i for i in range(len(so_far))},
        compiler_params=params(),
        cost_estimate=cost(quads * 10**10, 2**21),
        name="attn_forward",
    )(lo, hi, q, k_near, vt_near, idq_rows, idk_col, *so_far)


def attn_bwd_kernel(
    lo_ref, hi_ref, q_ref, before_ref, do_ref, behind_ref, k_ref, kt_ref, v_ref, stats_ref, idq_ref, idk_ref, *refs
):
    dq_ref, joined_ref, qs, dos, qst, dost, dk_acc, dv_acc, dq_acc = refs[-9:]
    t = pl.program_id(1)
    low, high = lo_ref[t], hi_ref[t]
    end = pl.num_programs(1) - RIM
    own_low, own_high = jnp.maximum(low, RIM), jnp.minimum(high, end)

    @pl.when((t == 0) & (pl.program_id(0) == 0))
    def _():
        qst[...] = jnp.zeros_like(qst)
        dost[...] = jnp.zeros_like(dost)

    @pl.when(t == 0)
    def _():
        dk_acc[...] = jnp.zeros_like(dk_acc)
        dv_acc[...] = jnp.zeros_like(dv_acc)

    @pl.when(low < high)
    def _():
        q = q_ref[...]
        do = jnp.where(t < RIM, before_ref[...], jnp.where(t >= end, behind_ref[...], do_ref[...]))
        stack_rows(q, qs)
        stack_rows(do, dos)
        stack_columns(jnp.transpose(q), qst)
        stack_columns(jnp.transpose(do), dost)
        lse_row, delta_row = (
            jnp.concatenate([stats_ref[s, 0, h : h + 1] for h in range(4)], axis=1) for s in (0, 1)
        )
        dq_acc[...] = jnp.zeros_like(dq_acc)

        def step(own, kt, carry):
            rows = pl.ds(pl.multiple_of(kt * TILE, TILE), TILE)
            bias = jnp.where(idk_ref[rows, :] == idq_ref[0], 0.0, NEG)
            s = nn(k_ref[rows, :], qst[...])
            dp = nn(v_ref[rows, :], dost[...])
            p = jnp.exp(s + jnp.concatenate([bias] * 4, axis=1) - lse_row)
            ds = (p * (dp - delta_row)).astype(bf16)
            if own:
                inside = pl.ds(pl.multiple_of((kt - RIM) * TILE, TILE), TILE)
                dv_acc[inside, :] += nn(p.astype(bf16), dos[...])
                dk_acc[inside, :] += nn(ds, qs[...])
            kt_tile = kt_ref[:, rows]
            for h in range(4):
                heads = slice(h * HEAD, (h + 1) * HEAD)
                dq_acc[heads, :] += nn(kt_tile[heads, :], ds[:, h * TILE : (h + 1) * TILE])
            return carry

        lax.fori_loop(low, jnp.minimum(high, RIM), functools.partial(step, False), 0)
        lax.fori_loop(own_low, own_high, functools.partial(step, True), 0)
        lax.fori_loop(jnp.maximum(low, end), high, functools.partial(step, False), 0)

        @pl.when((t >= RIM) & (t < end))
        def _():
            dq_ref[...] = (jnp.transpose(dq_acc[...]) * (HEAD**-0.5)).astype(bf16)

    @pl.when(t == pl.num_programs(1) - 1)
    def _():
        joined_ref[0] = dk_acc[...].astype(bf16)
        joined_ref[1] = dv_acc[...].astype(bf16)


def attn_bwd(lo, hi, q_near, before, do, behind, k_near, kt_near, v_near, stats, idq_rows, idk_col, side, begin=0, quads=2, so_far=()):
    rows, span = do.shape[0], k_near.shape[0]
    tiles, first = rows // TILE, 2 * side + begin
    near = pl.BlockSpec((span, 256), lambda g, t, *_: (0, g + first))
    return pl.pallas_call(
        attn_bwd_kernel,
        grid_spec=pltpu.PrefetchScalarGridSpec(
            num_scalar_prefetch=2,
            grid=(quads, span // TILE),
            in_specs=[
                pl.BlockSpec((TILE, 256), lambda g, t, *_: (t, g + first)),
                pl.BlockSpec((TILE, 256), lambda g, t, *_: (jnp.clip(t, 0, RIM - 1), g + first)),
                pl.BlockSpec((TILE, 256), lambda g, t, *_: (jnp.clip(t - RIM, 0, tiles - 1), g + first)),
                pl.BlockSpec((TILE, 256), lambda g, t, *_: (jnp.clip(t - RIM - tiles, 0, RIM - 1), g + first)),
                near,
                pl.BlockSpec((256, span), lambda g, t, *_: (g + first, 0)),
                near,
                pl.BlockSpec((2, 1, 8, TILE), lambda g, t, *_: (0, g + first, 0, t)),
                pl.BlockSpec((1, 1, TILE), lambda g, t, *_: (t, 0, 0)),
                pl.BlockSpec((span, 1), lambda g, t, *_: (0, 0)),
            ]
            + [pl.BlockSpec(memory_space=pl.ANY)] * len(so_far),
            out_specs=[
                pl.BlockSpec((TILE, 256), lambda g, t, *_: (jnp.clip(t - RIM, 0, tiles - 1), g + begin)),
                pl.BlockSpec((2, rows, 256), lambda g, t, *_: (0, 0, g + begin)),
            ],
            scratch_shapes=[
                pltpu.VMEM((4 * TILE, 256), bf16),
                pltpu.VMEM((4 * TILE, 256), bf16),
                pltpu.VMEM((256, 4 * TILE), bf16),
                pltpu.VMEM((256, 4 * TILE), bf16),
                pltpu.VMEM((rows, 256), f32),
                pltpu.VMEM((rows, 256), f32),
                pltpu.VMEM((256, TILE), f32),
            ],
        ),
        out_shape=[sds((rows, 512), bf16), sds((2, rows, 512), bf16)],
        input_output_aliases={12 + i: i for i in range(len(so_far))},
        compiler_params=params(),
        cost_estimate=cost(quads * 15 * 10**9, 2**22),
        name="attn_backward",
    )(lo, hi, q_near, before, do, behind, k_near, kt_near, v_near, stats, idq_rows, idk_col, *so_far)


def norm_stats(hidden):
    center = hidden - jnp.mean(hidden, axis=1, keepdims=True)
    rate = lax.rsqrt(jnp.mean(center * center, axis=1, keepdims=True) + NORM_EPS)
    return center * rate, rate


def norm_back(grad, unit, rate):
    return rate * (
        grad - jnp.mean(grad, axis=1, keepdims=True) - unit * jnp.mean(grad * unit, axis=1, keepdims=True)
    )


def mix_kernel(count, where_ref, *refs):
    pieces, refs = refs[:count], refs[count:]
    c_ref, b_ref, x_ref, g_ref, s_ref, normed_ref, low_ref, rate_ref, full_ref, w_ref, sem = refs
    join_weight(where_ref, pieces, w_ref, full_ref, sem)
    hidden = x_ref[...].astype(f32) + (nn(c_ref[...], w_ref[...]) + b_ref[...])
    unit, rate = norm_stats(hidden)
    normed = unit * g_ref[...] + s_ref[...]
    normed_ref[...] = normed
    low_ref[...] = normed.astype(bf16)
    rate_ref[...] = rate


def mix_and_norm(where, pieces, context, b, tokens, gain, shift):
    rows = tokens.shape[0]
    tile = pl.BlockSpec((TILE, D), lambda i: (i, 0))
    row = pl.BlockSpec((1, D), lambda i: (0, 0))
    return pl.pallas_call(
        functools.partial(mix_kernel, len(pieces)),
        grid=(rows // TILE,),
        in_specs=weight_specs(pieces) + [tile, row, tile, row, row],
        out_specs=[tile, tile, pl.BlockSpec((TILE, 1), lambda i: (i, 0)), pl.BlockSpec(memory_space=pl.ANY)],
        out_shape=[sds((rows, D), f32), sds((rows, D), bf16), sds((rows, 1), f32), sds((D, D), bf16)],
        scratch_shapes=weight_scratch(D, D),
        compiler_params=params(),
        cost_estimate=cost(2 * D * D * rows, 14 * 2**20),
        name="mix_and_norm",
    )(where, *pieces, context, b, tokens, gain, shift)


def gelu_parts(u):
    t = 1.0 / (1.0 + (0.3275911 * 0.7071067811865476) * jnp.abs(u))
    poly = t * (0.254829592 + t * (-0.284496736 + t * (1.421413741 + t * (-1.453152027 + t * 1.061405429))))
    bell = jnp.exp(-0.5 * u * u)
    tail = 0.5 * poly * bell
    share = jnp.where(u >= 0, 1.0 - tail, tail)
    return u * share, share + u * bell * 0.3989422804014327


def inner_kernel(count, where_ref, *refs):
    pieces, (x_ref, b_ref, act_ref, slope_ref, full_ref, w_ref, sem) = refs[:count], refs[count:]
    join_weight(where_ref, pieces, w_ref, full_ref, sem)
    wide = act_ref.shape[1]
    columns = pl.ds(pl.multiple_of(pl.program_id(0) * wide, wide), wide)
    weight = w_ref[:, columns]
    parts = [slice(i, i + 128) for i in range(0, x_ref.shape[0], 128)]
    ahead = nn(x_ref[parts[0], :], weight)
    for i, rows in enumerate(parts):
        pre = ahead
        if i + 1 < len(parts):
            ahead = nn(x_ref[parts[i + 1], :], weight)
        act, slope = gelu_parts(pre + b_ref[...])
        act_ref[rows, :] = act.astype(bf16)
        slope_ref[rows, :] = slope.astype(bf16)


def inner_forward(where, pieces, x, b):
    rows, wide = x.shape[0], 512
    block = pl.BlockSpec((rows, wide), lambda j: (0, j))
    return pl.pallas_call(
        functools.partial(inner_kernel, len(pieces)),
        grid=(FF // wide,),
        in_specs=weight_specs(pieces)
        + [pl.BlockSpec((rows, D), lambda j: (0, 0)), pl.BlockSpec((1, wide), lambda j: (0, j))],
        out_specs=[block, block, pl.BlockSpec(memory_space=pl.ANY)],
        out_shape=[sds((rows, FF), bf16), sds((rows, FF), bf16), sds((D, FF), bf16)],
        scratch_shapes=weight_scratch(D, FF),
        compiler_params=params(),
        cost_estimate=cost(2 * D * FF * rows, 26 * 2**20),
        name="inner_forward",
    )(where, *pieces, x, b)


def outer_kernel(count, where_ref, *refs):
    pieces, refs = refs[:count], refs[count:]
    coef_ref, act_ref, b_ref, normed_ref, g_ref, s_ref, teach_ref, cot_ref, flag_ref = refs[:9]
    out_ref, dsum_ref, dlow_ref, sums_ref, full_ref, w_ref, sem = refs[9:]
    join_weight(where_ref, pieces, w_ref, full_ref, sem)
    hidden = normed_ref[...] + (nn(act_ref[...], w_ref[...]) + b_ref[...])
    unit, rate = norm_stats(hidden)
    gain = g_ref[...]
    final = unit * gain + s_ref[...]
    out_ref[...] = final.astype(bf16)
    error = final - teach_ref[...].astype(f32)
    marked = flag_ref[...] * error
    grad = cot_ref[...].astype(f32) + coef_ref[0] * marked
    dsum = norm_back(grad * gain, unit, rate)
    dsum_ref[...] = dsum
    low = dsum.astype(bf16)
    dlow_ref[...] = low

    @pl.when(pl.program_id(0) == 0)
    def _():
        sums_ref[...] = jnp.zeros_like(sums_ref)

    sums_ref[0:1, :] += jnp.sum(grad * unit, axis=0, keepdims=True)
    sums_ref[1:2, :] += jnp.sum(grad, axis=0, keepdims=True)
    sums_ref[2:3, :] += jnp.sum(low.astype(f32), axis=0, keepdims=True)
    sums_ref[3:4, :] += jnp.sum(marked * error, axis=0, keepdims=True)


def outer_forward(where, pieces, coef, act, b, normed, gain, shift, teacher, cotangent, flags):
    rows = act.shape[0]
    tile = pl.BlockSpec((TILE, D), lambda i: (i, 0))
    row = pl.BlockSpec((1, D), lambda i: (0, 0))
    return pl.pallas_call(
        functools.partial(outer_kernel, len(pieces)),
        grid=(rows // TILE,),
        in_specs=weight_specs(pieces)
        + [
            pl.BlockSpec(memory_space=pltpu.SMEM),
            pl.BlockSpec((TILE, FF), lambda i: (i, 0)),
            row, tile, row, row, tile, tile,
            pl.BlockSpec((TILE, 1), lambda i: (i, 0)),
        ],
        out_specs=[
            tile, tile, tile, pl.BlockSpec((8, D), lambda i: (0, 0)), pl.BlockSpec(memory_space=pl.ANY),
        ],
        out_shape=[
            sds((rows, D), bf16), sds((rows, D), f32), sds((rows, D), bf16), sds((8, D), f32), sds((FF, D), bf16),
        ],
        scratch_shapes=weight_scratch(FF, D),
        compiler_params=params(),
        cost_estimate=cost(2 * D * FF * rows, 32 * 2**20),
        name="outer_forward",
    )(where, *pieces, coef, act, b, normed, gain, shift, teacher, cotangent, flags)


def put_halves(keep_ref, send_ref, first, begin, grad):
    half = keep_ref.shape[1]
    columns = slice(begin, begin + grad.shape[1])
    low, high = grad[:half], grad[half:]
    keep_ref[0, :, columns] = jnp.where(first, low, high).astype(bf16)
    send_ref[0, :, columns] = jnp.where(first, high, low).astype(bf16)


def gram_kernel(counts, order_ref, *refs):
    operands, keep_ref, send_ref = list(refs[:-2]), refs[-2], refs[-1]
    first = order_ref[pl.num_programs(0)] == 0
    at = 0
    for count in counts:
        left = operands.pop(0)[...]
        for _ in range(count):
            right_ref = operands.pop(0)
            put_halves(keep_ref, send_ref, first, at, tn(left, right_ref[...]))
            at += right_ref.shape[1]


def gram(order, shards, *groups):
    tokens, height = groups[0][0].shape
    part = height // shards
    columns = sum(right.shape[1] for group in groups for right in group[1:])
    out = pl.BlockSpec((1, part // 2, columns), lambda r, order_ref: (r, 0, 0))
    in_specs = []
    for group in groups:
        in_specs.append(pl.BlockSpec((tokens, part), lambda r, order_ref: (0, order_ref[r])))
        in_specs += [pl.BlockSpec((tokens, right.shape[1]), lambda r, order_ref: (0, 0)) for right in group[1:]]
    return pl.pallas_call(
        functools.partial(gram_kernel, [len(group) - 1 for group in groups]),
        grid_spec=pltpu.PrefetchScalarGridSpec(
            num_scalar_prefetch=1, grid=(shards,), in_specs=in_specs, out_specs=[out, out]
        ),
        out_shape=[sds((shards, part // 2, columns), bf16)] * 2,
        compiler_params=params(),
        cost_estimate=cost(2 * tokens * height * columns, 2 * (tokens * (height + columns) + height * columns)),
        name="gram",
    )(order, *[operand for group in groups for operand in group])


def feed_back_columns(db_ref, wo_ref, slope_ref, wi_ref, dpre_ref, bias_ref, total):
    ones = jnp.ones((8, TILE), bf16)
    bias = jnp.zeros(bias_ref.shape, f32)
    for i in range(db_ref.shape[0] // TILE):
        rows = slice(i * TILE, (i + 1) * TILE)
        pre = (nt(db_ref[rows, :], wo_ref[...]) * slope_ref[rows, :].astype(f32)).astype(bf16)
        dpre_ref[rows, :] = pre
        bias += nn(ones, pre)
        total[rows, :] += nt(pre, wi_ref[...])
    bias_ref[...] = bias


def feed_back_first_kernel(tie_ref, db_ref, wo_ref, slope_ref, wi_ref, dsum_ref, dpre_ref, bias_ref, total):
    @pl.when(pl.program_id(0) == 0)
    def _():
        total[...] = dsum_ref[...]

    feed_back_columns(db_ref, wo_ref, slope_ref, wi_ref, dpre_ref, bias_ref, total)


def feed_back_last_kernel(
    tie_ref, db_ref, wo_ref, slope_ref, wi_ref, dsum_ref, normed_ref, rate_ref, g_ref, s_ref,
    dpre_ref, bias_ref, done_ref, dattn_ref, sums_ref, total,
):
    @pl.when(pl.program_id(0) == 0)
    def _():
        total[...] = dsum_ref[...]

    feed_back_columns(db_ref, wo_ref, slope_ref, wi_ref, dpre_ref, bias_ref, total)

    @pl.when(pl.program_id(0) == pl.num_programs(0) - 1)
    def _():
        gain = g_ref[...]
        sums_ref[...] = jnp.zeros_like(sums_ref)
        for i in range(db_ref.shape[0] // TILE):
            rows = slice(i * TILE, (i + 1) * TILE)
            grad = total[rows, :]
            unit = (normed_ref[rows, :] - s_ref[...]) / gain
            done = norm_back(grad * gain, unit, rate_ref[rows, :])
            done_ref[rows, :] = done
            low = done.astype(bf16)
            dattn_ref[rows, :] = low
            sums_ref[0:1, :] += jnp.sum(grad * unit, axis=0, keepdims=True)
            sums_ref[1:2, :] += jnp.sum(grad, axis=0, keepdims=True)
            sums_ref[2:3, :] += jnp.sum(low.astype(f32), axis=0, keepdims=True)


def feed_back(tie, side, d_branch, w_outer, slope, w_inner, so_far, norm=None):
    rows, wide = d_branch.shape[0], 512
    steps = FF // wide // 2
    begin = side * steps
    whole = pl.BlockSpec((rows, D), lambda j: (0, 0))
    row = pl.BlockSpec((1, D), lambda j: (0, 0))
    in_specs = [
        pl.BlockSpec(memory_space=pltpu.SMEM),
        whole,
        pl.BlockSpec((wide, D), lambda j: (j + begin, 0)),
        pl.BlockSpec((rows, wide), lambda j: (0, j + begin)),
        pl.BlockSpec((D, wide), lambda j: (0, j + begin)),
        whole,
    ]
    out_specs = [pl.BlockSpec((rows, wide), lambda j: (0, j)), pl.BlockSpec((8, wide), lambda j: (0, j)), whole]
    out_shape = [sds((rows, FF // 2), bf16), sds((8, FF // 2), f32), sds((rows, D), f32)]
    args = (tie, d_branch, w_outer, slope, w_inner, so_far)
    common = dict(grid=(steps,), compiler_params=params(), cost_estimate=cost(2 * D * FF * rows, 30 * 2**20))
    if norm is None:
        return pl.pallas_call(
            feed_back_first_kernel,
            in_specs=in_specs,
            out_specs=out_specs,
            out_shape=out_shape,
            name="feed_back_first",
            **common,
        )(*args)
    return pl.pallas_call(
        feed_back_last_kernel,
        in_specs=in_specs + [whole, pl.BlockSpec((rows, 1), lambda j: (0, 0)), row, row],
        out_specs=out_specs + [whole, pl.BlockSpec((8, D), lambda j: (0, 0))],
        out_shape=out_shape + [sds((rows, D), bf16), sds((8, D), f32)],
        scratch_shapes=[pltpu.VMEM((rows, D), f32)],
        name="feed_back_last",
        **common,
    )(*args, *norm)


def turn_kernel(d_ref, w_ref, context_ref, out_ref, delta_ref):
    out = nt(d_ref[...], w_ref[...]).astype(bf16)
    out_ref[...] = out
    select = (
        lax.broadcasted_iota(jnp.int32, (8, 256), 1) // HEAD == lax.broadcasted_iota(jnp.int32, (8, 256), 0)
    ).astype(bf16)
    for g in range(D // 256):
        lanes = slice(g * 256, (g + 1) * 256)
        product = out[:, lanes].astype(f32) * context_ref[:, lanes].astype(f32)
        high = product.astype(bf16)
        low = (product - high.astype(f32)).astype(bf16)
        delta_ref[g] = nt(select, high) + nt(select, low)


def context_back(d, w, context):
    rows = d.shape[0]
    tile = pl.BlockSpec((TILE, D), lambda i: (i, 0))
    return pl.pallas_call(
        turn_kernel,
        grid=(rows // TILE,),
        in_specs=[tile, pl.BlockSpec((D, D), lambda i: (0, 0)), tile],
        out_specs=[tile, pl.BlockSpec((D // 256, 8, TILE), lambda i: (0, 0, i))],
        out_shape=[sds((rows, D), bf16), sds((D // 256, 8, rows), f32)],
        compiler_params=params(),
        cost_estimate=cost(2 * D * D * rows, 8 * 2**20),
        name="context_back",
    )(d, w, context)


def qkv_gradient_kernel(used, order_ref, x_ref, dq_ref, joined_ref, *refs):
    riders, (keep_ref, send_ref, sums_ref, rider) = refs[:-4], refs[-4:]
    rows, wide = dq_ref.shape
    first = order_ref[pl.num_programs(0)] == 0

    @pl.when(pl.program_id(0) == 0)
    def _():
        ones = jnp.ones((8, rows), bf16)
        sums_ref[:, :wide] = nn(ones, dq_ref[...])
        sums_ref[:, wide:] = nn(ones, joined_ref[1])

    x = x_ref[...]
    for i, grad in enumerate((dq_ref[...], joined_ref[0], joined_ref[1])):
        put_halves(keep_ref, send_ref, first, i * wide, tn(x, grad))
    if keep_ref.shape[2] > 3 * wide:
        lanes = rider.shape[1]

        @pl.when(pl.program_id(0) == 0)
        def _():
            rider[...] = jnp.zeros_like(rider)
            at = 0
            for ref, height in zip((*riders, sums_ref), (*used, 1)):
                for i in range(height):
                    for begin in range(0, ref.shape[1], lanes):
                        rider[at : at + 1, :] = ref[i : i + 1, begin : begin + lanes]
                        at += 1

        low = rider[...].astype(bf16)
        keep_ref[0, :, 3 * wide :] = low
        send_ref[0, :, 3 * wide :] = low


def qkv_gradient(order, tokens, dq, joined, shards, riders=()):
    rows, wide = dq.shape
    part = D // shards
    lanes = 16 * D // (part // 2)
    columns = 3 * wide + (lanes if riders else 0)
    sums = [array for array, _ in riders]
    out = pl.BlockSpec((1, part // 2, columns), lambda r, order_ref: (r, 0, 0))
    left = pl.BlockSpec((rows, part), lambda r, order_ref: (0, order_ref[r]))
    whole = pl.BlockSpec((rows, wide), lambda r, order_ref: (0, 0))
    both = pl.BlockSpec((2, rows, wide), lambda r, order_ref: (0, 0, 0))
    return pl.pallas_call(
        functools.partial(qkv_gradient_kernel, [height for _, height in riders]),
        grid_spec=pltpu.PrefetchScalarGridSpec(
            num_scalar_prefetch=1,
            grid=(shards,),
            in_specs=[left, whole, both]
            + [pl.BlockSpec(array.shape, lambda r, order_ref: (0, 0)) for array in sums],
            out_specs=[out, out, pl.BlockSpec((8, 2 * wide), lambda r, order_ref: (0, 0))],
            scratch_shapes=[pltpu.VMEM((part // 2, lanes), f32)],
        ),
        out_shape=[sds((shards, part // 2, columns), bf16)] * 2 + [sds((8, 2 * wide), f32)],
        compiler_params=params(),
        cost_estimate=cost(2 * rows * D * columns, 16 * 2**20),
        name="qkv_gradient",
    )(order, tokens, dq, joined, *sums)


def input_kernel(base_ref, *refs):
    grads, w_ref, out_ref = refs[:-2], refs[-2], refs[-1]
    total = base_ref[...]
    for side in (0, 1):
        dq_ref, joined_ref = grads[2 * side : 2 * side + 2]
        for which, grad in enumerate((dq_ref[...], joined_ref[0], joined_ref[1])):
            total += nt(grad, w_ref[:, qkv_columns(which, side)])
    out_ref[...] = total


def input_back(base, grads, w):
    rows = base.shape[0]
    tile = pl.BlockSpec((TILE, D), lambda i: (i, 0))
    side = [pl.BlockSpec((TILE, D // 2), lambda i: (i, 0)), pl.BlockSpec((2, TILE, D // 2), lambda i: (0, i, 0))]
    return pl.pallas_call(
        input_kernel,
        grid=(rows // TILE,),
        in_specs=[tile, *side, *side, pl.BlockSpec((D, 3 * D), lambda i: (0, 0))],
        out_specs=tile,
        out_shape=sds((rows, D), f32),
        compiler_params=params(),
        cost_estimate=cost(6 * D * D * rows, 20 * 2**20),
        name="input_back",
    )(base, *grads, w)


def swap(value, axis, bit):
    return lax.ppermute(value, axis, [(i, i ^ bit) for i in range(lax.axis_size(axis))])


def after(value, *others):
    return lax.optimization_barrier((value,) + others)[0]


def arrive(gate, value):
    return value if gate[0] is None else after(value, gate[0])


def gathering(gate, shard, own):
    n = lax.axis_size("fsdp")
    quarter = shard.shape[0] // 4
    near = [1 << b for b in range(n.bit_length() - 1)]
    whole = dict(zip(near, (yield [arrive(gate, swap(own, "fsdp", r)) for r in near])))
    held = {(r, s): value[s * quarter : (s + 1) * quarter] for r, value in whole.items() for s in (0, 1)}
    found = []
    for r in range(1, n):
        if r in whole:
            found.append(whole[r])
        else:
            for s, bit in ((0, 1 << (r.bit_length() - 1)), (1, r & -r)):
                held[r, s] = arrive(gate, swap(held[r ^ bit, s], "fsdp", bit))
                found.append(held[r, s])
    found = yield found
    yield [shard, *found, *[arrive(gate, swap(value, "ctx", 1)) for value in found]]


def half_sets(value, bit):
    shape = value.shape
    split = value.reshape((shape[0] // (2 * bit), 2, bit) + shape[1:])
    rest = (shape[0] // 2,) + shape[1:]
    return split[:, 0].reshape(rest), split[:, 1].reshape(rest)


def add_low(a, b):
    return (a.astype(f32) + b.astype(f32)).astype(bf16)


def reduction(gate, keep, send, parity, short=False):
    got = arrive(gate, swap(send, "ctx", 1))
    n = lax.axis_size("fsdp")
    quarter = keep.shape[1] // 2
    bits = [1 << b for b in range(n.bit_length() - 1)]
    streams = [(order, list(range(n))) for order in (bits, bits[::-1])]
    parts = [add_low(keep[:, s * quarter : (s + 1) * quarter], got[:, s * quarter : (s + 1) * quarter]) for s in (0, 1)]
    parts = list((yield parts))
    for k in range(len(bits)):
        for s, (order, ids) in enumerate(streams):
            bit = order[k]
            step = [i for i, r in enumerate(ids) if r & bit][0]
            ids[:] = [r for r in ids if not r & bit]
            mine, theirs = half_sets(parts[s], step)
            parts[s] = add_low(mine, arrive(gate, swap(theirs, "fsdp", bit)))
        if k < len(bits) - 1:
            parts = list((yield parts))
    value = jnp.concatenate([part[0] for part in parts], axis=0)
    (value,) = yield [value]
    if short:
        bit = 2
        while bit < lax.axis_size("ctx"):
            value = add_low(value, arrive(gate, swap(value, "ctx", bit)))
            (value,) = yield [value]
            bit *= 2
        yield from both_halves(gate, value, parity)
    else:
        yield from chain(gate, value, parity)


def chain(gate, value, parity):
    count = lax.axis_size("ctx") // 2
    position = lax.axis_index("ctx") // 2
    half = count // 2

    def move(value, chip_pairs):
        pairs = [(2 * a + c, 2 * b + c) for a, b in chip_pairs for c in (0, 1)]
        return arrive(gate, lax.ppermute(value, "ctx", pairs))

    for s in range(half - 1):
        value = add_low(value, move(value, [(s, s + 1), (count - 1 - s, count - 2 - s)]))
        (value,) = yield [value]
    inner = (position == half - 1) | (position == half)
    across = move(value, [(half - 1, half), (half, half - 1)])
    value = jnp.where(inner, add_low(value, across), value)
    (value,) = yield [value]
    for s in reversed(range(half - 1)):
        back = move(value, [(s + 1, s), (count - 2 - s, count - 1 - s)])
        value = jnp.where((position == s) | (position == count - 1 - s), back, value)
        (value,) = yield [value]
    yield from both_halves(gate, value, parity)


def wide_reduction(gate, keep, send, parity):
    value = add_low(keep, arrive(gate, swap(send, "ctx", 1)))
    (value,) = yield [value]
    (value,) = yield [lax.psum_scatter(value, "fsdp", scatter_dimension=0, tiled=True)[0]]
    yield from chain(gate, value, parity)


def both_halves(gate, value, parity):
    other = arrive(gate, swap(value, "ctx", 1))
    first = parity == 0
    yield [jnp.concatenate([jnp.where(first, value, other), jnp.where(first, other, value)], axis=0).astype(f32)]


def whole_reduction(gate, keep, send, parity):
    value = add_low(keep, arrive(gate, swap(send, "ctx", 1)))
    (value,) = yield [value]
    (value,) = yield [lax.psum_scatter(value, "fsdp", scatter_dimension=0, tiled=True)[0]]
    groups = [list(range(k, lax.axis_size("ctx"), 2)) for k in (0, 1)]
    (value,) = yield [lax.psum(value, "ctx", axis_index_groups=groups)]
    yield from both_halves(gate, value, parity)


class Staged:
    def __init__(self, stages, *args):
        self.gate, self.values, self.done = [None], None, False
        self.stages = stages(self.gate, *args)

    def step(self):
        try:
            self.values = self.stages.send(self.values)
        except StopIteration:
            self.done = True
        return not self.done

    def result(self):
        while self.step():
            pass
        return self.values


def boundary(done, tie, *transfers, hold=()):
    moving = list(hold)
    for transfer in transfers:
        transfer.gate[0] = done
        if transfer.step():
            moving.append(transfer)
    gates = () if done is None else (done,)
    tie, values = lax.optimization_barrier((tie, [transfer.values for transfer in moving], gates))[:2]
    for transfer, value in zip(moving, values):
        transfer.values = value
    return tie


def gathering_rows(gate, row):
    (value,) = yield [row]
    bit = 1
    while bit < lax.axis_size("fsdp"):
        value = jnp.concatenate([value, swap(value, "fsdp", bit)], axis=0)
        bit *= 2
        (value,) = yield [value]


def body(
    layer_input,
    teacher_states,
    out_cotangent,
    doc_start,
    valid_flag,
    query_weight,
    query_bias,
    key_weight,
    value_weight,
    value_bias,
    proj_weight,
    proj_bias,
    attn_gain,
    attn_shift,
    inner_weight,
    inner_bias,
    outer_weight,
    outer_bias,
    final_gain,
    final_shift,
):
    n_ctx, n_fsdp = lax.axis_size("ctx"), lax.axis_size("fsdp")
    c, f = lax.axis_index("ctx"), lax.axis_index("fsdp")
    parity = c % 2
    tokens = layer_input[0]
    rows = tokens.shape[0]
    part = query_weight.shape[0]
    where = jnp.stack([f, parity]).astype(jnp.int32)
    order = jnp.concatenate([f ^ jnp.arange(n_fsdp, dtype=jnp.int32), parity[None].astype(jnp.int32)])

    def own_half(shard):
        half = shard.shape[0] // 2
        return lax.dynamic_slice_in_dim(shard, parity * half, half)

    qkv_shard, own_qkv = pack_shards(where, query_weight, key_weight, value_weight)
    w_qkv = Staged(gathering, qkv_shard, own_qkv)

    up = [(i, i + 1) for i in range(n_ctx - 1)]
    down = [(b, a) for a, b in up]
    before = lax.ppermute(tokens[rows - DOC_MAX :], "ctx", up)
    behind = lax.ppermute(tokens[:DOC_MAX], "ctx", down)
    flags = valid_flag[0]
    valid = jnp.sum(flags)
    valid = jnp.pad(jnp.stack([valid // 64, valid % 64]).astype(bf16), (0, 126))
    flags = flags.astype(f32)[:, None]
    small = jnp.concatenate(
        [query_bias, value_bias, proj_bias, attn_gain, attn_shift, outer_bias, final_gain, final_shift, inner_bias, valid]
    )
    small = Staged(gathering_rows, small.reshape(1, -1))
    small.step()
    small.step()
    position = c * rows
    starts = doc_start[0]
    near_starts = lax.dynamic_slice_in_dim(
        jnp.concatenate(
            [jnp.full((DOC_MAX,), -1, jnp.int32), starts, jnp.full((DOC_MAX,), 2**30, jnp.int32)]
        ),
        position,
        rows + 2 * DOC_MAX,
    )
    tiles = near_starts.shape[0] // TILE
    low_tile = (near_starts[::TILE] - position + DOC_MAX) // TILE
    last = position - DOC_MAX + TILE * (1 + jnp.arange(tiles, dtype=jnp.int32)) - 1
    ends = jnp.sum((near_starts[None, :] <= last[:, None]).astype(jnp.int32), axis=1)
    high_tile = (ends + TILE - 1) // TILE
    inside = (jnp.arange(tiles) >= RIM) & (jnp.arange(tiles) < tiles - RIM)
    low_tile = jnp.where(inside, low_tile, jnp.maximum(low_tile, RIM))
    high_tile = jnp.where(inside, high_tile, jnp.minimum(high_tile, tiles - RIM))
    idq = near_starts.reshape(tiles, 1, TILE)
    idk = near_starts[:, None]

    own_proj, own_inner = boundary(None, (own_half(proj_weight), own_half(inner_weight)), w_qkv, small)
    w_proj = Staged(gathering, proj_weight, own_proj)
    w_inner = Staged(gathering, inner_weight, own_inner)
    before, behind, idq, idk, low_tile, high_tile, flags = boundary(
        None, (before, behind, idq, idk, low_tile, high_tile, flags), w_qkv
    )
    small = small.result()[0]
    valid = jnp.sum(small[:, -128:].astype(f32), axis=0)
    counted = valid[0] * 64 + valid[1]
    bit = 1
    while bit < n_ctx:
        counted = jnp.full((8, 128), counted, f32) if counted.ndim == 0 else counted
        counted = counted + swap(counted, "ctx", bit)
        bit *= 2
    count = counted[0, 0]
    b_query, b_value, b_proj, g_attn, s_attn, b_outer, g_final, s_final, b_inner = unpack_vectors(where, small)
    w_qkv.values, b_query, b_value, count = lax.optimization_barrier((w_qkv.values, b_query, b_value, count))

    def attend(side, tie, *so_far):
        return attn_fwd(tie, high_tile, query, keys, values_t, idq, idk, side, 2, so_far)

    query, keys, values, keys_t, values_t, w_qkv = project_qkv(where, w_qkv.result(), before, tokens, behind, b_query, b_value)
    tie, own_outer = boundary(query, (low_tile, own_half(outer_weight)), w_proj)
    w_outer = Staged(gathering, outer_weight, own_outer)
    context_a, log_a = attend(0, tie)
    context, log_totals = attend(1, boundary(context_a, low_tile, w_proj, w_inner, w_outer), context_a, log_a)
    normed, normed_low, rate, w_proj = mix_and_norm(
        boundary(context, where, w_proj, w_inner, w_outer), w_proj.values, context, b_proj, tokens, g_attn, s_attn
    )
    tie = boundary(normed, where, w_inner, w_outer)
    act, slope, w_inner = inner_forward(tie, w_inner.values, normed_low, b_inner)
    coef = (n_fsdp * n_ctx * rows / count).reshape(1)
    layer_out, d_sum_two, d_branch, final_sums, w_outer = outer_forward(
        where, w_outer.result(), coef, act, b_outer, normed, g_final, s_final, teacher_states[0], out_cotangent[0], flags
    )

    plain = jnp.concatenate([jnp.arange(n_fsdp, dtype=jnp.int32), order[n_fsdp:]])
    outer = Staged(wide_reduction, *gram(plain, n_fsdp, (act, d_branch)), parity)
    d_pre_a, bias_a, so_far = feed_back(where, 0, d_branch, w_outer, slope, w_inner, d_sum_two)
    d_pre_b, bias_b, d_sum_one, d_attn, attn_sums = feed_back(
        boundary(d_pre_a, where, outer), 1, d_branch, w_outer, slope, w_inner, so_far, (normed, rate, g_attn, s_attn)
    )
    inner_pair = gram(
        after(plain, d_attn), n_fsdp, (normed_low, d_pre_a, d_pre_b), (context, d_attn)
    )
    inner = Staged(whole_reduction, *inner_pair, parity)

    d_context, delta = context_back(after(d_attn, inner_pair[0]), w_proj, context)
    stats = jnp.stack([log_totals, delta])

    def rims(value, axis):
        size = value.shape[axis]
        before = lax.ppermute(lax.slice_in_dim(value, size - DOC_MAX, size, axis=axis), "ctx", up)
        behind = lax.ppermute(lax.slice_in_dim(value, 0, DOC_MAX, axis=axis), "ctx", down)
        return before, behind

    do_before, do_behind = rims(d_context, 0)
    stats_before, stats_behind = rims(stats, 3)
    stats = jnp.concatenate([stats_before, stats, stats_behind], axis=3)
    def attend_back(tie, *part):
        return attn_bwd(
            tie, high_tile, query, do_before, d_context, do_behind, keys, keys_t, values, stats, idq, idk, *part
        )

    parts_a = attend_back(boundary(d_context, low_tile, outer, inner), 0, 0, 1)
    parts_a = attend_back(boundary(parts_a[0], low_tile, outer), 0, 1, 1, parts_a)
    *first_pair, sums_a = qkv_gradient(boundary(parts_a[0], order, outer), tokens, *parts_a, n_fsdp)
    first = Staged(reduction, *first_pair, parity)
    parts_b = attend_back(boundary(first_pair[0], low_tile, inner, hold=[outer]), 1)
    riders = [(final_sums, 4), (attn_sums, 3), (bias_a, 1), (bias_b, 1), (sums_a, 1)]
    *last_pair, sums_b = qkv_gradient(
        boundary(parts_b[0], order, first, outer), tokens, *parts_b, n_fsdp, riders
    )
    last = Staged(reduction, *last_pair, parity, True)
    input_grad = input_back(d_sum_one, (*parts_a, *parts_b), boundary(last_pair[0], w_qkv, first))
    boundary(input_grad, where, last, first, inner)
    boundary(last.values[0], where, last, first)
    boundary(last.values[0], where, last, first)
    outer_grad, inner_grad, first, last = (transfer.result()[0] for transfer in (outer, inner, first, last))
    vectors = last[: part // 2, 3 * D // 2 :].reshape(16, D)
    query_sum, value_sum = vectors[11:13].reshape(2, 2, D // 2).transpose(1, 0, 2).reshape(2, D)
    inner_grad, proj_grad = inner_grad[:, :FF], inner_grad[:, FF:]
    sixth = D // 2
    query_grad, key_grad, value_grad = (
        jnp.concatenate([grad[:, i * sixth : (i + 1) * sixth] for grad in (first, last)], axis=1)
        for i in range(3)
    )
    mse = jnp.sum(vectors[3]) / (count * D)

    def mine(vector):
        length = vector.shape[0] // n_fsdp
        return lax.dynamic_slice_in_dim(vector, f * length, length)

    return (
        layer_out[None],
        input_grad[None],
        mse,
        query_grad,
        mine(query_sum),
        key_grad,
        value_grad,
        mine(value_sum),
        proj_grad,
        mine(vectors[6]),
        mine(vectors[4]),
        mine(vectors[5]),
        inner_grad,
        mine(vectors[7:11].reshape(FF)),
        outer_grad,
        mine(vectors[2]),
        mine(vectors[0]),
        mine(vectors[1]),
    )


def solution(mesh):
    tokens = P("fsdp", "ctx", None)
    matrix, vector = P("fsdp", None), P("fsdp")
    weights = (
        matrix, vector, matrix, matrix, vector, matrix, vector, vector, vector, matrix, vector, matrix, vector, vector, vector,
    )
    return jax.shard_map(
        body,
        mesh=mesh,
        in_specs=(tokens, tokens, tokens, matrix, P("fsdp", "ctx")) + weights,
        out_specs=(tokens, tokens, P()) + weights,
        check_vma=False,
    )
```

```python
import functools

import jax
import jax.numpy as jnp
from jax import lax
from jax.experimental import pallas as pl
from jax.experimental.pallas import tpu as pltpu
from jax.sharding import PartitionSpec as P

D = 1024
FF = 4096
HEAD = 64
DOC_MAX = 512
TILE = 256
RIM = DOC_MAX // TILE
NEG = -1e30
NORM_EPS = 1e-05
VMEM_BYTES = 56 * 2**20
bf16 = jnp.bfloat16
f32 = jnp.float32


def nn(a, b):
    return jnp.dot(a, b, preferred_element_type=f32)


def nt(a, b):
    return lax.dot_general(a, b, (((1,), (1,)), ((), ())), preferred_element_type=f32)


def tn(a, b):
    return lax.dot_general(a, b, (((0,), (0,)), ((), ())), preferred_element_type=f32)


def params():
    return pltpu.CompilerParams(vmem_limit_bytes=VMEM_BYTES)


def cost(flops, bytes_accessed):
    return pl.CostEstimate(flops=int(flops), bytes_accessed=int(bytes_accessed), transcendentals=0)


def sds(shape, dtype):
    return jax.ShapeDtypeStruct(shape, dtype)


def weight_copies(where_ref, pieces, full, out, sem):
    shard, mine, other = pieces[0], pieces[1 : len(pieces) // 2 + 1], pieces[len(pieces) // 2 + 1 :]
    f, parity = where_ref[0], where_ref[1]
    rows = shard.shape[0]
    half, quarter = rows // 2, rows // 4
    copies = []

    def add(source, begin):
        begin = pl.multiple_of(begin, 16)
        copies.append(pltpu.make_async_copy(source, full.at[pl.ds(begin, source.shape[0])], sem.at[len(copies)]))

    add(shard, f * rows)
    at = 0
    for r in range(1, full.shape[0] // rows):
        base = jnp.bitwise_xor(f, r) * rows
        for offset in (0,) if r & (r - 1) == 0 else (0, quarter):
            add(mine[at], base + offset + parity * half)
            add(other[at], base + offset + (1 - parity) * half)
            at += 1
    return copies, pltpu.make_async_copy(full, out, sem.at[len(copies)])


def join_weight(where_ref, pieces, full, out, sem):
    copies, save = weight_copies(where_ref, pieces, full, out, sem)

    @pl.when(pl.program_id(0) == 0)
    def _():
        for copy in copies:
            copy.start()
        for copy in copies:
            copy.wait()
        save.start()

    @pl.when(pl.program_id(0) == pl.num_programs(0) - 1)
    def _():
        save.wait()


def weight_specs(pieces):
    return [pl.BlockSpec(memory_space=pltpu.SMEM)] + [pl.BlockSpec(memory_space=pl.ANY)] * len(pieces)


def weight_scratch(rows, columns):
    return [pltpu.VMEM((rows, columns), bf16), pltpu.SemaphoreType.DMA((64,))]


def pack_kernel(where_ref, q_ref, k_ref, v_ref, shard_ref, own_ref):
    half = own_ref.shape[0]
    first = where_ref[1] == 0
    for side in (0, 1):
        for which, ref in enumerate((q_ref, k_ref, v_ref)):
            columns = qkv_columns(which, side)
            block = ref[:, side * D // 2 : (side + 1) * D // 2]
            shard_ref[:, columns] = block
            own_ref[:, columns] = jnp.where(first, block[:half], block[half:])


def pack_shards(where, q, k, v):
    part = q.shape[0]
    return pl.pallas_call(
        pack_kernel,
        in_specs=[pl.BlockSpec(memory_space=pltpu.SMEM)] + [pl.BlockSpec(memory_space=pltpu.VMEM)] * 3,
        out_specs=[pl.BlockSpec(memory_space=pltpu.VMEM)] * 2,
        out_shape=[sds((part, 3 * D), bf16), sds((part // 2, 3 * D), bf16)],
        compiler_params=params(),
        cost_estimate=cost(0, 4 * 2**20),
        name="pack_shards",
    )(where, q, k, v)


def unpack_kernel(where_ref, packed_ref, *outs):
    packed = packed_ref[...].astype(f32)
    shards = packed.shape[0]
    at = 0
    for out in outs:
        part = out.shape[1] // shards
        for r in range(shards):
            begin = pl.multiple_of(jnp.bitwise_xor(where_ref[0], r) * part, part)
            out[:, pl.ds(begin, part)] = packed[r : r + 1, at : at + part]
        at += part


def unpack_vectors(where, packed):
    return pl.pallas_call(
        unpack_kernel,
        in_specs=[pl.BlockSpec(memory_space=pltpu.SMEM), pl.BlockSpec(memory_space=pltpu.VMEM)],
        out_specs=[pl.BlockSpec(memory_space=pltpu.VMEM)] * 9,
        out_shape=[sds((1, D), f32)] * 8 + [sds((1, FF), f32)],
        compiler_params=params(),
        cost_estimate=cost(0, 2**17),
        name="unpack_vectors",
    )(where, packed)


def qkv_columns(which, side):
    begin = (3 * side + which) * D // 2
    return slice(begin, begin + D // 2)


def qkv_kernel(count, where_ref, *refs):
    pieces, refs = refs[:count], refs[count:]
    before_ref, x_ref, behind_ref, bq_ref, bv_ref, q_ref, k_ref, v_ref, kt_ref, vt_ref, full_ref, w_ref, sem = refs
    join_weight(where_ref, pieces, w_ref, full_ref, sem)
    i = pl.program_id(0)
    x = jnp.where(i == 0, before_ref[...], jnp.where(i == pl.num_programs(0) - 1, behind_ref[...], x_ref[...]))

    for s in (0, 1):
        half = slice(s * D // 2, (s + 1) * D // 2)
        query = (nn(x, w_ref[:, qkv_columns(0, s)]) + bq_ref[:, half]).astype(bf16)
        q_ref[:, half] = query * jnp.asarray(HEAD**-0.5, bf16)
        keys = nn(x, w_ref[:, qkv_columns(1, s)]).astype(bf16)
        k_ref[:, half] = keys
        kt_ref[half, :] = jnp.transpose(keys)
        values = (nn(x, w_ref[:, qkv_columns(2, s)]) + bv_ref[:, half]).astype(bf16)
        v_ref[:, half] = values
        vt_ref[half, :] = jnp.transpose(values)


def project_qkv(where, pieces, before, tokens, behind, bq, bv):
    rows = tokens.shape[0]
    span = rows + 2 * DOC_MAX
    rim = pl.BlockSpec((512, D), lambda i: (0, 0))
    inside = pl.BlockSpec((512, D), lambda i: (jnp.clip(i - 1, 0, rows // 512 - 1), 0))
    row = pl.BlockSpec((1, D), lambda i: (0, 0))
    tall = pl.BlockSpec((512, D), lambda i: (i, 0))
    wide = pl.BlockSpec((D, 512), lambda i: (0, i))
    return pl.pallas_call(
        functools.partial(qkv_kernel, len(pieces)),
        grid=(span // 512,),
        in_specs=weight_specs(pieces) + [rim, inside, rim, row, row],
        out_specs=[
            tall,
            tall,
            tall,
            wide,
            wide,
            pl.BlockSpec(memory_space=pl.ANY),
        ],
        scratch_shapes=weight_scratch(D, 3 * D),
        out_shape=[
            sds((span, D), bf16),
            sds((span, D), bf16),
            sds((span, D), bf16),
            sds((D, span), bf16),
            sds((D, span), bf16),
            sds((D, 3 * D), bf16),
        ],
        compiler_params=params(),
        cost_estimate=cost(2 * D * D * (rows + 2 * span), 30 * 2**20),
        name="project_qkv",
    )(where, *pieces, before, tokens, behind, bq, bv)


def stack_rows(block, stack):
    lanes = lax.broadcasted_iota(jnp.int32, block.shape, 1)
    for h in range(4):
        stack[h * TILE : (h + 1) * TILE, :] = jnp.where(lanes // HEAD == h, block, jnp.zeros_like(block))


def stack_columns(turned, stack):
    for h in range(4):
        heads = slice(h * HEAD, (h + 1) * HEAD)
        stack[heads, h * TILE : (h + 1) * TILE] = turned[heads, :]


def attn_fwd_kernel(lo_ref, hi_ref, q_ref, k_ref, vt_ref, idq_ref, idk_ref, *refs):
    out_ref, lse_ref, qs, acc, top, tot = refs[-6:]
    quads = qs.shape[0]
    t = pl.program_id(0)

    @pl.when(t == 0)
    def _():
        qs[...] = jnp.zeros_like(qs)

    turned = jnp.transpose(q_ref[...])
    for g in range(quads):
        stack_columns(turned[g * 256 : (g + 1) * 256], qs.at[g])
    acc[...] = jnp.zeros_like(acc)
    top[...] = jnp.full_like(top, NEG)
    tot[...] = jnp.zeros_like(tot)

    def step(kt, carry):
        rows = pl.ds(pl.multiple_of(kt * TILE, TILE), TILE)
        bias = jnp.where(idk_ref[rows, :] == idq_ref[0], 0.0, NEG)
        scores = [nn(k_ref[rows, g * 256 : (g + 1) * 256], qs[g]) for g in range(quads)]
        for g in range(quads):
            vt_tile = vt_ref[g * 256 : (g + 1) * 256, rows]
            for h in range(4):
                heads = slice(h * HEAD, (h + 1) * HEAD)
                own = scores[g][:, h * TILE : (h + 1) * TILE] + bias
                old = top[g, h : h + 1, :]
                new = jnp.maximum(old, jnp.max(own, axis=0, keepdims=True))
                top[g, h : h + 1, :] = new
                p = jnp.exp(own - new)
                fade = jnp.exp(old - new)
                tot[g, h : h + 1, :] = tot[g, h : h + 1, :] * fade + jnp.sum(p, axis=0, keepdims=True)
                acc[g, heads, :] = acc[g, heads, :] * fade + nn(vt_tile[heads, :], p.astype(bf16))
        return carry

    lax.fori_loop(lo_ref[t + RIM], hi_ref[t + RIM], step, 0)
    for g in range(quads):
        total = tot[g]
        inverse = 1.0 / total
        for h in range(4):
            heads = slice(h * HEAD, (h + 1) * HEAD)
            acc[g, heads, :] = acc[g, heads, :] * inverse[h : h + 1, :]
        out_ref[:, g * 256 : (g + 1) * 256] = jnp.transpose(acc[g]).astype(bf16)
        lse_ref[g] = top[g] + jnp.log(total)


def attn_fwd(lo, hi, q, k_near, vt_near, idq_rows, idk_col, side, quads, so_far=()):
    span, wide = k_near.shape[0], quads * 256
    rows = span - 2 * DOC_MAX
    return pl.pallas_call(
        attn_fwd_kernel,
        grid_spec=pltpu.PrefetchScalarGridSpec(
            num_scalar_prefetch=2,
            grid=(rows // TILE,),
            in_specs=[
                pl.BlockSpec((TILE, wide), lambda t, *_: (t + RIM, side)),
                pl.BlockSpec((span, wide), lambda t, *_: (0, side)),
                pl.BlockSpec((wide, span), lambda t, *_: (side, 0)),
                pl.BlockSpec((1, 1, TILE), lambda t, *_: (t + RIM, 0, 0)),
                pl.BlockSpec((span, 1), lambda t, *_: (0, 0)),
            ]
            + [pl.BlockSpec(memory_space=pl.ANY)] * len(so_far),
            out_specs=[
                pl.BlockSpec((TILE, wide), lambda t, *_: (t, side)),
                pl.BlockSpec((quads, 8, TILE), lambda t, *_: (side, 0, t)),
            ],
            scratch_shapes=[
                pltpu.VMEM((quads, 256, 4 * TILE), bf16),
                pltpu.VMEM((quads, 256, TILE), f32),
                pltpu.VMEM((quads, 8, TILE), f32),
                pltpu.VMEM((quads, 8, TILE), f32),
            ],
        ),
        out_shape=[sds((rows, D), bf16), sds((D // 256, 8, rows), f32)],
        input_output_aliases={7 + i: i for i in range(len(so_far))},
        compiler_params=params(),
        cost_estimate=cost(quads * 10**10, 2**21),
        name="attn_forward",
    )(lo, hi, q, k_near, vt_near, idq_rows, idk_col, *so_far)


def attn_bwd_kernel(
    lo_ref, hi_ref, q_ref, before_ref, do_ref, behind_ref, k_ref, kt_ref, v_ref, stats_ref, idq_ref, idk_ref, *refs
):
    dq_ref, joined_ref, qs, dos, qst, dost, dk_acc, dv_acc, dq_acc = refs[-9:]
    t = pl.program_id(1)
    low, high = lo_ref[t], hi_ref[t]
    end = pl.num_programs(1) - RIM
    own_low, own_high = jnp.maximum(low, RIM), jnp.minimum(high, end)

    @pl.when((t == 0) & (pl.program_id(0) == 0))
    def _():
        qst[...] = jnp.zeros_like(qst)
        dost[...] = jnp.zeros_like(dost)

    @pl.when(t == 0)
    def _():
        dk_acc[...] = jnp.zeros_like(dk_acc)
        dv_acc[...] = jnp.zeros_like(dv_acc)

    @pl.when(low < high)
    def _():
        q = q_ref[...]
        do = jnp.where(t < RIM, before_ref[...], jnp.where(t >= end, behind_ref[...], do_ref[...]))
        stack_rows(q, qs)
        stack_rows(do, dos)
        stack_columns(jnp.transpose(q), qst)
        stack_columns(jnp.transpose(do), dost)
        lse_row, delta_row = (
            jnp.concatenate([stats_ref[s, 0, h : h + 1] for h in range(4)], axis=1) for s in (0, 1)
        )
        dq_acc[...] = jnp.zeros_like(dq_acc)

        def step(own, answer, kt, carry):
            rows = pl.ds(pl.multiple_of(kt * TILE, TILE), TILE)
            bias = jnp.where(idk_ref[rows, :] == idq_ref[0], 0.0, NEG)
            s = nn(k_ref[rows, :], qst[...])
            dp = nn(v_ref[rows, :], dost[...])
            p = jnp.exp(s + jnp.concatenate([bias] * 4, axis=1) - lse_row)
            ds = (p * (dp - delta_row)).astype(bf16)
            if own:
                inside = pl.ds(pl.multiple_of((kt - RIM) * TILE, TILE), TILE)
                dv_acc[inside, :] += nn(p.astype(bf16), dos[...])
                dk_acc[inside, :] += nn(ds, qs[...])
            if answer:
                kt_tile = kt_ref[:, rows]
                for h in range(4):
                    heads = slice(h * HEAD, (h + 1) * HEAD)
                    dq_acc[heads, :] += nn(kt_tile[heads, :], ds[:, h * TILE : (h + 1) * TILE])
            return carry

        @pl.when((t < RIM) | (t >= end))
        def _():
            lax.fori_loop(own_low, own_high, functools.partial(step, True, False), 0)

        @pl.when((t >= RIM) & (t < end))
        def _():
            lax.fori_loop(low, jnp.minimum(high, RIM), functools.partial(step, False, True), 0)
            lax.fori_loop(own_low, own_high, functools.partial(step, True, True), 0)
            lax.fori_loop(jnp.maximum(low, end), high, functools.partial(step, False, True), 0)
            dq_ref[...] = (jnp.transpose(dq_acc[...]) * (HEAD**-0.5)).astype(bf16)

    @pl.when(t == pl.num_programs(1) - 1)
    def _():
        joined_ref[0] = dk_acc[...].astype(bf16)
        joined_ref[1] = dv_acc[...].astype(bf16)


def attn_bwd(lo, hi, q_near, before, do, behind, k_near, kt_near, v_near, stats, idq_rows, idk_col, side, begin=0, quads=2, so_far=()):
    rows, span = do.shape[0], k_near.shape[0]
    tiles, first = rows // TILE, 2 * side + begin
    near = pl.BlockSpec((span, 256), lambda g, t, *_: (0, g + first))
    return pl.pallas_call(
        attn_bwd_kernel,
        grid_spec=pltpu.PrefetchScalarGridSpec(
            num_scalar_prefetch=2,
            grid=(quads, span // TILE),
            in_specs=[
                pl.BlockSpec((TILE, 256), lambda g, t, *_: (t, g + first)),
                pl.BlockSpec((TILE, 256), lambda g, t, *_: (jnp.clip(t, 0, RIM - 1), g + first)),
                pl.BlockSpec((TILE, 256), lambda g, t, *_: (jnp.clip(t - RIM, 0, tiles - 1), g + first)),
                pl.BlockSpec((TILE, 256), lambda g, t, *_: (jnp.clip(t - RIM - tiles, 0, RIM - 1), g + first)),
                near,
                pl.BlockSpec((256, span), lambda g, t, *_: (g + first, 0)),
                near,
                pl.BlockSpec((2, 1, 8, TILE), lambda g, t, *_: (0, g + first, 0, t)),
                pl.BlockSpec((1, 1, TILE), lambda g, t, *_: (t, 0, 0)),
                pl.BlockSpec((span, 1), lambda g, t, *_: (0, 0)),
            ]
            + [pl.BlockSpec(memory_space=pl.ANY)] * len(so_far),
            out_specs=[
                pl.BlockSpec((TILE, 256), lambda g, t, *_: (jnp.clip(t - RIM, 0, tiles - 1), g + begin)),
                pl.BlockSpec((2, rows, 256), lambda g, t, *_: (0, 0, g + begin)),
            ],
            scratch_shapes=[
                pltpu.VMEM((4 * TILE, 256), bf16),
                pltpu.VMEM((4 * TILE, 256), bf16),
                pltpu.VMEM((256, 4 * TILE), bf16),
                pltpu.VMEM((256, 4 * TILE), bf16),
                pltpu.VMEM((rows, 256), f32),
                pltpu.VMEM((rows, 256), f32),
                pltpu.VMEM((256, TILE), f32),
            ],
        ),
        out_shape=[sds((rows, 512), bf16), sds((2, rows, 512), bf16)],
        input_output_aliases={12 + i: i for i in range(len(so_far))},
        compiler_params=params(),
        cost_estimate=cost(quads * 15 * 10**9, 2**22),
        name="attn_backward",
    )(lo, hi, q_near, before, do, behind, k_near, kt_near, v_near, stats, idq_rows, idk_col, *so_far)


def norm_stats(hidden):
    center = hidden - jnp.mean(hidden, axis=1, keepdims=True)
    rate = lax.rsqrt(jnp.mean(center * center, axis=1, keepdims=True) + NORM_EPS)
    return center * rate, rate


def norm_back(grad, unit, rate):
    return rate * (
        grad - jnp.mean(grad, axis=1, keepdims=True) - unit * jnp.mean(grad * unit, axis=1, keepdims=True)
    )


def mix_kernel(count, where_ref, *refs):
    pieces, refs = refs[:count], refs[count:]
    c_ref, b_ref, x_ref, g_ref, s_ref, normed_ref, low_ref, rate_ref, full_ref, w_ref, sem = refs
    join_weight(where_ref, pieces, w_ref, full_ref, sem)
    hidden = x_ref[...].astype(f32) + (nn(c_ref[...], w_ref[...]) + b_ref[...])
    unit, rate = norm_stats(hidden)
    normed = unit * g_ref[...] + s_ref[...]
    normed_ref[...] = normed
    low_ref[...] = normed.astype(bf16)
    rate_ref[...] = rate


def mix_and_norm(where, pieces, context, b, tokens, gain, shift):
    rows = tokens.shape[0]
    tile = pl.BlockSpec((TILE, D), lambda i: (i, 0))
    row = pl.BlockSpec((1, D), lambda i: (0, 0))
    return pl.pallas_call(
        functools.partial(mix_kernel, len(pieces)),
        grid=(rows // TILE,),
        in_specs=weight_specs(pieces) + [tile, row, tile, row, row],
        out_specs=[tile, tile, pl.BlockSpec((TILE, 1), lambda i: (i, 0)), pl.BlockSpec(memory_space=pl.ANY)],
        out_shape=[sds((rows, D), f32), sds((rows, D), bf16), sds((rows, 1), f32), sds((D, D), bf16)],
        scratch_shapes=weight_scratch(D, D),
        compiler_params=params(),
        cost_estimate=cost(2 * D * D * rows, 14 * 2**20),
        name="mix_and_norm",
    )(where, *pieces, context, b, tokens, gain, shift)


def gelu_parts(u):
    t = 1.0 / (1.0 + (0.3275911 * 0.7071067811865476) * jnp.abs(u))
    poly = t * (0.254829592 + t * (-0.284496736 + t * (1.421413741 + t * (-1.453152027 + t * 1.061405429))))
    bell = jnp.exp(-0.5 * u * u)
    tail = 0.5 * poly * bell
    share = jnp.where(u >= 0, 1.0 - tail, tail)
    return u * share, share + u * bell * 0.3989422804014327


def inner_kernel(count, where_ref, *refs):
    pieces, (x_ref, b_ref, act_ref, slope_ref, full_ref, w_ref, sem) = refs[:count], refs[count:]
    join_weight(where_ref, pieces, w_ref, full_ref, sem)
    wide = act_ref.shape[1]
    columns = pl.ds(pl.multiple_of(pl.program_id(0) * wide, wide), wide)
    weight = w_ref[:, columns]
    parts = [slice(i, i + 128) for i in range(0, x_ref.shape[0], 128)]
    ahead = nn(x_ref[parts[0], :], weight)
    for i, rows in enumerate(parts):
        pre = ahead
        if i + 1 < len(parts):
            ahead = nn(x_ref[parts[i + 1], :], weight)
        act, slope = gelu_parts(pre + b_ref[...])
        act_ref[rows, :] = act.astype(bf16)
        slope_ref[rows, :] = slope.astype(bf16)


def inner_forward(where, pieces, x, b):
    rows, wide = x.shape[0], 512
    block = pl.BlockSpec((rows, wide), lambda j: (0, j))
    return pl.pallas_call(
        functools.partial(inner_kernel, len(pieces)),
        grid=(FF // wide,),
        in_specs=weight_specs(pieces)
        + [pl.BlockSpec((rows, D), lambda j: (0, 0)), pl.BlockSpec((1, wide), lambda j: (0, j))],
        out_specs=[block, block, pl.BlockSpec(memory_space=pl.ANY)],
        out_shape=[sds((rows, FF), bf16), sds((rows, FF), bf16), sds((D, FF), bf16)],
        scratch_shapes=weight_scratch(D, FF),
        compiler_params=params(),
        cost_estimate=cost(2 * D * FF * rows, 26 * 2**20),
        name="inner_forward",
    )(where, *pieces, x, b)


def outer_kernel(count, where_ref, *refs):
    pieces, refs = refs[:count], refs[count:]
    coef_ref, act_ref, b_ref, normed_ref, g_ref, s_ref, teach_ref, cot_ref, flag_ref = refs[:9]
    out_ref, dsum_ref, dlow_ref, sums_ref, full_ref, w_ref, sem = refs[9:]
    join_weight(where_ref, pieces, w_ref, full_ref, sem)
    hidden = normed_ref[...] + (nn(act_ref[...], w_ref[...]) + b_ref[...])
    unit, rate = norm_stats(hidden)
    gain = g_ref[...]
    final = unit * gain + s_ref[...]
    out_ref[...] = final.astype(bf16)
    error = final - teach_ref[...].astype(f32)
    marked = flag_ref[...] * error
    grad = cot_ref[...].astype(f32) + coef_ref[0] * marked
    dsum = norm_back(grad * gain, unit, rate)
    dsum_ref[...] = dsum
    low = dsum.astype(bf16)
    dlow_ref[...] = low

    @pl.when(pl.program_id(0) == 0)
    def _():
        sums_ref[...] = jnp.zeros_like(sums_ref)

    sums_ref[0:1, :] += jnp.sum(grad * unit, axis=0, keepdims=True)
    sums_ref[1:2, :] += jnp.sum(grad, axis=0, keepdims=True)
    sums_ref[2:3, :] += jnp.sum(low.astype(f32), axis=0, keepdims=True)
    sums_ref[3:4, :] += jnp.sum(marked * error, axis=0, keepdims=True)


def outer_forward(where, pieces, coef, act, b, normed, gain, shift, teacher, cotangent, flags):
    rows = act.shape[0]
    tile = pl.BlockSpec((TILE, D), lambda i: (i, 0))
    row = pl.BlockSpec((1, D), lambda i: (0, 0))
    return pl.pallas_call(
        functools.partial(outer_kernel, len(pieces)),
        grid=(rows // TILE,),
        in_specs=weight_specs(pieces)
        + [
            pl.BlockSpec(memory_space=pltpu.SMEM),
            pl.BlockSpec((TILE, FF), lambda i: (i, 0)),
            row, tile, row, row, tile, tile,
            pl.BlockSpec((TILE, 1), lambda i: (i, 0)),
        ],
        out_specs=[
            tile, tile, tile, pl.BlockSpec((8, D), lambda i: (0, 0)), pl.BlockSpec(memory_space=pl.ANY),
        ],
        out_shape=[
            sds((rows, D), bf16), sds((rows, D), f32), sds((rows, D), bf16), sds((8, D), f32), sds((FF, D), bf16),
        ],
        scratch_shapes=weight_scratch(FF, D),
        compiler_params=params(),
        cost_estimate=cost(2 * D * FF * rows, 32 * 2**20),
        name="outer_forward",
    )(where, *pieces, coef, act, b, normed, gain, shift, teacher, cotangent, flags)


def put_halves(keep_ref, send_ref, first, begin, grad):
    half = keep_ref.shape[1]
    columns = slice(begin, begin + grad.shape[1])
    low, high = grad[:half], grad[half:]
    keep_ref[0, :, columns] = jnp.where(first, low, high).astype(bf16)
    send_ref[0, :, columns] = jnp.where(first, high, low).astype(bf16)


def gram_kernel(counts, order_ref, *refs):
    operands, keep_ref, send_ref = list(refs[:-2]), refs[-2], refs[-1]
    first = order_ref[pl.num_programs(0)] == 0
    at = 0
    for count in counts:
        left = operands.pop(0)[...]
        for _ in range(count):
            right_ref = operands.pop(0)
            put_halves(keep_ref, send_ref, first, at, tn(left, right_ref[...]))
            at += right_ref.shape[1]


def gram(order, shards, *groups):
    tokens, height = groups[0][0].shape
    part = height // shards
    columns = sum(right.shape[1] for group in groups for right in group[1:])
    out = pl.BlockSpec((1, part // 2, columns), lambda r, order_ref: (r, 0, 0))
    in_specs = []
    for group in groups:
        in_specs.append(pl.BlockSpec((tokens, part), lambda r, order_ref: (0, order_ref[r])))
        in_specs += [pl.BlockSpec((tokens, right.shape[1]), lambda r, order_ref: (0, 0)) for right in group[1:]]
    return pl.pallas_call(
        functools.partial(gram_kernel, [len(group) - 1 for group in groups]),
        grid_spec=pltpu.PrefetchScalarGridSpec(
            num_scalar_prefetch=1, grid=(shards,), in_specs=in_specs, out_specs=[out, out]
        ),
        out_shape=[sds((shards, part // 2, columns), bf16)] * 2,
        compiler_params=params(),
        cost_estimate=cost(2 * tokens * height * columns, 2 * (tokens * (height + columns) + height * columns)),
        name="gram",
    )(order, *[operand for group in groups for operand in group])


def feed_back_columns(db_ref, wo_ref, slope_ref, wi_ref, dpre_ref, bias_ref, total):
    ones = jnp.ones((8, TILE), bf16)
    bias = jnp.zeros(bias_ref.shape, f32)
    for i in range(db_ref.shape[0] // TILE):
        rows = slice(i * TILE, (i + 1) * TILE)
        pre = (nt(db_ref[rows, :], wo_ref[...]) * slope_ref[rows, :].astype(f32)).astype(bf16)
        dpre_ref[rows, :] = pre
        bias += nn(ones, pre)
        total[rows, :] += nt(pre, wi_ref[...])
    bias_ref[...] = bias


def feed_back_first_kernel(tie_ref, db_ref, wo_ref, slope_ref, wi_ref, dsum_ref, dpre_ref, bias_ref, total):
    @pl.when(pl.program_id(0) == 0)
    def _():
        total[...] = dsum_ref[...]

    feed_back_columns(db_ref, wo_ref, slope_ref, wi_ref, dpre_ref, bias_ref, total)


def feed_back_last_kernel(
    tie_ref, db_ref, wo_ref, slope_ref, wi_ref, dsum_ref, normed_ref, rate_ref, g_ref, s_ref,
    dpre_ref, bias_ref, done_ref, dattn_ref, sums_ref, total,
):
    @pl.when(pl.program_id(0) == 0)
    def _():
        total[...] = dsum_ref[...]

    feed_back_columns(db_ref, wo_ref, slope_ref, wi_ref, dpre_ref, bias_ref, total)

    @pl.when(pl.program_id(0) == pl.num_programs(0) - 1)
    def _():
        gain = g_ref[...]
        sums_ref[...] = jnp.zeros_like(sums_ref)
        for i in range(db_ref.shape[0] // TILE):
            rows = slice(i * TILE, (i + 1) * TILE)
            grad = total[rows, :]
            unit = (normed_ref[rows, :] - s_ref[...]) / gain
            done = norm_back(grad * gain, unit, rate_ref[rows, :])
            done_ref[rows, :] = done
            low = done.astype(bf16)
            dattn_ref[rows, :] = low
            sums_ref[0:1, :] += jnp.sum(grad * unit, axis=0, keepdims=True)
            sums_ref[1:2, :] += jnp.sum(grad, axis=0, keepdims=True)
            sums_ref[2:3, :] += jnp.sum(low.astype(f32), axis=0, keepdims=True)


def feed_back(tie, side, d_branch, w_outer, slope, w_inner, so_far, norm=None):
    rows, wide = d_branch.shape[0], 512
    steps = FF // wide // 2
    begin = side * steps
    whole = pl.BlockSpec((rows, D), lambda j: (0, 0))
    row = pl.BlockSpec((1, D), lambda j: (0, 0))
    in_specs = [
        pl.BlockSpec(memory_space=pltpu.SMEM),
        whole,
        pl.BlockSpec((wide, D), lambda j: (j + begin, 0)),
        pl.BlockSpec((rows, wide), lambda j: (0, j + begin)),
        pl.BlockSpec((D, wide), lambda j: (0, j + begin)),
        whole,
    ]
    out_specs = [pl.BlockSpec((rows, wide), lambda j: (0, j)), pl.BlockSpec((8, wide), lambda j: (0, j)), whole]
    out_shape = [sds((rows, FF // 2), bf16), sds((8, FF // 2), f32), sds((rows, D), f32)]
    args = (tie, d_branch, w_outer, slope, w_inner, so_far)
    common = dict(grid=(steps,), compiler_params=params(), cost_estimate=cost(2 * D * FF * rows, 30 * 2**20))
    if norm is None:
        return pl.pallas_call(
            feed_back_first_kernel,
            in_specs=in_specs,
            out_specs=out_specs,
            out_shape=out_shape,
            name="feed_back_first",
            **common,
        )(*args)
    return pl.pallas_call(
        feed_back_last_kernel,
        in_specs=in_specs + [whole, pl.BlockSpec((rows, 1), lambda j: (0, 0)), row, row],
        out_specs=out_specs + [whole, pl.BlockSpec((8, D), lambda j: (0, 0))],
        out_shape=out_shape + [sds((rows, D), bf16), sds((8, D), f32)],
        scratch_shapes=[pltpu.VMEM((rows, D), f32)],
        name="feed_back_last",
        **common,
    )(*args, *norm)


def turn_kernel(d_ref, w_ref, context_ref, out_ref, delta_ref):
    out = nt(d_ref[...], w_ref[...]).astype(bf16)
    out_ref[...] = out
    select = (
        lax.broadcasted_iota(jnp.int32, (8, 256), 1) // HEAD == lax.broadcasted_iota(jnp.int32, (8, 256), 0)
    ).astype(bf16)
    for g in range(D // 256):
        lanes = slice(g * 256, (g + 1) * 256)
        product = out[:, lanes].astype(f32) * context_ref[:, lanes].astype(f32)
        high = product.astype(bf16)
        low = (product - high.astype(f32)).astype(bf16)
        delta_ref[g] = nt(select, high) + nt(select, low)


def context_back(d, w, context):
    rows = d.shape[0]
    tile = pl.BlockSpec((TILE, D), lambda i: (i, 0))
    return pl.pallas_call(
        turn_kernel,
        grid=(rows // TILE,),
        in_specs=[tile, pl.BlockSpec((D, D), lambda i: (0, 0)), tile],
        out_specs=[tile, pl.BlockSpec((D // 256, 8, TILE), lambda i: (0, 0, i))],
        out_shape=[sds((rows, D), bf16), sds((D // 256, 8, rows), f32)],
        compiler_params=params(),
        cost_estimate=cost(2 * D * D * rows, 8 * 2**20),
        name="context_back",
    )(d, w, context)


def qkv_gradient_kernel(used, order_ref, x_ref, dq_ref, joined_ref, *refs):
    riders, (keep_ref, send_ref, sums_ref, rider) = refs[:-4], refs[-4:]
    rows, wide = dq_ref.shape
    first = order_ref[pl.num_programs(0)] == 0

    @pl.when(pl.program_id(0) == 0)
    def _():
        ones = jnp.ones((8, rows), bf16)
        sums_ref[:, :wide] = nn(ones, dq_ref[...])
        sums_ref[:, wide:] = nn(ones, joined_ref[1])

    x = x_ref[...]
    for i, grad in enumerate((dq_ref[...], joined_ref[0], joined_ref[1])):
        put_halves(keep_ref, send_ref, first, i * wide, tn(x, grad))
    if keep_ref.shape[2] > 3 * wide:
        lanes = rider.shape[1]

        @pl.when(pl.program_id(0) == 0)
        def _():
            rider[...] = jnp.zeros_like(rider)
            at = 0
            for ref, height in zip((*riders, sums_ref), (*used, 1)):
                for i in range(height):
                    for begin in range(0, ref.shape[1], lanes):
                        rider[at : at + 1, :] = ref[i : i + 1, begin : begin + lanes]
                        at += 1

        low = rider[...].astype(bf16)
        keep_ref[0, :, 3 * wide :] = low
        send_ref[0, :, 3 * wide :] = low


def qkv_gradient(order, tokens, dq, joined, shards, riders=()):
    rows, wide = dq.shape
    part = D // shards
    lanes = 16 * D // (part // 2)
    columns = 3 * wide + (lanes if riders else 0)
    sums = [array for array, _ in riders]
    out = pl.BlockSpec((1, part // 2, columns), lambda r, order_ref: (r, 0, 0))
    left = pl.BlockSpec((rows, part), lambda r, order_ref: (0, order_ref[r]))
    whole = pl.BlockSpec((rows, wide), lambda r, order_ref: (0, 0))
    both = pl.BlockSpec((2, rows, wide), lambda r, order_ref: (0, 0, 0))
    return pl.pallas_call(
        functools.partial(qkv_gradient_kernel, [height for _, height in riders]),
        grid_spec=pltpu.PrefetchScalarGridSpec(
            num_scalar_prefetch=1,
            grid=(shards,),
            in_specs=[left, whole, both]
            + [pl.BlockSpec(array.shape, lambda r, order_ref: (0, 0)) for array in sums],
            out_specs=[out, out, pl.BlockSpec((8, 2 * wide), lambda r, order_ref: (0, 0))],
            scratch_shapes=[pltpu.VMEM((part // 2, lanes), f32)],
        ),
        out_shape=[sds((shards, part // 2, columns), bf16)] * 2 + [sds((8, 2 * wide), f32)],
        compiler_params=params(),
        cost_estimate=cost(2 * rows * D * columns, 16 * 2**20),
        name="qkv_gradient",
    )(order, tokens, dq, joined, *sums)


def input_kernel(base_ref, *refs):
    grads, w_ref, out_ref = refs[:-2], refs[-2], refs[-1]
    total = base_ref[...]
    for side in (0, 1):
        dq_ref, joined_ref = grads[2 * side : 2 * side + 2]
        for which, grad in enumerate((dq_ref[...], joined_ref[0], joined_ref[1])):
            total += nt(grad, w_ref[:, qkv_columns(which, side)])
    out_ref[...] = total


def input_back(base, grads, w):
    rows = base.shape[0]
    tile = pl.BlockSpec((TILE, D), lambda i: (i, 0))
    side = [pl.BlockSpec((TILE, D // 2), lambda i: (i, 0)), pl.BlockSpec((2, TILE, D // 2), lambda i: (0, i, 0))]
    return pl.pallas_call(
        input_kernel,
        grid=(rows // TILE,),
        in_specs=[tile, *side, *side, pl.BlockSpec((D, 3 * D), lambda i: (0, 0))],
        out_specs=tile,
        out_shape=sds((rows, D), f32),
        compiler_params=params(),
        cost_estimate=cost(6 * D * D * rows, 20 * 2**20),
        name="input_back",
    )(base, *grads, w)


def swap(value, axis, bit):
    return lax.ppermute(value, axis, [(i, i ^ bit) for i in range(lax.axis_size(axis))])


def after(value, *others):
    return lax.optimization_barrier((value,) + others)[0]


def arrive(gate, value):
    return value if gate[0] is None else after(value, gate[0])


def gathering(gate, shard, own):
    n = lax.axis_size("fsdp")
    quarter = shard.shape[0] // 4
    near = [1 << b for b in range(n.bit_length() - 1)]
    whole = dict(zip(near, (yield [arrive(gate, swap(own, "fsdp", r)) for r in near])))
    held = {(r, s): value[s * quarter : (s + 1) * quarter] for r, value in whole.items() for s in (0, 1)}
    found = []
    for r in range(1, n):
        if r in whole:
            found.append(whole[r])
        else:
            for s, bit in ((0, 1 << (r.bit_length() - 1)), (1, r & -r)):
                held[r, s] = arrive(gate, swap(held[r ^ bit, s], "fsdp", bit))
                found.append(held[r, s])
    found = yield found
    yield [shard, *found, *[arrive(gate, swap(value, "ctx", 1)) for value in found]]


def half_sets(value, bit):
    shape = value.shape
    split = value.reshape((shape[0] // (2 * bit), 2, bit) + shape[1:])
    rest = (shape[0] // 2,) + shape[1:]
    return split[:, 0].reshape(rest), split[:, 1].reshape(rest)


def add_low(a, b):
    return (a.astype(f32) + b.astype(f32)).astype(bf16)


def reduction(gate, keep, send, parity, short=False):
    got = arrive(gate, swap(send, "ctx", 1))
    n = lax.axis_size("fsdp")
    quarter = keep.shape[1] // 2
    bits = [1 << b for b in range(n.bit_length() - 1)]
    streams = [(order, list(range(n))) for order in (bits, bits[::-1])]
    parts = [add_low(keep[:, s * quarter : (s + 1) * quarter], got[:, s * quarter : (s + 1) * quarter]) for s in (0, 1)]
    parts = list((yield parts))
    for k in range(len(bits)):
        for s, (order, ids) in enumerate(streams):
            bit = order[k]
            step = [i for i, r in enumerate(ids) if r & bit][0]
            ids[:] = [r for r in ids if not r & bit]
            mine, theirs = half_sets(parts[s], step)
            parts[s] = add_low(mine, arrive(gate, swap(theirs, "fsdp", bit)))
        if k < len(bits) - 1:
            parts = list((yield parts))
    value = jnp.concatenate([part[0] for part in parts], axis=0)
    (value,) = yield [value]
    if short:
        bit = 2
        while bit < lax.axis_size("ctx"):
            value = add_low(value, arrive(gate, swap(value, "ctx", bit)))
            (value,) = yield [value]
            bit *= 2
        yield from both_halves(gate, value, parity)
    else:
        yield from chain(gate, value, parity)


def chain(gate, value, parity):
    count = lax.axis_size("ctx") // 2
    position = lax.axis_index("ctx") // 2
    half = count // 2

    def move(value, chip_pairs):
        pairs = [(2 * a + c, 2 * b + c) for a, b in chip_pairs for c in (0, 1)]
        return arrive(gate, lax.ppermute(value, "ctx", pairs))

    for s in range(half - 1):
        value = add_low(value, move(value, [(s, s + 1), (count - 1 - s, count - 2 - s)]))
        (value,) = yield [value]
    inner = (position == half - 1) | (position == half)
    across = move(value, [(half - 1, half), (half, half - 1)])
    value = jnp.where(inner, add_low(value, across), value)
    (value,) = yield [value]
    for s in reversed(range(half - 1)):
        back = move(value, [(s + 1, s), (count - 2 - s, count - 1 - s)])
        value = jnp.where((position == s) | (position == count - 1 - s), back, value)
        (value,) = yield [value]
    yield from both_halves(gate, value, parity)


def wide_reduction(gate, keep, send, parity):
    value = add_low(keep, arrive(gate, swap(send, "ctx", 1)))
    (value,) = yield [value]
    (value,) = yield [lax.psum_scatter(value, "fsdp", scatter_dimension=0, tiled=True)[0]]
    yield from chain(gate, value, parity)


def both_halves(gate, value, parity):
    other = arrive(gate, swap(value, "ctx", 1))
    first = parity == 0
    yield [jnp.concatenate([jnp.where(first, value, other), jnp.where(first, other, value)], axis=0).astype(f32)]


def whole_reduction(gate, keep, send, parity):
    value = add_low(keep, arrive(gate, swap(send, "ctx", 1)))
    (value,) = yield [value]
    (value,) = yield [lax.psum_scatter(value, "fsdp", scatter_dimension=0, tiled=True)[0]]
    groups = [list(range(k, lax.axis_size("ctx"), 2)) for k in (0, 1)]
    (value,) = yield [lax.psum(value, "ctx", axis_index_groups=groups)]
    yield from both_halves(gate, value, parity)


class Staged:
    def __init__(self, stages, *args):
        self.gate, self.values, self.done = [None], None, False
        self.stages = stages(self.gate, *args)

    def step(self):
        try:
            self.values = self.stages.send(self.values)
        except StopIteration:
            self.done = True
        return not self.done

    def result(self):
        while self.step():
            pass
        return self.values


def boundary(done, tie, *transfers, hold=()):
    moving = list(hold)
    for transfer in transfers:
        transfer.gate[0] = done
        if transfer.step():
            moving.append(transfer)
    gates = () if done is None else (done,)
    tie, values = lax.optimization_barrier((tie, [transfer.values for transfer in moving], gates))[:2]
    for transfer, value in zip(moving, values):
        transfer.values = value
    return tie


def gathering_rows(gate, row):
    (value,) = yield [row]
    bit = 1
    while bit < lax.axis_size("fsdp"):
        value = jnp.concatenate([value, swap(value, "fsdp", bit)], axis=0)
        bit *= 2
        (value,) = yield [value]


def body(
    layer_input,
    teacher_states,
    out_cotangent,
    doc_start,
    valid_flag,
    query_weight,
    query_bias,
    key_weight,
    value_weight,
    value_bias,
    proj_weight,
    proj_bias,
    attn_gain,
    attn_shift,
    inner_weight,
    inner_bias,
    outer_weight,
    outer_bias,
    final_gain,
    final_shift,
):
    n_ctx, n_fsdp = lax.axis_size("ctx"), lax.axis_size("fsdp")
    c, f = lax.axis_index("ctx"), lax.axis_index("fsdp")
    parity = c % 2
    tokens = layer_input[0]
    rows = tokens.shape[0]
    part = query_weight.shape[0]
    where = jnp.stack([f, parity]).astype(jnp.int32)
    order = jnp.concatenate([f ^ jnp.arange(n_fsdp, dtype=jnp.int32), parity[None].astype(jnp.int32)])

    def own_half(shard):
        half = shard.shape[0] // 2
        return lax.dynamic_slice_in_dim(shard, parity * half, half)

    qkv_shard, own_qkv = pack_shards(where, query_weight, key_weight, value_weight)
    w_qkv = Staged(gathering, qkv_shard, own_qkv)

    up = [(i, i + 1) for i in range(n_ctx - 1)]
    down = [(b, a) for a, b in up]
    before = lax.ppermute(tokens[rows - DOC_MAX :], "ctx", up)
    behind = lax.ppermute(tokens[:DOC_MAX], "ctx", down)
    flags = valid_flag[0]
    valid = jnp.sum(flags)
    valid = jnp.pad(jnp.stack([valid // 64, valid % 64]).astype(bf16), (0, 126))
    flags = flags.astype(f32)[:, None]
    small = jnp.concatenate(
        [query_bias, value_bias, proj_bias, attn_gain, attn_shift, outer_bias, final_gain, final_shift, inner_bias, valid]
    )
    small = Staged(gathering_rows, small.reshape(1, -1))
    small.step()
    small.step()
    position = c * rows
    starts = doc_start[0]
    near_starts = lax.dynamic_slice_in_dim(
        jnp.concatenate(
            [jnp.full((DOC_MAX,), -1, jnp.int32), starts, jnp.full((DOC_MAX,), 2**30, jnp.int32)]
        ),
        position,
        rows + 2 * DOC_MAX,
    )
    tiles = near_starts.shape[0] // TILE
    low_tile = (near_starts[::TILE] - position + DOC_MAX) // TILE
    last = position - DOC_MAX + TILE * (1 + jnp.arange(tiles, dtype=jnp.int32)) - 1
    ends = jnp.sum((near_starts[None, :] <= last[:, None]).astype(jnp.int32), axis=1)
    high_tile = (ends + TILE - 1) // TILE
    inside = (jnp.arange(tiles) >= RIM) & (jnp.arange(tiles) < tiles - RIM)
    low_tile = jnp.where(inside, low_tile, jnp.maximum(low_tile, RIM))
    high_tile = jnp.where(inside, high_tile, jnp.minimum(high_tile, tiles - RIM))
    idq = near_starts.reshape(tiles, 1, TILE)
    idk = near_starts[:, None]

    own_proj, own_inner = boundary(None, (own_half(proj_weight), own_half(inner_weight)), w_qkv, small)
    w_proj = Staged(gathering, proj_weight, own_proj)
    w_inner = Staged(gathering, inner_weight, own_inner)
    before, behind, idq, idk, low_tile, high_tile, flags = boundary(
        None, (before, behind, idq, idk, low_tile, high_tile, flags), w_qkv
    )
    small = small.result()[0]
    valid = jnp.sum(small[:, -128:].astype(f32), axis=0)
    counted = valid[0] * 64 + valid[1]
    bit = 1
    while bit < n_ctx:
        counted = jnp.full((8, 128), counted, f32) if counted.ndim == 0 else counted
        counted = counted + swap(counted, "ctx", bit)
        bit *= 2
    count = counted[0, 0]
    b_query, b_value, b_proj, g_attn, s_attn, b_outer, g_final, s_final, b_inner = unpack_vectors(where, small)
    w_qkv.values, b_query, b_value, count = lax.optimization_barrier((w_qkv.values, b_query, b_value, count))

    def attend(side, tie, *so_far):
        return attn_fwd(tie, high_tile, query, keys, values_t, idq, idk, side, 2, so_far)

    query, keys, values, keys_t, values_t, w_qkv = project_qkv(where, w_qkv.result(), before, tokens, behind, b_query, b_value)
    tie, own_outer = boundary(query, (low_tile, own_half(outer_weight)), w_proj)
    w_outer = Staged(gathering, outer_weight, own_outer)
    context_a, log_a = attend(0, tie)
    context, log_totals = attend(1, boundary(context_a, low_tile, w_proj, w_inner, w_outer), context_a, log_a)
    normed, normed_low, rate, w_proj = mix_and_norm(
        boundary(context, where, w_proj, w_inner, w_outer), w_proj.values, context, b_proj, tokens, g_attn, s_attn
    )
    tie = boundary(normed, where, w_inner, w_outer)
    act, slope, w_inner = inner_forward(tie, w_inner.values, normed_low, b_inner)
    coef = (n_fsdp * n_ctx * rows / count).reshape(1)
    layer_out, d_sum_two, d_branch, final_sums, w_outer = outer_forward(
        where, w_outer.result(), coef, act, b_outer, normed, g_final, s_final, teacher_states[0], out_cotangent[0], flags
    )

    plain = jnp.concatenate([jnp.arange(n_fsdp, dtype=jnp.int32), order[n_fsdp:]])
    outer = Staged(wide_reduction, *gram(plain, n_fsdp, (act, d_branch)), parity)
    d_pre_a, bias_a, so_far = feed_back(where, 0, d_branch, w_outer, slope, w_inner, d_sum_two)
    d_pre_b, bias_b, d_sum_one, d_attn, attn_sums = feed_back(
        boundary(d_pre_a, where, outer), 1, d_branch, w_outer, slope, w_inner, so_far, (normed, rate, g_attn, s_attn)
    )
    inner_pair = gram(
        after(plain, d_attn), n_fsdp, (normed_low, d_pre_a, d_pre_b), (context, d_attn)
    )
    inner = Staged(whole_reduction, *inner_pair, parity)

    d_context, delta = context_back(after(d_attn, inner_pair[0]), w_proj, context)
    stats = jnp.stack([log_totals, delta])

    def rims(value, axis):
        size = value.shape[axis]
        before = lax.ppermute(lax.slice_in_dim(value, size - DOC_MAX, size, axis=axis), "ctx", up)
        behind = lax.ppermute(lax.slice_in_dim(value, 0, DOC_MAX, axis=axis), "ctx", down)
        return before, behind

    do_before, do_behind = rims(d_context, 0)
    stats_before, stats_behind = rims(stats, 3)
    stats = jnp.concatenate([stats_before, stats, stats_behind], axis=3)
    def attend_back(tie, *part):
        return attn_bwd(
            tie, high_tile, query, do_before, d_context, do_behind, keys, keys_t, values, stats, idq, idk, *part
        )

    parts_a = attend_back(boundary(d_context, low_tile, outer, inner), 0, 0, 1)
    parts_a = attend_back(boundary(parts_a[0], low_tile, outer), 0, 1, 1, parts_a)
    *first_pair, sums_a = qkv_gradient(boundary(parts_a[0], order, outer), tokens, *parts_a, n_fsdp)
    first = Staged(reduction, *first_pair, parity)
    parts_b = attend_back(boundary(first_pair[0], low_tile, inner, hold=[outer]), 1)
    riders = [(final_sums, 4), (attn_sums, 3), (bias_a, 1), (bias_b, 1), (sums_a, 1)]
    *last_pair, sums_b = qkv_gradient(
        boundary(parts_b[0], order, first, outer), tokens, *parts_b, n_fsdp, riders
    )
    last = Staged(reduction, *last_pair, parity, True)
    input_grad = input_back(d_sum_one, (*parts_a, *parts_b), boundary(last_pair[0], w_qkv, first))
    boundary(input_grad, where, last, first, inner)
    boundary(last.values[0], where, last, first)
    boundary(last.values[0], where, last, first)
    outer_grad, inner_grad, first, last = (transfer.result()[0] for transfer in (outer, inner, first, last))
    vectors = last[: part // 2, 3 * D // 2 :].reshape(16, D)
    query_sum, value_sum = vectors[11:13].reshape(2, 2, D // 2).transpose(1, 0, 2).reshape(2, D)
    inner_grad, proj_grad = inner_grad[:, :FF], inner_grad[:, FF:]
    sixth = D // 2
    query_grad, key_grad, value_grad = (
        jnp.concatenate([grad[:, i * sixth : (i + 1) * sixth] for grad in (first, last)], axis=1)
        for i in range(3)
    )
    mse = jnp.sum(vectors[3]) / (count * D)

    def mine(vector):
        length = vector.shape[0] // n_fsdp
        return lax.dynamic_slice_in_dim(vector, f * length, length)

    return (
        layer_out[None],
        input_grad[None],
        mse,
        query_grad,
        mine(query_sum),
        key_grad,
        value_grad,
        mine(value_sum),
        proj_grad,
        mine(vectors[6]),
        mine(vectors[4]),
        mine(vectors[5]),
        inner_grad,
        mine(vectors[7:11].reshape(FF)),
        outer_grad,
        mine(vectors[2]),
        mine(vectors[0]),
        mine(vectors[1]),
    )


def solution(mesh):
    tokens = P("fsdp", "ctx", None)
    matrix, vector = P("fsdp", None), P("fsdp")
    weights = (
        matrix, vector, matrix, matrix, vector, matrix, vector, vector, vector, matrix, vector, matrix, vector, vector, vector,
    )
    return jax.shard_map(
        body,
        mesh=mesh,
        in_specs=(tokens, tokens, tokens, matrix, P("fsdp", "ctx")) + weights,
        out_specs=(tokens, tokens, P()) + weights,
        check_vma=False,
    )
```
